128 devices in a mesh: seq: 32 (over z, x, core), head: 4 (over y).
Axes of the slice: x: 4, y: 4, z: 4, core: 2. Of those that a mesh axis runs over, the one named last changes fastest.
Arguments:
- inputs: bfloat16 [8192, 2048], P('seq'), may hold values from -6 to 6
- gain_first: float32 [2048], replicated, may hold values from 0.5 to 1.5
- w_query: bfloat16 [2048, 2048], P(None, 'head'), may hold values from -0.125 to 0.125
- a_query: bfloat16 [2048, 8], replicated, may hold values from -0.125 to 0.125
- b_query: bfloat16 [8, 2048], P(None, 'head'), may hold values from -2 to 2
- key_projection_weight: bfloat16 [2048, 512], P(None, 'head'), may hold values from -0.125 to 0.125
- a_key: bfloat16 [2048, 8], replicated, may hold values from -0.125 to 0.125
- key_adapter_second: bfloat16 [8, 512], P(None, 'head'), may hold values from -2 to 2
- value_projection_weight: bfloat16 [2048, 512], P(None, 'head'), may hold values from -0.125 to 0.125
- a_value: bfloat16 [2048, 8], replicated, may hold values from -0.125 to 0.125
- value_adapter_second: bfloat16 [8, 512], P(None, 'head'), may hold values from -2 to 2
- feature_query: bfloat16 [32, 64, 64], P('head'), may hold values from -0.75 to 0.75
- key_hedgehog_map: bfloat16 [8, 64, 64], P('head'), may hold values from -0.75 to 0.75
- w_out: bfloat16 [2048, 2048], P('head'), may hold values from -1 to 1
- a_out: bfloat16 [2048, 8], P('head'), may hold values from -1 to 1
- b_out: bfloat16 [8, 2048], replicated, may hold values from -2 to 2
- gain_second: float32 [2048], replicated, may hold values from 0.5 to 1.5
- w_gate: bfloat16 [2048, 8192], P(None, 'head'), may hold values from -0.125 to 0.125
- w_up: bfloat16 [2048, 8192], P(None, 'head'), may hold values from -0.125 to 0.125
- w_down: bfloat16 [8192, 2048], P('head'), may hold values from -0.0625 to 0.0625
- lengths: int32 [3], replicated, may hold values from 1 to 7936, as said below
- cotangent: bfloat16 [8192, 2048], P('seq'), may hold values from -6 to 6
Outputs:
- block_out: bfloat16 [8192, 2048], P('seq', 'head')
- grad_inputs: float32 [8192, 2048], P('seq', 'head')
- grad_gain_first: float32 [2048], P('head')
- grad_w_query: float32 [2048, 2048], P('seq', 'head')
- grad_a_query: float32 [2048, 8], replicated
- grad_b_query: float32 [8, 2048], P(None, 'head')
- grad_w_key: float32 [2048, 512], P('seq', 'head')
- grad_a_key: float32 [2048, 8], replicated
- grad_b_key: float32 [8, 512], P(None, 'head')
- grad_w_value: float32 [2048, 512], P('seq', 'head')
- grad_a_value: float32 [2048, 8], replicated
- grad_b_value: float32 [8, 512], P(None, 'head')
- grad_feature_query: float32 [32, 64, 64], P('head')
- grad_feature_key: float32 [8, 64, 64], P('head')
- grad_w_out: float32 [2048, 2048], P('head', 'seq')
- grad_a_out: float32 [2048, 8], P('head')
- grad_b_out: float32 [8, 2048], replicated
- grad_gain_second: float32 [2048], P('head')
- grad_w_gate: float32 [2048, 8192], P('seq', 'head')
- grad_w_up: float32 [2048, 8192], P('seq', 'head')
- grad_w_down: float32 [8192, 2048], P('head', 'seq')
The draws below stay inside these ranges and needn't reach their ends.
Inputs may be any that keep to these rules, and one draw needn't show every extreme that they name: Three documents in order whose lengths sum to 8192; the first and the last together hold 256 tokens, so the second starts on the first device of seq and ends on the last.
All inputs are finite; a program needn't handle non-finite values.
Results may differ from the reference program's by a relative error of at most 0.014.
The reference program's roundings to bfloat16 on the way count: a program that leaves them out, or rounds other values in their place, can miss the bound.
Values may be sent and summed in bfloat16 or wider, within the bound.
A program may use at most 256 MiB of HBM per device.

```python
import jax
import jax.numpy as jnp
from jax import lax

MODEL_DIMENSION = 2048
QUERY_HEADS = 32
KEY_VALUE_HEADS = 8
HEAD_SIZE = 64
FF = 8192
ADAPTER_RANK = 8
WINDOW = 64
QUERY_ROWS = 512
TOK_DEV = 256
TOKENS = 8192


def draw_lengths(key, part):
    key = jax.random.fold_in(key, 7)
    leading = jax.random.randint(key, (), 1, TOK_DEV, dtype=jnp.int32)
    middle = jnp.asarray(TOKENS - TOK_DEV, jnp.int32)
    return jnp.stack([leading, middle, TOK_DEV - leading]).astype(jnp.int32)


def raised(drawn, own_key, source, target, parts, factor):
    owner, partner = [(jnp.arange(drawn.shape[axis_at]) // (drawn.shape[axis_at] // parts)).reshape([-1 if axis == axis_at else 1 for axis in range(drawn.ndim)]) for axis_at in (source, target)]
    chosen = jax.random.permutation(own_key, parts)[partner]
    strong = (owner == chosen) | (owner == (partner + parts // 2) % parts)
    return jnp.where(strong, factor * drawn, drawn)


def block_levels(key, shape, shards, smallest, largest):
    def one(dim, blocks):
        steps = jax.random.uniform(jax.random.fold_in(jax.random.fold_in(key, 6), dim), (blocks,), jnp.float32, smallest / len(shards), largest / len(shards))
        return jnp.repeat(jnp.exp(steps), shape[dim] // blocks).reshape((-1,) + (1,) * (len(shape) - dim - 1))

    level = one(*shards[0])
    for cut in shards[1:]:
        level = level * one(*cut)
    return level


def gaussian(key, extent, spread, bound, shards=(), kind=jnp.bfloat16):
    gain = block_levels(key, extent, shards, -0.22, 0.18) if shards else 1.0
    values = jax.random.normal(key, extent, jnp.float32) * spread * gain
    return jnp.minimum(jnp.maximum(values, -bound), bound).astype(kind)


def bell_draw_with(stream_key, dims, width, bound, cuts, heavy, held_as=jnp.bfloat16):
    entries = width * jax.random.normal(stream_key, dims, jnp.float32)
    if cuts:
        entries = entries * block_levels(stream_key, dims, cuts, -0.22, 0.18)
    return jnp.clip(raised(entries, jax.random.fold_in(stream_key, 3), *heavy), -bound, bound).astype(held_as)


def setup_inputs(seed: int = 0) -> dict:
    key_list = jax.random.split(jax.random.key(seed), 23)
    inputs = gaussian(key_list[0], (TOKENS, MODEL_DIMENSION), 1.0, 6.0, ((0, 32),))
    gain_first = jnp.clip(1.0 + 0.1 * jax.random.normal(key_list[1], (MODEL_DIMENSION,), jnp.float32), 0.5, 1.5)
    w_query = gaussian(key_list[2], (MODEL_DIMENSION, QUERY_HEADS * HEAD_SIZE), MODEL_DIMENSION ** -0.5, 0.125, ((1, 4),))
    a_query = gaussian(key_list[3], (MODEL_DIMENSION, ADAPTER_RANK), MODEL_DIMENSION ** -0.5, 0.125)
    b_query = gaussian(key_list[4], (ADAPTER_RANK, QUERY_HEADS * HEAD_SIZE), ADAPTER_RANK ** -0.5, 2.0, ((1, 4),))
    key_projection_weight = gaussian(key_list[5], (MODEL_DIMENSION, KEY_VALUE_HEADS * HEAD_SIZE), MODEL_DIMENSION ** -0.5, 0.125, ((1, 4),))
    a_key = gaussian(key_list[6], (MODEL_DIMENSION, ADAPTER_RANK), MODEL_DIMENSION ** -0.5, 0.125)
    key_adapter_second = gaussian(key_list[7], (ADAPTER_RANK, KEY_VALUE_HEADS * HEAD_SIZE), ADAPTER_RANK ** -0.5, 2.0, ((1, 4),))
    value_projection_weight = gaussian(key_list[8], (MODEL_DIMENSION, KEY_VALUE_HEADS * HEAD_SIZE), MODEL_DIMENSION ** -0.5, 0.125, ((1, 4),))
    a_value = gaussian(key_list[9], (MODEL_DIMENSION, ADAPTER_RANK), MODEL_DIMENSION ** -0.5, 0.125)
    value_adapter_second = gaussian(key_list[10], (ADAPTER_RANK, KEY_VALUE_HEADS * HEAD_SIZE), ADAPTER_RANK ** -0.5, 2.0, ((1, 4),))
    feature_query = gaussian(key_list[11], (QUERY_HEADS, HEAD_SIZE, HEAD_SIZE), HEAD_SIZE ** -0.5, 0.75, ((0, 4),))
    key_hedgehog_map = gaussian(key_list[12], (KEY_VALUE_HEADS, HEAD_SIZE, HEAD_SIZE), HEAD_SIZE ** -0.5, 0.75, ((0, 4),))
    w_out = gaussian(key_list[13], (QUERY_HEADS * HEAD_SIZE, MODEL_DIMENSION), (QUERY_HEADS * HEAD_SIZE // WINDOW) ** -0.5, 1.0, ((0, 4),))
    a_out = gaussian(key_list[14], (QUERY_HEADS * HEAD_SIZE, ADAPTER_RANK), (QUERY_HEADS * HEAD_SIZE // WINDOW) ** -0.5, 1.0, ((0, 4),))
    b_out = gaussian(key_list[15], (ADAPTER_RANK, MODEL_DIMENSION), ADAPTER_RANK ** -0.5, 2.0)
    gain_second = jnp.clip(1.0 + 0.1 * jax.random.normal(key_list[16], (MODEL_DIMENSION,), jnp.float32), 0.5, 1.5)
    w_gate = gaussian(key_list[17], (MODEL_DIMENSION, FF), MODEL_DIMENSION ** -0.5, 0.125, ((1, 4),))
    w_up = gaussian(key_list[18], (MODEL_DIMENSION, FF), MODEL_DIMENSION ** -0.5, 0.125, ((1, 4),))
    w_down = gaussian(key_list[19], (FF, MODEL_DIMENSION), FF ** -0.5, 0.0625, ((0, 4),))
    lengths = draw_lengths(jax.random.fold_in(key_list[22], 71), 0)
    cotangent = bell_draw_with(key_list[21], (TOKENS, MODEL_DIMENSION), 1.0, 6.0, ((0, 32),), (0, 1, 32, 2.75))
    return {"inputs": inputs, "gain_first": gain_first, "w_query": w_query, "a_query": a_query, "b_query": b_query, "key_projection_weight": key_projection_weight, "a_key": a_key, "key_adapter_second": key_adapter_second, "value_projection_weight": value_projection_weight, "a_value": a_value, "value_adapter_second": value_adapter_second, "feature_query": feature_query, "key_hedgehog_map": key_hedgehog_map, "w_out": w_out, "a_out": a_out, "b_out": b_out, "gain_second": gain_second, "w_gate": w_gate, "w_up": w_up, "w_down": w_down, "lengths": lengths, "cotangent": cotangent}


@jax.custom_vjp
def low(v):
    return lax.optimization_barrier(v.astype(jnp.bfloat16)).astype(jnp.float32)

@jax.custom_vjp
def low_back(v):
    return v

def low_keep(v):
    return (low(v), None)

def low_pass(kept, grad):
    return (grad,)

def back_keep(v):
    return (v, None)

def back_low(kept, grad):
    return (low(grad),)
low.defvjp(low_keep, low_pass)
low_back.defvjp(back_keep, back_low)
EPS = 1e-05
NEG = -1e+30
HIGH = lax.Precision.HIGHEST

def round_both(values):
    return low_back(low(values))

def matmul(left_side, right_side):
    return jnp.dot(left_side, right_side, precision=HIGH, preferred_element_type=jnp.float32)

def rms_norm(values, gain_vector):
    return values * lax.rsqrt(lax.optimization_barrier(jnp.mean(values * values, axis=-1, keepdims=True)) + EPS) * gain_vector

def feature(inputs, feature_table):
    logits = jnp.einsum('hnd,hde->hne', inputs, feature_table, precision=HIGH)
    return low(jnp.concatenate([jax.nn.softmax(logits, axis=-1), jax.nn.softmax(-logits, axis=-1)], axis=-1))

def doc_of(positions, starts):
    return (lax.optimization_barrier(jnp.sum((starts[None, :] <= positions[:, None]).astype(jnp.int32), axis=1)) - 1).astype(jnp.int32)

def attend_block(block_of_queries, block_features, keys_block, phi_keys, values_block, state_sum, norm_sums, query_pos, key_pos, starts):
    row_count = block_of_queries.shape[2]
    query_doc = doc_of(query_pos, starts)
    key_doc = doc_of(key_pos, starts)
    offset = query_pos[:, None] - key_pos[None, :]
    same_doc = query_doc[:, None] == key_doc[None, :]
    within = same_doc & (offset >= 0) & (offset < WINDOW)
    beyond = same_doc & (offset >= WINDOW)
    scores = low_back(jnp.einsum('kgrd,kcd->kgrc', block_of_queries, keys_block, precision=HIGH) * HEAD_SIZE ** (-0.5))
    masked = jnp.where(within, scores, NEG)
    maxima = lax.optimization_barrier(jnp.max(masked, axis=-1, keepdims=True))
    weights_near = jnp.exp(masked - maxima)
    damping = jnp.exp(-maxima)
    linear = low_back(jnp.einsum('kgrf,kcf->kgrc', block_features, phi_keys, precision=HIGH))
    weights_far = jnp.where(beyond, linear, 0.0) * damping
    carry_on = (query_doc == doc_of(query_pos[:1] - WINDOW - 1, starts)[0]).astype(jnp.float32)
    gating = damping[..., 0] * carry_on
    numerator = jnp.einsum('kgrc,kcd->kgrd', low(weights_near), values_block, precision=HIGH) + jnp.einsum('kgrc,kcd->kgrd', weights_far, values_block, precision=HIGH) + gating[..., None] * jnp.einsum('kgrf,kfd->kgrd', block_features, state_sum, precision=HIGH)
    denominator = lax.optimization_barrier(jnp.sum(weights_near, axis=-1)) + lax.optimization_barrier(jnp.sum(weights_far, axis=-1)) + gating * jnp.einsum('kgrf,kf->kgr', block_features, norm_sums, precision=HIGH)
    keeping = (key_doc[:row_count] == key_doc[row_count - 1]).astype(jnp.float32)
    own_phi = phi_keys[:, :row_count] * keeping[None, :, None]
    resets = jnp.any((starts >= key_pos[0]) & (starts <= key_pos[row_count - 1])).astype(jnp.float32)
    new_state = jnp.einsum('kcf,kcd->kfd', own_phi, values_block[:, :row_count], precision=HIGH) + (1.0 - resets) * state_sum
    new_norms = lax.optimization_barrier(jnp.sum(own_phi, axis=1)) + (1.0 - resets) * norm_sums
    return (numerator / denominator[..., None], (new_state, new_norms))

def attention(queries, incoming_keys, incoming_values, feature_query, key_hedgehog_map, starts):
    token_stream = queries.shape[0]
    group_count = QUERY_HEADS // KEY_VALUE_HEADS
    heads_of_queries = queries.reshape(token_stream, QUERY_HEADS, HEAD_SIZE).transpose(1, 0, 2)
    heads_of_keys = incoming_keys.reshape(token_stream, KEY_VALUE_HEADS, HEAD_SIZE).transpose(1, 0, 2)
    heads_of_values = incoming_values.reshape(token_stream, KEY_VALUE_HEADS, HEAD_SIZE).transpose(1, 0, 2)
    query_features = feature(heads_of_queries, feature_query)
    padding = ((0, 0), (WINDOW, 0), (0, 0))
    keys_all = jnp.pad(heads_of_keys, padding)
    values_all = jnp.pad(heads_of_values, padding)
    phi_keys = jnp.pad(feature(heads_of_keys, key_hedgehog_map), padding)

    def one_block(state_pair, block_index):
        offset_lookup = (block_index * QUERY_ROWS).astype(jnp.int32)
        block_of_queries = lax.dynamic_slice_in_dim(heads_of_queries, offset_lookup, QUERY_ROWS, 1).reshape(KEY_VALUE_HEADS, group_count, QUERY_ROWS, HEAD_SIZE)
        block_features = lax.dynamic_slice_in_dim(query_features, offset_lookup, QUERY_ROWS, 1).reshape(KEY_VALUE_HEADS, group_count, QUERY_ROWS, 2 * HEAD_SIZE)
        keys_block = lax.dynamic_slice_in_dim(keys_all, offset_lookup, QUERY_ROWS + WINDOW, 1)
        values_block = lax.dynamic_slice_in_dim(values_all, offset_lookup, QUERY_ROWS + WINDOW, 1)
        phi_keys_block = lax.dynamic_slice_in_dim(phi_keys, offset_lookup, QUERY_ROWS + WINDOW, 1)
        query_pos = offset_lookup + jnp.arange(QUERY_ROWS, dtype=jnp.int32)
        key_pos = offset_lookup - WINDOW + jnp.arange(QUERY_ROWS + WINDOW, dtype=jnp.int32)
        result, state_pair = attend_block(block_of_queries, block_features, keys_block, phi_keys_block, values_block, state_pair[0], state_pair[1], query_pos, key_pos, starts)
        return (state_pair, result.reshape(QUERY_HEADS, QUERY_ROWS, HEAD_SIZE))
    starting_state = (jnp.zeros((KEY_VALUE_HEADS, 2 * HEAD_SIZE, HEAD_SIZE), jnp.float32), jnp.zeros((KEY_VALUE_HEADS, 2 * HEAD_SIZE), jnp.float32))
    unused, results = lax.scan(jax.checkpoint(one_block), starting_state, jnp.arange(token_stream // QUERY_ROWS, dtype=jnp.int32))
    return results.transpose(0, 2, 1, 3).reshape(token_stream, QUERY_HEADS * HEAD_SIZE)

def block_layer(inputs, gain_first, w_query, a_query, b_query, key_projection_weight, a_key, key_adapter_second, value_projection_weight, a_value, value_adapter_second, feature_query, key_hedgehog_map, w_out, a_out, b_out, gain_second, w_gate, w_up, w_down, starts):
    normed = low(rms_norm(inputs, gain_first))

    def project(weight, down_map, up_map):
        return round_both(matmul(normed, weight) + matmul(low(matmul(normed, down_map)), up_map))
    queries = project(w_query, a_query, b_query)
    incoming_keys = project(key_projection_weight, a_key, key_adapter_second)
    incoming_values = project(value_projection_weight, a_value, value_adapter_second)
    mixed_heads = round_both(attention(queries, incoming_keys, incoming_values, feature_query, key_hedgehog_map, starts))
    branch = low_back(matmul(mixed_heads, w_out) + matmul(low(matmul(mixed_heads, a_out)), b_out))
    hidden_in = inputs + branch
    normed_second = low(rms_norm(hidden_in, gain_second))
    gate_pre = low_back(matmul(normed_second, w_gate))
    up_pre = low_back(matmul(normed_second, w_up))
    hidden = low(jax.nn.silu(gate_pre) * up_pre)
    return hidden_in + matmul(hidden, w_down)

def reference(inputs, gain_first, w_query, a_query, b_query, key_projection_weight, a_key, key_adapter_second, value_projection_weight, a_value, value_adapter_second, feature_query, key_hedgehog_map, w_out, a_out, b_out, gain_second, w_gate, w_up, w_down, lengths, cotangent):
    starts = (jnp.cumsum(lengths) - lengths).astype(jnp.int32)
    weights = [member.astype(jnp.float32) for member in (gain_first, w_query, a_query, b_query, key_projection_weight, a_key, key_adapter_second, value_projection_weight, a_value, value_adapter_second, feature_query, key_hedgehog_map, w_out, a_out, b_out, gain_second, w_gate, w_up, w_down)]

    def forward(values, *params):
        return block_layer(values, *params, starts)
    result, pullback = jax.vjp(forward, inputs.astype(jnp.float32), *weights)
    grads = pullback(cotangent.astype(jnp.float32))
    return (result.astype(jnp.bfloat16), grads[0], grads[1], grads[2], grads[3], grads[4], grads[5], grads[6], grads[7], grads[8], grads[9], grads[10], grads[11], grads[12], grads[13], grads[14], grads[15], grads[16], grads[17], grads[18], grads[19])
```

```python
import jax
import jax.numpy as jnp
from jax import lax
from jax.experimental import pallas as pl
from jax.experimental.pallas import tpu as pltpu
from jax.sharding import PartitionSpec as P

WINDOW = 64


EPS = 1e-05
NEG = -1e30
HIGH = lax.Precision.HIGHEST

MESH = pl.DeviceIdType.MESH
F32 = jnp.float32
BF16 = jnp.bfloat16


def spot():
    s = lax.axis_index("seq")
    y = lax.axis_index("head")
    return lax.div(s, 8), lax.rem(lax.div(s, 2), 4), lax.rem(s, 2), y


def at(z, x, c, y):
    return ((z * 4 + x) * 2 + c, y)


def turned(p, steps):
    return lax.rem(p + steps, 4)


def greet(partners):
    barrier = pltpu.get_barrier_semaphore()
    for partner in partners:
        pl.semaphore_signal(barrier, inc=1, device_id=partner, device_id_type=MESH)
    pl.semaphore_wait(barrier, len(partners))


def send(src, dst, ss, rs, device):
    return pltpu.make_async_remote_copy(
        src_ref=src, dst_ref=dst, send_sem=ss, recv_sem=rs, device_id=device, device_id_type=MESH
    )


class Ring:
    def __init__(self, refs, rows, term, finish):
        self.sb, self.ra, self.rf, self.tb, self.ra3, self.rf3, self.ss, self.rs = refs
        self.rows, self.term, self.finish = rows, term, finish
        z, x, c, y = spot()
        self.axes = (
            (x, at(z, turned(x, 1), c, y), at(z, turned(x, 3), c, y)),
            (z, at(turned(z, 1), x, c, y), at(turned(z, 3), x, c, y)),
        )

    @staticmethod
    def scratch(count, rows, width):
        return [
            pltpu.VMEM((count, 3, 4 * rows, width), BF16),
            pltpu.VMEM((count, 2, 2 * rows, width), BF16),
            pltpu.VMEM((count, 2, 4 * rows, width), BF16),
            pltpu.VMEM((count, 4, rows, width), BF16),
            pltpu.VMEM((count, 2, rows // 2, width), BF16),
            pltpu.VMEM((count, 2, rows, width), BF16),
            pltpu.SemaphoreType.DMA((count, 12)),
            pltpu.SemaphoreType.DMA((count, 12)),
        ]

    def copy(self, t, k, i):
        p, ahead, behind = self.axes[k]
        q, ahead3, behind3 = self.axes[1 - k]
        h, g = 2 * self.rows, self.rows // 2
        lo, hi, lo3, hi3 = pl.ds(0, h), pl.ds(h, h), pl.ds(0, g), pl.ds(g, g)
        sb, ra, rf, tb, ra3, rf3 = self.sb, self.ra, self.rf, self.tb, self.ra3, self.rf3
        src, dst, device = (
            lambda: (sb.at[t, 0, lo], ra.at[t, 0], ahead),
            lambda: (sb.at[t, 0, hi], ra.at[t, 1], behind),
            lambda: (sb.at[t, 1, hi], rf.at[t, 0, hi], ahead),
            lambda: (sb.at[t, 2, lo], rf.at[t, 1, lo], behind),
            lambda: (sb.at[t, 1, lo], rf.at[t, 0, lo], ahead),
            lambda: (sb.at[t, 2, hi], rf.at[t, 1, hi], behind),
            lambda: (tb.at[t, turned(q, 2), lo3], ra3.at[t, 0], ahead3),
            lambda: (tb.at[t, turned(q, 2), hi3], ra3.at[t, 1], behind3),
            lambda: (tb.at[t, turned(q, 1), hi3], rf3.at[t, 0, hi3], ahead3),
            lambda: (tb.at[t, turned(q, 3), lo3], rf3.at[t, 1, lo3], behind3),
            lambda: (tb.at[t, turned(q, 1), lo3], rf3.at[t, 0, lo3], ahead3),
            lambda: (tb.at[t, turned(q, 3), hi3], rf3.at[t, 1, hi3], behind3),
        )[i]()
        return send(src, dst, self.ss.at[t, i], self.rs.at[t, i], device)

    def start(self, t, k):
        p = self.axes[k][0]
        h = 2 * self.rows
        self.sb[t, 0] = self.term(t, k, turned(p, 2), 0, 4).astype(BF16)
        self.copy(t, k, 0).start()
        self.copy(t, k, 1).start()
        self.sb[t, 1, h:] = self.term(t, k, turned(p, 1), 2, 4).astype(BF16)
        self.copy(t, k, 2).start()
        self.sb[t, 2, :h] = self.term(t, k, turned(p, 3), 0, 2).astype(BF16)
        self.copy(t, k, 3).start()

    def merge(self, t, k):
        p = self.axes[k][0]
        h = 2 * self.rows
        self.copy(t, k, 0).wait_recv()
        self.sb[t, 1, :h] = (self.term(t, k, turned(p, 1), 0, 2) + self.ra[t, 0].astype(F32)).astype(BF16)
        self.copy(t, k, 4).start()
        self.copy(t, k, 1).wait_recv()
        self.sb[t, 2, h:] = (self.term(t, k, turned(p, 3), 2, 4) + self.ra[t, 1].astype(F32)).astype(BF16)
        self.copy(t, k, 5).start()

    def cross(self, t, k):
        p = self.axes[k][0]
        own = self.term(t, k, p, 0, 4)
        for i in (2, 3, 4, 5):
            self.copy(t, k, i).wait_recv()
        own = own + self.rf[t, 0].astype(F32) + self.rf[t, 1].astype(F32)
        self.tb[t] = own.astype(BF16).reshape(self.tb.shape[1:])
        for i in (6, 7, 8, 9):
            self.copy(t, k, i).start()

    def merge_cross(self, t, k):
        q = self.axes[1 - k][0]
        g = self.rows // 2
        self.copy(t, k, 6).wait_recv()
        ahead, behind = turned(q, 1), turned(q, 3)
        self.tb[t, ahead, :g] = (self.tb[t, ahead, :g].astype(F32) + self.ra3[t, 0].astype(F32)).astype(BF16)
        self.copy(t, k, 10).start()
        self.copy(t, k, 7).wait_recv()
        self.tb[t, behind, g:] = (self.tb[t, behind, g:].astype(F32) + self.ra3[t, 1].astype(F32)).astype(BF16)
        self.copy(t, k, 11).start()

    def end(self, t, k):
        q = self.axes[1 - k][0]
        for i in (8, 9, 10, 11):
            self.copy(t, k, i).wait_recv()
        self.finish(
            t, k, self.tb[t, q].astype(F32) + self.rf3[t, 0].astype(F32) + self.rf3[t, 1].astype(F32)
        )

    def drain(self, t, k):
        for i in range(12):
            self.copy(t, k, i).wait_send()


def over_pairs(count, step):
    def both(u, carry):
        step(2 * u, 0)
        step(2 * u + 1, 1)
        return carry

    lax.fori_loop(0, count // 2, both, 0)


FFN_TILES, FFN_WIDTH = 12, 512
ATT_TILES, ATT_WIDTH = 5, 256
PACK = 32


def sums_kernel(
    xt_ffn, y_ffn, xt_att, y_att, pack,
    out_ffn, out_att, out_pack,
    xf, yf, xa, ya, pk, sem_ffn, sem_att, sem_pack,
    *rest,
):
    ring_ffn, ring_att, ring_pack = rest[0:8], rest[8:16], rest[16:24]
    ysum, sem_y, sem_zx = rest[24:27]
    z, x, c, y = spot()
    sibling = at(z, x, 1 - c, y)
    others = (1, 2, 3)
    z_mates = [at(turned(z, i), x, c, y) for i in others]
    x_mates = [at(z, turned(x, i), c, y) for i in others]
    y_mates = [at(z, x, c, turned(y, i)) for i in others]
    greet([sibling] + z_mates + x_mates + y_mates)

    own_rows, far_rows = pl.ds(0, 256), pl.ds(256, 256)

    def factors(xt, yt, xd, yd, sem, m, t):
        copies = []
        if m is not None:
            copies.append(pltpu.make_async_copy(xt.at[m, c], xd.at[m, :, :, :, own_rows], sem.at[0, m]))
            copies.append(
                send(xt.at[m, 1 - c], xd.at[m, :, :, :, far_rows], sem.at[1, m], sem.at[2, m], sibling)
            )
        if t is not None:
            copies.append(pltpu.make_async_copy(yt.at[t], yd.at[t, own_rows], sem.at[0, 2 + t]))
            copies.append(send(yt.at[t], yd.at[t, far_rows], sem.at[1, 2 + t], sem.at[2, 2 + t], sibling))
        return copies

    ffn = (xt_ffn, y_ffn, xf, yf, sem_ffn)
    att = (xt_att, y_att, xa, ya, sem_att)
    pack_own = pltpu.make_async_copy(pack.at[c], pk.at[0], sem_pack.at[0])
    pack_far = send(pack.at[1 - c], pk.at[1], sem_pack.at[1], sem_pack.at[2], sibling)
    for m in range(2):
        for copy in factors(*ffn, m, None):
            copy.start()

    def open_ffn(t, carry):
        for copy in factors(*ffn, None, t):
            copy.start()
        return carry

    lax.fori_loop(0, FFN_TILES, open_ffn, 0)
    for m in range(2):
        for copy in factors(*att, m, None):
            copy.start()
    for t in range(ATT_TILES):
        for copy in factors(*att, None, t):
            copy.start()
    pack_own.start()
    pack_far.start()

    def product(xd, yd, kind):
        def term(t, k, dest, first, last):
            m = kind(t)
            if k == 0:
                rows = xd[m, first:last, dest]
            else:
                rows = xd[m, dest, first:last]
            rows = rows.reshape((last - first) * 64, 512)
            return jnp.dot(rows, yd[t], preferred_element_type=F32)

        return term

    def finish_ffn(t, k, value):
        out_ffn[t] = value

    def finish_att(t, k, value):
        out_att[t] = value

    def term_pack(t, k, dest, first, last):
        both = (pk[0, first:last, dest], pk[1, first:last, dest])
        return (both[0] + both[1]).reshape((last - first) * PACK, 128)

    def finish_pack(t, k, value):
        out_pack[c, z, x] = value

    big = Ring(ring_ffn, 64, product(xf, yf, lambda t: lax.div(t, 8)), finish_ffn)
    mid = Ring(ring_att, 64, product(xa, ya, lambda t: t // 3), finish_att)
    low = Ring(ring_pack, PACK, term_pack, finish_pack)

    for m in range(2):
        for copy in factors(*ffn, m, None):
            copy.wait()

    def first_ffn(t, k):
        for copy in factors(*ffn, None, t):
            copy.wait()
        big.start(t, k)

    over_pairs(FFN_TILES, first_ffn)
    for m in range(2):
        for copy in factors(*att, m, None):
            copy.wait()
    for t in range(ATT_TILES):
        for copy in factors(*att, None, t):
            copy.wait()
        mid.start(t, t % 2)
    pack_own.wait()
    pack_far.wait()
    low.start(0, 0)
    over_pairs(FFN_TILES, big.merge)
    for t in range(ATT_TILES):
        mid.merge(t, t % 2)
    low.merge(0, 0)
    over_pairs(FFN_TILES, big.cross)
    for t in range(ATT_TILES):
        mid.cross(t, t % 2)
    low.cross(0, 0)
    over_pairs(FFN_TILES, big.merge_cross)
    for t in range(ATT_TILES):
        mid.merge_cross(t, t % 2)
    low.merge_cross(0, 0)
    over_pairs(FFN_TILES, big.end)
    for t in range(ATT_TILES):
        mid.end(t, t % 2)
    low.end(0, 0)
    top = pl.ds(0, 16)
    turns = [
        send(out_pack.at[c, z, x, top], ysum.at[i], sem_y.at[0, i], sem_y.at[1, i], y_mates[i]) for i in range(3)
    ]
    for copy in turns:
        copy.start()
    for copy in turns:
        copy.wait()
    out_pack[c, z, x, top] = out_pack[c, z, x, top] + ysum[0] + ysum[1] + ysum[2]
    turns = [
        send(out_pack.at[c, z, x], out_pack.at[c, z, x], sem_zx.at[0, i], sem_zx.at[1, i], z_mates[i])
        for i in range(3)
    ]
    for copy in turns:
        copy.start()
    for i in range(3):
        came = out_pack.at[c, turned(z, 3 - i), x]
        send(came, came, sem_zx.at[0, i], sem_zx.at[1, i], z_mates[i]).wait()
    turns = [
        send(out_pack.at[c, :, x], out_pack.at[c, :, x], sem_zx.at[0, 3 + i], sem_zx.at[1, 3 + i], x_mates[i])
        for i in range(3)
    ]
    for copy in turns:
        copy.start()
    for i in range(3):
        came = out_pack.at[c, :, turned(x, 3 - i)]
        send(came, came, sem_zx.at[0, 3 + i], sem_zx.at[1, 3 + i], x_mates[i]).wait()
    last = send(out_pack.at[c], out_pack.at[c], sem_zx.at[0, 6], sem_zx.at[1, 6], sibling)
    last.start()
    came = out_pack.at[1 - c]
    send(came, came, sem_zx.at[0, 6], sem_zx.at[1, 6], sibling).wait()
    over_pairs(FFN_TILES, big.drain)
    for t in range(ATT_TILES):
        mid.drain(t, t % 2)
    low.drain(0, 0)


def seq_sums(xt_ffn, y_ffn, xt_att, y_att, pack):
    anywhere = pl.BlockSpec(memory_space=pl.ANY)
    vmem = pl.BlockSpec(memory_space=pltpu.VMEM)
    return pl.pallas_call(
        sums_kernel,
        out_shape=(
            jax.ShapeDtypeStruct((FFN_TILES, 64, FFN_WIDTH), F32),
            jax.ShapeDtypeStruct((ATT_TILES, 64, ATT_WIDTH), F32),
            jax.ShapeDtypeStruct((2, 4, 4, PACK, 128), F32),
        ),
        in_specs=[anywhere] * 5,
        out_specs=(vmem,) * 3,
        scratch_shapes=[
            pltpu.VMEM((2, 4, 4, 64, 512), BF16),
            pltpu.VMEM((FFN_TILES, 512, FFN_WIDTH), BF16),
            pltpu.VMEM((2, 4, 4, 64, 512), BF16),
            pltpu.VMEM((ATT_TILES, 512, ATT_WIDTH), BF16),
            pltpu.VMEM((2, 4, 4, PACK, 128), F32),
            pltpu.SemaphoreType.DMA((3, 2 + FFN_TILES)),
            pltpu.SemaphoreType.DMA((3, 2 + ATT_TILES)),
            pltpu.SemaphoreType.DMA((3,)),
            *Ring.scratch(FFN_TILES, 64, FFN_WIDTH),
            *Ring.scratch(ATT_TILES, 64, ATT_WIDTH),
            *Ring.scratch(1, PACK, 128),
            pltpu.VMEM((3, 16, 128), F32),
            pltpu.SemaphoreType.DMA((2, 3)),
            pltpu.SemaphoreType.DMA((2, 7)),
        ],
        compiler_params=pltpu.CompilerParams(
            collective_id=0, has_side_effects=True, vmem_limit_bytes=60 * 2**20
        ),
        name="seq_sums",
    )(xt_ffn, y_ffn, xt_att, y_att, pack)


def by_owner(rows):
    return rows.reshape(rows.shape[0], 4, 4, 2, 64).transpose(3, 1, 2, 4, 0)


def tiles_of(rows, width):
    return rows.reshape(rows.shape[0], -1, width).transpose(1, 0, 2)


def untile(tiles):
    return tiles.transpose(1, 0, 2).reshape(tiles.shape[1], -1)


def pack_small(a_rows, b_out, f_query, f_key, b_rows, a_out, gain_one, gain_two):
    top = jnp.concatenate([a_rows[:12], b_out[:4], a_rows[12:], b_out[4:]], axis=0)
    top = top.reshape(2, 16, 16, 128).transpose(2, 0, 1, 3).reshape(32, 16, 128)
    bottom = jnp.concatenate(
        [
            f_query.reshape(4, 2, 64, 64).transpose(0, 2, 1, 3).reshape(16, 16, 128),
            f_key.transpose(1, 0, 2).reshape(4, 16, 128),
            b_rows.reshape(8, 6, 128).transpose(1, 0, 2).reshape(3, 16, 128),
            a_out.reshape(8, 4, 128).transpose(1, 0, 2).reshape(2, 16, 128),
            jnp.concatenate([gain_one.reshape(4, 128), gain_two.reshape(4, 128), jnp.zeros((8, 128), F32)])[None],
            jnp.zeros((6, 16, 128), F32),
        ]
    )
    return jnp.concatenate([top, bottom], axis=1).reshape(2, 4, 4, 32, 128)


def unpack_small(packed):
    flat = packed.reshape(32, 32, 128)
    top = flat[:, :16].reshape(16, 2, 16, 128).transpose(1, 2, 0, 3).reshape(2, 16, 2048)
    a_rows = jnp.concatenate([top[0, :12], top[1, :12]])
    b_out = jnp.concatenate([top[0, 12:], top[1, 12:]])
    bottom = flat[:, 16:]
    f_query = bottom[:16].reshape(4, 64, 2, 64).transpose(0, 2, 1, 3).reshape(8, 64, 64)
    f_key = bottom[16:20].reshape(64, 2, 64).transpose(1, 0, 2)
    b_rows = bottom[20:23].reshape(6, 8, 128).transpose(1, 0, 2).reshape(8, 768)
    a_out = bottom[23:25].reshape(4, 8, 128).transpose(1, 0, 2).reshape(8, 512)
    gains = bottom[25]
    return a_rows, b_out, f_query, f_key, b_rows, a_out, gains[:4].reshape(512), gains[4:8].reshape(512)


def passed_along(value, axis, steps):
    count = lax.axis_size(axis)
    leading, last = (max(0, -steps), min(count, count - steps))
    return lax.ppermute(value, axis, [(source, source + steps) for source in range(leading, last)])


def entering(part, axis, combine, identity, reverse):
    count = lax.axis_size(axis)
    place = lax.axis_index(axis)
    ahead = count - 1 - place if reverse else place
    gathered = jax.tree.map(lambda a: lax.all_gather(a, axis), part)
    state = jax.tree.map(lambda a, e: jnp.zeros_like(a) + jnp.asarray(e, a.dtype), part, identity)

    def one(turn, state):
        source = count - 1 - turn if reverse else turn
        return combine(
            state, jax.tree.map(lambda a: lax.dynamic_index_in_dim(a, source, 0, False), gathered)
        )

    return lax.fori_loop(0, ahead, one, state)


def dot_plain(left_side, right_side):
    return jnp.dot(left_side, right_side, preferred_element_type=jnp.float32)


def by_transpose(left_side, right_side):
    return lax.dot_general(
        left_side, right_side, (((1,), (1,)), ((), ())), preferred_element_type=jnp.float32
    )


def by_transpose_exact(left_side, right_side):
    return lax.dot_general(
        left_side,
        right_side.astype(jnp.float32),
        (((1,), (1,)), ((), ())),
        precision=HIGH,
        preferred_element_type=jnp.float32,
    )


def transpose_by(left_side, right_side):
    return lax.dot_general(
        left_side, right_side, (((0,), (0,)), ((), ())), preferred_element_type=jnp.float32
    )


def transpose_by_exact(left_side, right_side):
    return lax.dot_general(
        left_side.astype(jnp.float32),
        right_side,
        (((0,), (0,)), ((), ())),
        precision=HIGH,
        preferred_element_type=jnp.float32,
    )


def rms_scale(values):
    return lax.rsqrt(jnp.mean(values * values, axis=-1, keepdims=True) + EPS)


def norm_back(grad_normed, values, factor, gain_vector):
    weighted = grad_normed * gain_vector
    return factor * weighted - values * factor * factor * factor * jnp.mean(
        weighted * values, axis=-1, keepdims=True
    )


def feature_map(inputs, feature_table):
    logits = jnp.einsum("hnd,hde->hne", inputs, feature_table, preferred_element_type=jnp.float32)
    return jnp.concatenate(
        [jax.nn.softmax(logits, axis=-1), jax.nn.softmax(-logits, axis=-1)], axis=-1
    ).astype(jnp.bfloat16)


def feature_back(inputs, feature_table, grad_phi):
    logits = jnp.einsum("hnd,hde->hne", inputs, feature_table, preferred_element_type=jnp.float32)
    half_width = logits.shape[-1]
    upper_soft = jax.nn.softmax(logits, axis=-1)
    lower_soft = jax.nn.softmax(-logits, axis=-1)
    grad_upper = grad_phi[..., :half_width]
    grad_lower = grad_phi[..., half_width:]
    grad_logits = upper_soft * (
        grad_upper - jnp.sum(upper_soft * grad_upper, axis=-1, keepdims=True)
    ) - lower_soft * (grad_lower - jnp.sum(lower_soft * grad_lower, axis=-1, keepdims=True))
    grad_inputs = jnp.einsum(
        "hne,hde->hnd", grad_logits, feature_table.astype(jnp.float32), precision=HIGH
    )
    grad_table = jnp.einsum("hnd,hne->hde", inputs.astype(jnp.float32), grad_logits, precision=HIGH)
    return (grad_inputs, grad_table)


def doc_of(positions, starts):
    return jnp.sum((starts[None, :] <= positions[:, None]).astype(jnp.int32), axis=1) - 1


def geometry(first_pos, row_count, starts):
    query_pos = first_pos + jnp.arange(row_count, dtype=jnp.int32)
    key_pos = first_pos - WINDOW + jnp.arange(row_count + WINDOW, dtype=jnp.int32)
    query_doc = doc_of(query_pos, starts)
    key_doc = doc_of(key_pos, starts)
    offset = query_pos[:, None] - key_pos[None, :]
    same_doc = query_doc[:, None] == key_doc[None, :]
    within = same_doc & (offset >= 0) & (offset < WINDOW)
    beyond = same_doc & (offset >= WINDOW)
    carry_on = (query_doc == doc_of(query_pos[:1] - WINDOW - 1, starts)[0]).astype(jnp.float32)
    keeping = (key_doc[:row_count] == key_doc[row_count - 1]).astype(jnp.float32)
    resets = jnp.any((starts >= key_pos[0]) & (starts <= key_pos[row_count - 1])).astype(
        jnp.float32
    )
    return (within, beyond, carry_on, keeping, resets)


def segment_join(earlier, later_part):
    passing = 1.0 - later_part[2]
    return (
        later_part[0] + passing * earlier[0],
        later_part[1] + passing * earlier[1],
        jnp.maximum(earlier[2], later_part[2]),
    )


def attend(query_group, phi_group, keys_all, phi_keys, values_all, prefix, layout):
    within, beyond, carry_on = layout
    factor = query_group.shape[-1] ** (-0.5)
    scores = (
        jnp.einsum("kgrd,kcd->kgrc", query_group, keys_all, preferred_element_type=jnp.float32)
        * factor
    )
    masked = jnp.where(within, scores, NEG)
    maxima = jnp.max(masked, axis=-1, keepdims=True)
    weights_near = jnp.exp(masked - maxima)
    damping = jnp.exp(-maxima)
    linear = jnp.einsum("kgrf,kcf->kgrc", phi_group, phi_keys, preferred_element_type=jnp.float32)
    weights_far = jnp.where(beyond, linear, 0.0) * damping
    gating = damping[..., 0] * carry_on
    phi_float = phi_group.astype(jnp.float32)
    numerator = (
        jnp.einsum(
            "kgrc,kcd->kgrd",
            weights_near.astype(jnp.bfloat16),
            values_all,
            preferred_element_type=jnp.float32,
        )
        + jnp.einsum("kgrc,kcd->kgrd", weights_far, values_all.astype(jnp.float32), precision=HIGH)
        + gating[..., None] * jnp.einsum("kgrf,kfd->kgrd", phi_float, prefix[0], precision=HIGH)
    )
    denominator = (
        jnp.sum(weights_near, axis=-1)
        + jnp.sum(weights_far, axis=-1)
        + gating * jnp.einsum("kgrf,kf->kgr", phi_float, prefix[1], precision=HIGH)
    )
    return (
        numerator / denominator[..., None],
        weights_near,
        weights_far,
        gating,
        denominator,
        damping,
    )


def body(
    inputs,
    gain_first,
    w_query,
    a_query,
    b_query,
    key_projection_weight,
    a_key,
    key_adapter_second,
    value_projection_weight,
    a_value,
    value_adapter_second,
    feature_query,
    key_hedgehog_map,
    w_out,
    a_out,
    b_out,
    gain_second,
    w_gate,
    w_up,
    w_down,
    lengths,
    cotangent,
):
    row_count = inputs.shape[0]
    model_width = inputs.shape[1]
    head_dim = feature_query.shape[-1]
    heads_of_queries = feature_query.shape[0]
    heads_of_keys = key_hedgehog_map.shape[0]
    group_count = heads_of_queries // heads_of_keys
    columns = model_width // lax.axis_size("head")
    column_at = lax.axis_index("head") * columns
    starts = jnp.cumsum(lengths) - lengths
    within, beyond, carry_on, keeping, resets = geometry(
        lax.axis_index("seq") * row_count, row_count, starts
    )
    layout = (within, beyond, carry_on)
    residual = inputs.astype(jnp.float32)
    scale_first = rms_scale(residual)
    normed = (residual * scale_first * gain_first).astype(jnp.bfloat16)
    low_query = dot_plain(normed, a_query).astype(jnp.bfloat16)
    low_key = dot_plain(normed, a_key).astype(jnp.bfloat16)
    low_value = dot_plain(normed, a_value).astype(jnp.bfloat16)
    queries = (dot_plain(normed, w_query) + dot_plain(low_query, b_query)).astype(jnp.bfloat16)
    keys_own = (
        dot_plain(normed, key_projection_weight) + dot_plain(low_key, key_adapter_second)
    ).astype(jnp.bfloat16)
    values_own = (
        dot_plain(normed, value_projection_weight) + dot_plain(low_value, value_adapter_second)
    ).astype(jnp.bfloat16)
    query_split = queries.reshape(row_count, heads_of_queries, head_dim).transpose(1, 0, 2)
    key_split = keys_own.reshape(row_count, heads_of_keys, head_dim).transpose(1, 0, 2)
    value_split = values_own.reshape(row_count, heads_of_keys, head_dim).transpose(1, 0, 2)
    tail_pair = passed_along(
        jnp.stack([key_split[:, row_count - WINDOW :], value_split[:, row_count - WINDOW :]]),
        "seq",
        1,
    )
    keys_all = jnp.concatenate([tail_pair[0], key_split], axis=1)
    values_all = jnp.concatenate([tail_pair[1], value_split], axis=1)
    query_features = feature_map(query_split, feature_query)
    phi_keys = feature_map(keys_all, key_hedgehog_map)
    query_group = query_split.reshape(heads_of_keys, group_count, row_count, head_dim)
    phi_group = query_features.reshape(heads_of_keys, group_count, row_count, 2 * head_dim)
    own_phi = phi_keys[:, :row_count].astype(jnp.float32) * keeping[None, :, None]
    own_values = values_all[:, :row_count].astype(jnp.float32)
    local_sum = (
        jnp.einsum("kcf,kcd->kfd", own_phi, own_values, precision=HIGH),
        jnp.sum(own_phi, axis=1),
        resets,
    )
    identity = (
        jnp.zeros_like(local_sum[0]),
        jnp.zeros_like(local_sum[1]),
        jnp.zeros((), jnp.float32),
    )
    prefix = entering(local_sum, "seq", segment_join, identity, False)
    attended = attend(query_group, phi_group, keys_all, phi_keys, values_all, prefix, layout)[0]
    mixed_heads = (
        attended.reshape(heads_of_queries, row_count, head_dim)
        .transpose(1, 0, 2)
        .reshape(row_count, heads_of_queries * head_dim)
        .astype(jnp.bfloat16)
    )
    branch, low_mix = lax.psum(
        (dot_plain(mixed_heads, w_out), dot_plain(mixed_heads, a_out)), "head"
    )
    low_mix = low_mix.astype(jnp.bfloat16)
    hidden_in = residual + branch + dot_plain(low_mix, b_out)
    scale_second = rms_scale(hidden_in)
    normed_second = (hidden_in * scale_second * gain_second).astype(jnp.bfloat16)
    gate_pre = dot_plain(normed_second, w_gate)
    up_pre = dot_plain(normed_second, w_up)
    sigmoid_gate = jax.nn.sigmoid(gate_pre)
    activated = gate_pre * sigmoid_gate
    hidden = (activated * up_pre).astype(jnp.bfloat16)
    ffn_part = lax.psum_scatter(dot_plain(hidden, w_down), "head", scatter_dimension=1, tiled=True)
    block_out = (lax.dynamic_slice_in_dim(hidden_in, column_at, columns, 1) + ffn_part).astype(
        jnp.bfloat16
    )
    grad_hidden = by_transpose(cotangent, w_down)
    grad_gate = (
        grad_hidden * up_pre * sigmoid_gate * (1.0 + gate_pre * (1.0 - sigmoid_gate))
    ).astype(jnp.bfloat16)
    grad_up = (grad_hidden * activated).astype(jnp.bfloat16)
    grad_second = lax.psum(by_transpose(grad_gate, w_gate) + by_transpose(grad_up, w_up), "head")
    grad_residual = cotangent.astype(jnp.float32) + norm_back(
        grad_second, hidden_in, scale_second, gain_second
    )
    grad_gain_second = jnp.sum(grad_second * hidden_in * scale_second, axis=0)
    grad_branch = grad_residual.astype(jnp.bfloat16)
    grad_low_mix = by_transpose(grad_branch, b_out)
    grad_mixed = by_transpose(grad_branch, w_out) + by_transpose_exact(grad_low_mix, a_out)
    grad_b_out = transpose_by(low_mix, grad_branch)
    grad_a_out = transpose_by_exact(mixed_heads, grad_low_mix).T
    grad_heads = (
        grad_mixed.astype(jnp.bfloat16)
        .reshape(row_count, heads_of_queries, head_dim)
        .transpose(1, 0, 2)
        .reshape(heads_of_keys, group_count, row_count, head_dim)
    )
    attended, weights_near, weights_far, gating, denominator, damping = attend(
        query_group, phi_group, keys_all, phi_keys, values_all, prefix, layout
    )
    grad_float = grad_heads.astype(jnp.float32)
    grad_num = grad_float / denominator[..., None]
    grad_den = -jnp.sum(grad_float * attended, axis=-1) / denominator
    grad_weights = (
        jnp.einsum("kgrd,kcd->kgrc", grad_heads, values_all, preferred_element_type=jnp.float32)
        / denominator[..., None]
        + grad_den[..., None]
    )
    grad_scores = (weights_near * grad_weights).astype(jnp.bfloat16)
    grad_linear = jnp.where(beyond, grad_weights * damping, 0.0).astype(jnp.bfloat16)
    factor = head_dim ** (-0.5)
    grad_q_scores = (
        jnp.einsum("kgrc,kcd->kgrd", grad_scores, keys_all, preferred_element_type=jnp.float32)
        * factor
    )
    grad_keys = (
        jnp.einsum("kgrc,kgrd->kcd", grad_scores, query_group, preferred_element_type=jnp.float32)
        * factor
    )
    grad_phi_q = jnp.einsum(
        "kgrc,kcf->kgrf", grad_linear, phi_keys, preferred_element_type=jnp.float32
    )
    grad_phi_k = jnp.einsum(
        "kgrc,kgrf->kcf", grad_linear, phi_group, preferred_element_type=jnp.float32
    )
    mixed_weights = weights_near.astype(jnp.bfloat16).astype(jnp.float32) + weights_far
    grad_values = jnp.einsum("kgrc,kgrd->kcd", mixed_weights, grad_num, precision=HIGH)
    state_grad = gating[..., None] * grad_num
    phi_float = phi_group.astype(jnp.float32)
    grad_phi_q = (
        grad_phi_q
        + jnp.einsum("kgrd,kfd->kgrf", state_grad, prefix[0], precision=HIGH)
        + (gating * grad_den)[..., None] * prefix[1][:, None, None, :]
    )
    grad_state = jnp.einsum("kgrf,kgrd->kfd", phi_float, state_grad, precision=HIGH)
    grad_norms = jnp.einsum("kgrf,kgr->kf", phi_float, gating * grad_den, precision=HIGH)
    suffix = entering((grad_state, grad_norms, resets), "seq", segment_join, identity, True)
    padding = ((0, 0), (0, WINDOW), (0, 0))
    grad_phi_k = grad_phi_k + jnp.pad(
        (jnp.einsum("kfd,kcd->kcf", suffix[0], own_values, precision=HIGH) + suffix[1][:, None, :])
        * keeping[None, :, None],
        padding,
    )
    grad_values = grad_values + jnp.pad(
        jnp.einsum("kcf,kfd->kcd", own_phi, suffix[0], precision=HIGH), padding
    )
    grad_key_feature, grad_feature_key = feature_back(keys_all, key_hedgehog_map, grad_phi_k)
    grad_keys = grad_keys + grad_key_feature
    grad_query_feature, grad_feature_query = feature_back(
        query_split, feature_query, grad_phi_q.reshape(heads_of_queries, row_count, 2 * head_dim)
    )
    grad_query = grad_q_scores.reshape(heads_of_queries, row_count, head_dim) + grad_query_feature
    returned = passed_along(jnp.stack([grad_keys[:, :WINDOW], grad_values[:, :WINDOW]]), "seq", -1)
    tail_pad = ((0, 0), (row_count - WINDOW, 0), (0, 0))
    grad_keys_own = grad_keys[:, WINDOW:] + jnp.pad(returned[0], tail_pad)
    grad_values_own = grad_values[:, WINDOW:] + jnp.pad(returned[1], tail_pad)
    grad_q_rows = (
        grad_query.transpose(1, 0, 2)
        .reshape(row_count, heads_of_queries * head_dim)
        .astype(jnp.bfloat16)
    )
    grad_k_rows = (
        grad_keys_own.transpose(1, 0, 2)
        .reshape(row_count, heads_of_keys * head_dim)
        .astype(jnp.bfloat16)
    )
    grad_v_rows = (
        grad_values_own.transpose(1, 0, 2)
        .reshape(row_count, heads_of_keys * head_dim)
        .astype(jnp.bfloat16)
    )
    grad_low_query = by_transpose(grad_q_rows, b_query)
    grad_low_key = by_transpose(grad_k_rows, key_adapter_second)
    grad_low_value = by_transpose(grad_v_rows, value_adapter_second)
    grad_b_query = transpose_by(low_query, grad_q_rows)
    grad_b_key = transpose_by(low_key, grad_k_rows)
    grad_b_value = transpose_by(low_value, grad_v_rows)
    grad_a_query = transpose_by_exact(normed, grad_low_query)
    grad_a_key = transpose_by_exact(normed, grad_low_key)
    grad_a_value = transpose_by_exact(normed, grad_low_value)
    partial_first = (
        by_transpose(grad_q_rows, w_query)
        + by_transpose(grad_k_rows, key_projection_weight)
        + by_transpose(grad_v_rows, value_projection_weight)
        + by_transpose_exact(grad_low_query, a_query)
        + by_transpose_exact(grad_low_key, a_key)
        + by_transpose_exact(grad_low_value, a_value)
    )
    grad_first = lax.psum(partial_first, "head")
    grad_full = grad_residual + norm_back(grad_first, residual, scale_first, gain_first)
    grad_inputs = lax.dynamic_slice_in_dim(grad_full, column_at, columns, 1)
    grad_gain_first = jnp.sum(grad_first * residual * scale_first, axis=0)
    packed = pack_small(
        jnp.concatenate([grad_a_query, grad_a_key, grad_a_value], axis=1).T,
        0.25 * grad_b_out,
        grad_feature_query,
        grad_feature_key,
        jnp.concatenate([grad_b_query, grad_b_key, grad_b_value], axis=1),
        grad_a_out,
        lax.dynamic_slice_in_dim(grad_gain_first, column_at, columns, 0),
        lax.dynamic_slice_in_dim(grad_gain_second, column_at, columns, 0),
    )
    out_ffn, out_att, out_pack = seq_sums(
        jnp.stack([by_owner(normed_second), by_owner(cotangent)]),
        jnp.concatenate([tiles_of(a, FFN_WIDTH) for a in (grad_gate, grad_up, hidden)]),
        jnp.stack([by_owner(normed), by_owner(grad_branch)]),
        jnp.concatenate(
            [tiles_of(a, ATT_WIDTH) for a in (grad_q_rows, jnp.concatenate([grad_k_rows, grad_v_rows], axis=1), mixed_heads)]
        ),
        packed,
    )
    a_rows, b_out_sum, f_query, f_key, b_rows, a_out_sum, gain_one, gain_two = unpack_small(out_pack)
    a_rows = a_rows.T
    return (
        block_out,
        grad_inputs,
        gain_one,
        untile(out_att[:2]),
        a_rows[:, :8],
        b_rows[:, :512],
        out_att[2, :, :128],
        a_rows[:, 8:16],
        b_rows[:, 512:640],
        out_att[2, :, 128:],
        a_rows[:, 16:],
        b_rows[:, 640:],
        f_query,
        f_key,
        untile(out_att[3:]).T,
        a_out_sum.T,
        b_out_sum,
        gain_two,
        untile(out_ffn[:4]),
        untile(out_ffn[4:8]),
        untile(out_ffn[8:]).T,
    )


def solution(mesh):
    return jax.shard_map(
        body,
        mesh=mesh,
        in_specs=(
            P("seq", None),
            P(),
            P(None, "head"),
            P(),
            P(None, "head"),
            P(None, "head"),
            P(),
            P(None, "head"),
            P(None, "head"),
            P(),
            P(None, "head"),
            P("head", None, None),
            P("head", None, None),
            P("head", None),
            P("head", None),
            P(),
            P(),
            P(None, "head"),
            P(None, "head"),
            P("head", None),
            P(),
            P("seq", None),
        ),
        out_specs=(
            P("seq", "head"),
            P("seq", "head"),
            P("head"),
            P("seq", "head"),
            P(),
            P(None, "head"),
            P("seq", "head"),
            P(),
            P(None, "head"),
            P("seq", "head"),
            P(),
            P(None, "head"),
            P("head", None, None),
            P("head", None, None),
            P("head", "seq"),
            P("head", None),
            P(),
            P("head"),
            P("seq", "head"),
            P("seq", "head"),
            P("head", "seq"),
        ),
        check_vma=False,
    )
```

```python
import jax
import jax.numpy as jnp
from jax import lax
from jax.experimental import pallas as pl
from jax.experimental.pallas import tpu as pltpu
from jax.sharding import PartitionSpec as P

MESH = pl.DeviceIdType.MESH
F32 = jnp.float32
BF16 = jnp.bfloat16


def spot():
    s = lax.axis_index("seq")
    y = lax.axis_index("head")
    return lax.div(s, 8), lax.rem(lax.div(s, 2), 4), lax.rem(s, 2), y


def at(z, x, c, y):
    return ((z * 4 + x) * 2 + c, y)


def turned(p, steps):
    return lax.rem(p + steps, 4)


def greet(partners):
    barrier = pltpu.get_barrier_semaphore()
    for partner in partners:
        pl.semaphore_signal(barrier, inc=1, device_id=partner, device_id_type=MESH)
    pl.semaphore_wait(barrier, len(partners))


def send(src, dst, ss, rs, device):
    return pltpu.make_async_remote_copy(
        src_ref=src, dst_ref=dst, send_sem=ss, recv_sem=rs, device_id=device, device_id_type=MESH
    )


class Ring:
    def __init__(self, refs, rows, term, finish):
        self.sb, self.ra, self.rf, self.ra3, self.rf3, self.ss, self.rs = refs
        self.rows, self.term, self.finish = rows, term, finish
        z, x, c, y = spot()
        self.axes = (
            (x, at(z, turned(x, 1), c, y), at(z, turned(x, 3), c, y)),
            (z, at(turned(z, 1), x, c, y), at(turned(z, 3), x, c, y)),
        )

    @staticmethod
    def scratch(count, rows, width):
        return [
            pltpu.VMEM((count, 2, 4 * rows, width), BF16),
            pltpu.VMEM((count, 2, 2 * rows, width), BF16),
            pltpu.VMEM((count, 2, 4 * rows, width), BF16),
            pltpu.VMEM((count, 2, rows // 2, width), BF16),
            pltpu.VMEM((count, 2, rows, width), BF16),
            pltpu.SemaphoreType.DMA((count, 12)),
            pltpu.SemaphoreType.DMA((count, 12)),
        ]

    def block(self, b, part):
        g = self.rows // 2
        if part is None:
            return pl.ds(pl.multiple_of(b * self.rows, self.rows), self.rows)
        return pl.ds(pl.multiple_of(b * self.rows + part * g, g), g)

    def copy(self, t, k, i):
        p, ahead, behind = self.axes[k]
        q, ahead3, behind3 = self.axes[1 - k]
        h, g = 2 * self.rows, self.rows // 2
        lo, hi, lo3, hi3 = pl.ds(0, h), pl.ds(h, h), pl.ds(0, g), pl.ds(g, g)
        sb, ra, rf, ra3, rf3, block = self.sb, self.ra, self.rf, self.ra3, self.rf3, self.block
        src, dst, device = (
            lambda: (sb.at[t, 0, lo], ra.at[t, 0], ahead),
            lambda: (sb.at[t, 0, hi], ra.at[t, 1], behind),
            lambda: (sb.at[t, 1, hi], rf.at[t, 0, hi], ahead),
            lambda: (sb.at[t, 1, lo], rf.at[t, 1, lo], behind),
            lambda: (ra.at[t, 0], rf.at[t, 0, lo], ahead),
            lambda: (ra.at[t, 1], rf.at[t, 1, hi], behind),
            lambda: (sb.at[t, 0, block(turned(q, 2), 0)], ra3.at[t, 0], ahead3),
            lambda: (sb.at[t, 0, block(turned(q, 2), 1)], ra3.at[t, 1], behind3),
            lambda: (sb.at[t, 0, block(turned(q, 1), 1)], rf3.at[t, 0, hi3], ahead3),
            lambda: (sb.at[t, 0, block(turned(q, 3), 0)], rf3.at[t, 1, lo3], behind3),
            lambda: (ra3.at[t, 0], rf3.at[t, 0, lo3], ahead3),
            lambda: (ra3.at[t, 1], rf3.at[t, 1, hi3], behind3),
        )[i]()
        return send(src, dst, self.ss.at[t, i], self.rs.at[t, i], device)

    def start(self, t, k):
        p = self.axes[k][0]
        h = 2 * self.rows
        self.sb[t, 0] = self.term(t, k, turned(p, 2), 0, 4).astype(BF16)
        self.copy(t, k, 0).start()
        self.copy(t, k, 1).start()
        self.sb[t, 1, h:] = self.term(t, k, turned(p, 1), 2, 4).astype(BF16)
        self.copy(t, k, 2).start()
        self.sb[t, 1, :h] = self.term(t, k, turned(p, 3), 0, 2).astype(BF16)
        self.copy(t, k, 3).start()

    def merge(self, t, k):
        p = self.axes[k][0]
        for way, dest, first in ((0, turned(p, 1), 0), (1, turned(p, 3), 2)):
            self.copy(t, k, way).wait_recv()
            self.ra[t, way] = (self.term(t, k, dest, first, first + 2) + self.ra[t, way].astype(F32)).astype(BF16)
            self.copy(t, k, 4 + way).start()

    def cross(self, t, k):
        p = self.axes[k][0]
        own = self.term(t, k, p, 0, 4)
        for i in (0, 1):
            self.copy(t, k, i).wait_send()
        for i in (2, 3, 4, 5):
            self.copy(t, k, i).wait_recv()
        self.sb[t, 0] = (own + self.rf[t, 0].astype(F32) + self.rf[t, 1].astype(F32)).astype(BF16)
        for i in (6, 7, 8, 9):
            self.copy(t, k, i).start()

    def merge_cross(self, t, k):
        q = self.axes[1 - k][0]
        for way, dest in ((0, turned(q, 1)), (1, turned(q, 3))):
            self.copy(t, k, 6 + way).wait_recv()
            mine = self.sb[t, 0, self.block(dest, way), :]
            self.ra3[t, way] = (mine.astype(F32) + self.ra3[t, way].astype(F32)).astype(BF16)
            self.copy(t, k, 10 + way).start()

    def end(self, t, k):
        q = self.axes[1 - k][0]
        for i in (8, 9, 10, 11):
            self.copy(t, k, i).wait_recv()
        mine = self.sb[t, 0, self.block(q, None), :].astype(F32)
        self.finish(t, k, mine + self.rf3[t, 0].astype(F32) + self.rf3[t, 1].astype(F32))

    def drain(self, t, k):
        for i in range(2, 12):
            self.copy(t, k, i).wait_send()


def over_pairs(first, last, step):
    def both(u, carry):
        step(2 * u, 0)
        step(2 * u + 1, 1)
        return carry

    lax.fori_loop(first, last, both, 0)


FFN_TILES, FFN_WIDTH = 12, 512
ATT_TILES, ATT_WIDTH = 5, 256
PACK = 32


def untile(tiles):
    return tiles.transpose(1, 0, 2).reshape(tiles.shape[1], -1)


def unpack_small(packed):
    flat = packed.reshape(32, 32, 128)
    top = flat[:, :16].reshape(16, 2, 16, 128).transpose(1, 2, 0, 3).reshape(2, 16, 2048)
    a_rows = jnp.concatenate([top[0, :12], top[1, :12]])
    b_out = jnp.concatenate([top[0, 12:], top[1, 12:]])
    bottom = flat[:, 16:]
    f_query = bottom[:16].reshape(4, 64, 2, 64).transpose(0, 2, 1, 3).reshape(8, 64, 64)
    f_key = bottom[16:20].reshape(64, 2, 64).transpose(1, 0, 2)
    b_rows = bottom[20:23].reshape(6, 8, 128).transpose(1, 0, 2).reshape(8, 768)
    a_out = bottom[23:25].reshape(4, 8, 128).transpose(1, 0, 2).reshape(8, 512)
    gains = bottom[25]
    return a_rows, b_out, f_query, f_key, b_rows, a_out, gains[:4].reshape(512), gains[4:8].reshape(512)


EPS = 1e-05
NEG = -1e30
HIGH = lax.Precision.HIGHEST
ROWS = 256
WINDOW = 64
SPAN = ROWS + WINDOW
COLS = 512
HEADS, KEY_HEADS, DIM = 8, 2, 64
STATE = 72


def mm(a, b):
    return jnp.dot(a, b, preferred_element_type=F32)


def mm_nt(a, b, precision=None):
    return lax.dot_general(a, b, (((1,), (1,)), ((), ())), precision=precision, preferred_element_type=F32)


def mm_tn(a, b, precision=None):
    return lax.dot_general(a, b, (((0,), (0,)), ((), ())), precision=precision, preferred_element_type=F32)


def halves(value):
    top = value.astype(BF16)
    return top, (value - top.astype(F32)).astype(BF16)


def soft_pair(rows, table):
    both = mm(rows, jnp.concatenate([table, -table], axis=1))
    left = lax.broadcasted_iota(jnp.int32, both.shape, 1) < DIM
    upper = jnp.max(jnp.where(left, both, NEG), axis=1, keepdims=True)
    lower = jnp.max(jnp.where(left, NEG, both), axis=1, keepdims=True)
    grown = jnp.exp(both - jnp.where(left, upper, lower))
    sum_left = jnp.sum(jnp.where(left, grown, 0.0), axis=1, keepdims=True)
    sum_right = jnp.sum(jnp.where(left, 0.0, grown), axis=1, keepdims=True)
    return grown / jnp.where(left, sum_left, sum_right)


def doc_at(positions, lengths):
    first = lengths[0]
    second = first + lengths[1]
    return (
        (positions >= 0).astype(jnp.int32)
        + (positions >= first).astype(jnp.int32)
        + (positions >= second).astype(jnp.int32)
    )


def write_masks(near, far, lengths):
    base = lax.axis_index("seq") * ROWS
    row = lax.broadcasted_iota(jnp.int32, (ROWS, SPAN), 0) + base
    column = lax.broadcasted_iota(jnp.int32, (ROWS, SPAN), 1) + base - WINDOW
    same = doc_at(row, lengths) == doc_at(column, lengths)
    offset = row - column
    near[...] = jnp.where(same & (offset >= 0) & (offset < WINDOW), 0.0, NEG)
    far[...] = jnp.where(same & (offset >= WINDOW), 1.0, 0.0)


def middle(count, first, lengths):
    base = lax.axis_index("seq") * ROWS + first
    position = lax.broadcasted_iota(jnp.int32, (count, 1), 0) + base
    return (doc_at(position, lengths) == 2).astype(F32)


def value_columns(kv):
    lane = lax.broadcasted_iota(jnp.int32, kv.shape, 1)
    v = jnp.concatenate([kv[:, DIM:], kv[:, :DIM]], axis=1)
    return jnp.where(lane < DIM, v, jnp.where(lane == DIM, 1.0, 0.0).astype(kv.dtype))


class Scan:
    def __init__(self, refs, reverse):
        self.own, self.pair, self.line, self.plane, self.sem = refs
        self.reverse = reverse
        z, x, c, y = spot()
        self.z, self.x, self.c = z, x, c
        self.sibling = at(z, x, 1 - c, y)
        self.x_mates = [at(z, turned(x, i), c, y) for i in (1, 2, 3)]
        self.z_mates = [at(turned(z, i), x, c, y) for i in (1, 2, 3)]

    @staticmethod
    def scratch(shape):
        return [
            pltpu.VMEM((3, *shape), F32),
            pltpu.VMEM(shape, F32),
            pltpu.VMEM((3, *shape), F32),
            pltpu.VMEM((3, *shape), F32),
            pltpu.SemaphoreType.DMA((2, 7)),
        ]

    def pair_copy(self):
        return send(self.own.at[0], self.pair, self.sem.at[0, 0], self.sem.at[1, 0], self.sibling)

    def line_copy(self, i):
        return send(self.own.at[1], self.line.at[i], self.sem.at[0, 1 + i], self.sem.at[1, 1 + i], self.x_mates[i])

    def plane_copy(self, i):
        return send(self.own.at[2], self.plane.at[i], self.sem.at[0, 4 + i], self.sem.at[1, 4 + i], self.z_mates[i])

    def counts(self, me, other):
        return ((other > me) if self.reverse else (other < me)).astype(F32)

    def open(self):
        self.pair_copy().start()

    def along_x(self):
        self.pair_copy().wait()
        self.own[1] = self.own[0] + self.pair[...]
        for i in range(3):
            self.line_copy(i).start()

    def along_z(self):
        for i in range(3):
            self.line_copy(i).wait()
        self.own[2] = self.own[1] + self.line[0] + self.line[1] + self.line[2]
        for i in range(3):
            self.plane_copy(i).start()

    def close(self):
        for i in range(3):
            self.plane_copy(i).wait()
        total = self.pair[...] * self.counts(self.c, 1 - self.c)
        for i in range(3):
            total = total + self.line[i] * self.counts(self.x, turned(self.x, 3 - i))
        for i in range(3):
            total = total + self.plane[i] * self.counts(self.z, turned(self.z, 3 - i))
        return total


def front_kernel(
    x_ref, gain_one, gain_two, a_in, b_q, b_k, b_v, f_q, f_k, a_out, b_out, lengths, w_q, w_k, w_v, w_o,
    normed_out, low_out, q_out, kv_out, state_out, att_out, stat_out, mixed_out, lowmix_out, hidden_out, ns_out, r2_out, r1_out,
    wq, wk, wv, wo, w_sem, qh, phq, phk, num, near, far, tail_sem,
    part, came, y_sem, low_part, low_came, square, square_came,
    *scan_refs,
):
    z, x, c, y = spot()
    s = lax.axis_index("seq")
    following, leading = (lax.rem(s + 1, 32), y), (lax.rem(s + 31, 32), y)
    y_mates = [at(z, x, c, turned(y, i)) for i in (1, 2, 3)]
    scan = Scan(scan_refs, False)
    greet([following, leading, scan.sibling] + scan.x_mates + scan.z_mates + y_mates)
    loads = [
        pltpu.make_async_copy(src, dst, w_sem.at[i])
        for i, (src, dst) in enumerate(((w_q, wq), (w_k, wk), (w_v, wv), (w_o, wo)))
    ]
    for load in loads:
        load.start()
    for i in range(4):
        rows = pl.ds(64 * i, 64)
        value = x_ref[rows, :].astype(F32)
        scale = lax.rsqrt(jnp.mean(value * value, axis=1, keepdims=True) + EPS)
        r1_out[rows, :] = scale
        normed_out[rows, :] = (value * scale * gain_one[...]).astype(BF16)
    write_masks(near, far, lengths)
    low_out[...] = mm(normed_out[...], a_in[...]).astype(BF16)
    low = low_out[...]
    loads[1].wait()
    loads[2].wait()
    k = (mm(normed_out[...], wk[...]) + mm(low[:, 8:16], b_k[...])).astype(BF16)
    v = (mm(normed_out[...], wv[...]) + mm(low[:, 16:24], b_v[...])).astype(BF16)
    for j in range(KEY_HEADS):
        cut = slice(j * DIM, (j + 1) * DIM)
        kv_out[j, WINDOW:] = jnp.concatenate([k[:, cut], v[:, cut]], axis=1)
    tail = send(
        kv_out.at[:, pl.ds(ROWS, WINDOW)], kv_out.at[:, pl.ds(0, WINDOW)], tail_sem.at[0], tail_sem.at[1], following
    )
    tail.start()
    loads[0].wait()
    for i in range(2):
        cut = slice(i * 256, (i + 1) * 256)
        q_out[:, cut] = (mm(normed_out[...], wq[:, cut]) + mm(low[:, :8], b_q[:, cut])).astype(BF16)
    for h in range(HEADS):
        qh[h] = q_out[:, h * DIM : (h + 1) * DIM]
    tail.wait()
    inside = middle(ROWS, -WINDOW, lengths)
    for j in range(KEY_HEADS):
        phk[j] = soft_pair(kv_out[j][:, :DIM], f_k[j]).astype(BF16)
        counted = (phk[j, :ROWS].astype(F32) * inside).astype(BF16)
        scan.own[0, j] = mm_tn(value_columns(kv_out[j, :ROWS]), counted)[:STATE]
    scan.open()

    def features(h, carry):
        phq[h] = soft_pair(qh[h], f_q[h]).astype(BF16)
        return carry

    lax.fori_loop(0, HEADS, features, 0)
    scan.along_x()

    def inner(h, carry):
        j = lax.div(h, 4)
        kv = kv_out[j]
        scores = mm_nt(qh[h], kv[:, :DIM]) * (DIM**-0.5) + near[...]
        top = jnp.max(scores, axis=1, keepdims=True)
        weights = jnp.exp(scores - top)
        distant = mm_nt(phq[h], phk[j]) * far[...] * jnp.exp(-top)
        total = weights + distant
        high = total.astype(BF16)
        rest = ((total - high.astype(F32)) * far[...]).astype(BF16)
        v = kv[:, DIM:]
        num[h] = mm(high, v) + mm(rest, v)
        stat_out[h, :, 0:1] = top
        stat_out[h, :, 1:2] = jnp.sum(total, axis=1, keepdims=True)
        return carry

    lax.fori_loop(0, 4, inner, 0)
    scan.along_z()
    lax.fori_loop(4, HEADS, inner, 0)
    state_out[...] = scan.close()
    mine = middle(ROWS, 0, lengths)
    for h in range(HEADS):
        top, rest = halves(state_out[h // 4])
        carried = mm_nt(phq[h], top) + mm_nt(phq[h], rest)
        gate = jnp.exp(-stat_out[h, :, 0:1]) * mine
        total = stat_out[h, :, 1:2] + gate * carried[:, DIM : DIM + 1]
        stat_out[h, :, 1:2] = total
        stat_out[h, :, 2:3] = gate
        cut = slice(h * DIM, (h + 1) * DIM)
        attended = (num[h] + gate * carried[:, :DIM]) / total
        att_out[:, cut] = attended
        mixed_out[:, cut] = attended.astype(BF16)
    mixed = mixed_out[...]
    low_part[0] = mm_nt(a_out[...], mixed)
    low_turns = [send(low_part.at[0], low_came.at[i], y_sem.at[0, i], y_sem.at[1, i], y_mates[i]) for i in range(3)]
    for turn in low_turns:
        turn.start()
    loads[3].wait()

    def columns(ref, d):
        return ref[:, pl.ds(pl.multiple_of(d * COLS, COLS), COLS)]

    turns = [send(part.at[i], came.at[i], y_sem.at[0, 3 + i], y_sem.at[1, 3 + i], y_mates[i]) for i in range(3)]
    for i in (1, 0, 2):
        part[i] = mm(mixed, columns(wo, turned(y, 1 + i))).astype(BF16)
        turns[i].start()
    value = mm(mixed, columns(wo, y)) + columns(x_ref, y).astype(F32)
    for turn in low_turns:
        turn.wait()
    low_sum = low_part[0] + low_came[0] + low_came[1] + low_came[2]
    lowmix_out[...] = low_sum.T.astype(BF16)
    value = value + mm(lowmix_out[...], columns(b_out, y))
    for turn in turns:
        turn.wait()
    value = value + came[0].astype(F32) + came[1].astype(F32) + came[2].astype(F32)
    hidden_out[...] = value
    square[...] = mm_nt(jnp.ones((8, COLS), F32), value * value, HIGH)
    turns = [send(square, square_came.at[i], y_sem.at[0, 6 + i], y_sem.at[1, 6 + i], y_mates[i]) for i in range(3)]
    for turn in turns:
        turn.start()
    for turn in turns:
        turn.wait()
    mean = (square[...] + square_came[0] + square_came[1] + square_came[2]) * (1.0 / 2048)
    scale = lax.rsqrt(mean + EPS).T[:, 0:1]
    r2_out[...] = scale
    ns_out[y] = (hidden_out[...] * scale * columns(gain_two, y)).astype(BF16)
    turns = [send(ns_out.at[y], ns_out.at[y], y_sem.at[0, 9 + i], y_sem.at[1, 9 + i], y_mates[i]) for i in range(3)]
    for turn in turns:
        turn.start()
    for i in range(3):
        here = ns_out.at[turned(y, 3 - i)]
        send(here, here, y_sem.at[0, 9 + i], y_sem.at[1, 9 + i], y_mates[i]).wait_recv()
    for turn in turns:
        turn.wait_send()


def front(x, gain_one, gain_two, a_in, b_q, b_k, b_v, f_q, f_k, a_out, b_out, lengths, w_q, w_k, w_v, w_o):
    anywhere = pl.BlockSpec(memory_space=pl.ANY)
    vmem = pl.BlockSpec(memory_space=pltpu.VMEM)
    shapes = (
        ((ROWS, 2048), BF16),
        ((ROWS, 24), BF16),
        ((ROWS, 512), BF16),
        ((KEY_HEADS, SPAN, 128), BF16),
        ((KEY_HEADS, STATE, 128), F32),
        ((ROWS, 512), F32),
        ((HEADS, ROWS, 8), F32),
        ((ROWS, 512), BF16),
        ((ROWS, 8), BF16),
        ((ROWS, COLS), F32),
        ((4, ROWS, COLS), BF16),
        ((ROWS, 1), F32),
        ((ROWS, 1), F32),
    )
    return pl.pallas_call(
        front_kernel,
        out_shape=tuple(jax.ShapeDtypeStruct(*shape) for shape in shapes),
        in_specs=[vmem] * 11 + [pl.BlockSpec(memory_space=pltpu.SMEM)] + [anywhere] * 4,
        out_specs=(vmem,) * len(shapes),
        scratch_shapes=[
            pltpu.VMEM((2048, 512), BF16),
            pltpu.VMEM((2048, 128), BF16),
            pltpu.VMEM((2048, 128), BF16),
            pltpu.VMEM((512, 2048), BF16),
            pltpu.SemaphoreType.DMA((4,)),
            pltpu.VMEM((HEADS, ROWS, DIM), BF16),
            pltpu.VMEM((HEADS, ROWS, 128), BF16),
            pltpu.VMEM((KEY_HEADS, SPAN, 128), BF16),
            pltpu.VMEM((HEADS, ROWS, DIM), F32),
            pltpu.VMEM((ROWS, SPAN), F32),
            pltpu.VMEM((ROWS, SPAN), F32),
            pltpu.SemaphoreType.DMA((2,)),
            pltpu.VMEM((3, ROWS, COLS), BF16),
            pltpu.VMEM((3, ROWS, COLS), BF16),
            pltpu.SemaphoreType.DMA((2, 12)),
            pltpu.VMEM((1, 8, ROWS), F32),
            pltpu.VMEM((3, 8, ROWS), F32),
            pltpu.VMEM((8, ROWS), F32),
            pltpu.VMEM((3, 8, ROWS), F32),
            *Scan.scratch((KEY_HEADS, STATE, 128)),
        ],
        compiler_params=pltpu.CompilerParams(
            collective_id=1, has_side_effects=True, vmem_limit_bytes=60 * 2**20
        ),
        name="front",
    )(x, gain_one, gain_two, a_in, b_q, b_k, b_v, f_q, f_k, a_out, b_out, lengths, w_q, w_k, w_v, w_o)


def ffn_kernel(ns, cot, normed, wg, wu, wd, y_out, gs_out, ffn_out, xt_out, gs_sum, ffn_sum):
    j = pl.program_id(0)
    gate = jnp.zeros((ROWS, COLS), F32)
    up = jnp.zeros((ROWS, COLS), F32)
    for k in range(4):
        cut = slice(k * COLS, (k + 1) * COLS)
        gate = gate + mm(ns[k], wg[cut])
        up = up + mm(ns[k], wu[cut])
    grad = mm_nt(cot[...], wd[...])
    sigmoid = jax.nn.sigmoid(gate)
    active = gate * sigmoid
    hidden = (active * up).astype(BF16)
    grad_gate = (grad * up * sigmoid * (1.0 + gate * (1.0 - sigmoid))).astype(BF16)
    grad_up = (grad * active).astype(BF16)
    y_out[0, 0] = grad_gate
    y_out[1, 0] = grad_up
    y_out[2, 0] = hidden
    for k in range(4):
        cut = slice(k * COLS, (k + 1) * COLS)
        back = mm_nt(grad_gate, wg[cut]) + mm_nt(grad_up, wu[cut])
        forth = mm(hidden, wd[:, cut])

        @pl.when(j == 0)
        def _():
            gs_sum[k] = back
            ffn_sum[k] = forth

        @pl.when((j > 0) & (j < 3))
        def _():
            gs_sum[k] = gs_sum[k] + back
            ffn_sum[k] = ffn_sum[k] + forth

        @pl.when(j == 3)
        def _():
            gs_out[k] = (gs_sum[k] + back).astype(BF16)
            ffn_out[k] = (ffn_sum[k] + forth).astype(BF16)

    def turn(m, block_of):
        for i in range(16):
            block = block_of(i).T
            xt_out[m, 0, i // 4, i % 4] = block[:64]
            xt_out[m, 1, i // 4, i % 4] = block[64:]

    @pl.when(j == 0)
    def _():
        turn(0, lambda i: ns[i // 4, :, (i % 4) * 128 : (i % 4 + 1) * 128])

    @pl.when(j == 1)
    def _():
        turn(1, lambda i: cot[:, i * 128 : (i + 1) * 128])

    @pl.when(j == 2)
    def _():
        turn(2, lambda i: normed[:, i * 128 : (i + 1) * 128])


def ffn(ns, cot, normed, w_gate, w_up, w_down):
    def whole(*shape):
        return pl.BlockSpec(shape, lambda j: (0,) * len(shape))

    return pl.pallas_call(
        ffn_kernel,
        grid=(4,),
        out_shape=(
            jax.ShapeDtypeStruct((3, 4, ROWS, COLS), BF16),
            jax.ShapeDtypeStruct((4, ROWS, COLS), BF16),
            jax.ShapeDtypeStruct((4, ROWS, COLS), BF16),
            jax.ShapeDtypeStruct((3, 2, 4, 4, 64, ROWS), BF16),
        ),
        in_specs=[
            whole(4, ROWS, COLS),
            whole(ROWS, 2048),
            whole(ROWS, 2048),
            pl.BlockSpec((2048, COLS), lambda j: (0, j)),
            pl.BlockSpec((2048, COLS), lambda j: (0, j)),
            pl.BlockSpec((COLS, 2048), lambda j: (j, 0)),
        ],
        out_specs=(
            pl.BlockSpec((3, 1, ROWS, COLS), lambda j: (0, j, 0, 0)),
            whole(4, ROWS, COLS),
            whole(4, ROWS, COLS),
            whole(3, 2, 4, 4, 64, ROWS),
        ),
        scratch_shapes=[pltpu.VMEM((4, ROWS, COLS), F32), pltpu.VMEM((4, ROWS, COLS), F32)],
        compiler_params=pltpu.CompilerParams(vmem_limit_bytes=60 * 2**20),
        name="ffn",
    )(ns, cot, normed, w_gate, w_up, w_down)


def soft_back(soft, grad):
    left = lax.broadcasted_iota(jnp.int32, soft.shape, 1) < DIM
    part = soft * grad
    sum_left = jnp.sum(jnp.where(left, part, 0.0), axis=1, keepdims=True)
    sum_right = jnp.sum(jnp.where(left, 0.0, part), axis=1, keepdims=True)
    both = part - soft * jnp.where(left, sum_left, sum_right)
    return both[:, :DIM] - both[:, DIM:]


def back_kernel(
    hidden_in, r1, r2, gain_one, gain_two, mixed, low_mix, att, stat, state, q_in, kv, low,
    f_q, f_k, a_in, a_out, b_out, b_q, b_k, b_v, lengths,
    gs_hbm, ffn_hbm, normed_hbm, x_hbm, cot_hbm, xt_hbm, y_hbm, w_q, w_k, w_v, w_o,
    out_block, out_inputs, out_ffn, out_att, out_pack,
    wide_w, wk, wv, x_own, cot_own, gs_own, ffn_own, w_sem,
    gs_came, ffn_came, gf_part, dot_part, dot_came, gb, gres, gsum, y_sem,
    xf, yf, sem_ffn, xa, ya, xgb, sem_att, pk, sem_pack,
    near, far, qh, gh, pq, pkey, dext, dk, dv, gfq, gfk, ret, ret_came, ret_sem, glow, gkv, wide, gao, gbo,
    ysum, sem_zx,
    *rest,
):
    scan = Scan(rest[0:5], True)
    refs_big, refs_mid, refs_low = rest[5:12], rest[12:19], rest[19:26]
    z, x, c, y = spot()
    s = lax.axis_index("seq")
    following, leading = (lax.rem(s + 1, 32), y), (lax.rem(s + 31, 32), y)
    y_mates = [at(z, x, c, turned(y, i)) for i in (1, 2, 3)]
    sibling = scan.sibling
    greet([following, leading, sibling] + scan.x_mates + scan.z_mates + y_mates)

    def columns(ref, d):
        return ref[:, pl.ds(pl.multiple_of(d * COLS, COLS), COLS)]

    def to_mates(base, pieces, slots):
        return [
            send(pieces(i), slots.at[i], y_sem.at[0, base + i], y_sem.at[1, base + i], y_mates[i]) for i in range(3)
        ]

    own_columns = pl.ds(pl.multiple_of(y * COLS, COLS), COLS)
    gs_turns = to_mates(0, lambda i: gs_hbm.at[turned(y, 1 + i)], gs_came)
    for turn in gs_turns:
        turn.start()
    early = [
        pltpu.make_async_copy(src, dst, w_sem.at[i])
        for i, (src, dst) in enumerate(
            (
                (gs_hbm.at[y], gs_own),
                (cot_hbm.at[:, own_columns], cot_own),
                (x_hbm.at[:, own_columns], x_own),
                (ffn_hbm.at[y], ffn_own),
                (w_k, wk),
                (w_v, wv),
            )
        )
    ]

    def quarter(k):
        return pl.ds(k * COLS, COLS)

    load_o = [pltpu.make_async_copy(w_o.at[:, quarter(k)], wide_w.at[k], w_sem.at[6 + k]) for k in range(4)]
    load_q = [pltpu.make_async_copy(w_q.at[quarter(k)], wide_w.at[k], w_sem.at[10 + k]) for k in range(4)]
    load_n = [pltpu.make_async_copy(normed_hbm.at[:, quarter(k)], gb.at[k], w_sem.at[14 + k]) for k in range(4)]
    own_rows, far_rows = pl.ds(0, ROWS), pl.ds(ROWS, ROWS)

    def left_ffn(m):
        return [
            pltpu.make_async_copy(xt_hbm.at[m, c], xf.at[m, :, :, :, own_rows], sem_ffn.at[0, m]),
            send(xt_hbm.at[m, 1 - c], xf.at[m, :, :, :, far_rows], sem_ffn.at[1, m], sem_ffn.at[2, m], sibling),
        ]

    def right_ffn(t):
        return [
            pltpu.make_async_copy(y_hbm.at[t], yf.at[t, own_rows], sem_ffn.at[0, 2 + t]),
            send(y_hbm.at[t], yf.at[t, far_rows], sem_ffn.at[1, 2 + t], sem_ffn.at[2, 2 + t], sibling),
        ]

    left_att = [
        pltpu.make_async_copy(xt_hbm.at[2, c], xa.at[0, :, :, :, own_rows], sem_att.at[0, 0]),
        send(xt_hbm.at[2, 1 - c], xa.at[0, :, :, :, far_rows], sem_att.at[1, 0], sem_att.at[2, 0], sibling),
    ]

    def right_att(t):
        return send(ya.at[t, own_rows], ya.at[t, far_rows], sem_att.at[1, 2 + t], sem_att.at[2, 2 + t], sibling)

    for m in range(2):
        for copy in left_ffn(m):
            copy.start()

    def open_ffn(t, carry):
        for copy in right_ffn(t):
            copy.start()
        return carry

    lax.fori_loop(0, FFN_TILES, open_ffn, 0)
    for load in early + load_o:
        load.start()
    for copy in left_att:
        copy.start()

    def product(xd, yd, kind):
        def term(t, k, dest, first, last):
            m = kind(t)
            rows = xd[m, first:last, dest] if k == 0 else xd[m, dest, first:last]
            return mm(rows.reshape((last - first) * 64, 2 * ROWS), yd[t])

        return term

    def finish_ffn(t, k, value):
        out_ffn[t] = value

    def finish_att(t, k, value):
        out_att[t] = value

    def term_pack(t, k, dest, first, last):
        return (pk[c, first:last, dest] + pk[2, first:last, dest]).reshape((last - first) * PACK, 128)

    def finish_pack(t, k, value):
        out_pack[c, z, x] = value

    big = Ring(refs_big, 64, product(xf, yf, lambda t: lax.div(t, 8)), finish_ffn)
    mid = Ring(refs_mid, 64, product(xa, ya, lambda t: t // 3), finish_att)
    low_ring = Ring(refs_low, PACK, term_pack, finish_pack)

    for m in range(2):
        for copy in left_ffn(m):
            copy.wait()

    def first_ffn(t, k):
        for copy in right_ffn(t):
            copy.wait()
        big.start(t, k)

    over_pairs(0, 6, first_ffn)

    for load in early:
        load.wait()
    for turn in gs_turns:
        turn.wait()
    total = gs_own[...].astype(F32) + gs_came[0].astype(F32) + gs_came[1].astype(F32) + gs_came[2].astype(F32)
    gsum[...] = total
    ones = jnp.ones((8, COLS), F32)

    def mean_over(base, value):
        dot_part[...] = mm_nt(ones, value, HIGH)
        turns = to_mates(base, lambda i: dot_part, dot_came)
        for turn in turns:
            turn.start()
        return turns

    dot_turns = mean_over(3, total * columns(gain_two, y) * hidden_in[...])
    write_masks(near, far, lengths)
    for h in range(HEADS):
        qh[h] = q_in[:, h * DIM : (h + 1) * DIM]
    gain_rows_two = jnp.sum(total * hidden_in[...] * r2[...], axis=0, keepdims=True)
    for turn in dot_turns:
        turn.wait()

    def mean_column():
        return ((dot_part[...] + dot_came[0] + dot_came[1] + dot_came[2]) * (1.0 / 2048)).T[:, 0:1]

    scale = r2[...]
    residual = (
        cot_own[...].astype(F32)
        + scale * (gsum[...] * columns(gain_two, y))
        - hidden_in[...] * (scale * scale * scale * mean_column())
    )
    gres[...] = residual
    gb[y] = residual.astype(BF16)
    gb_turns = [
        send(gb.at[y], gb.at[y], y_sem.at[0, 6 + i], y_sem.at[1, 6 + i], y_mates[i]) for i in range(3)
    ]
    for turn in gb_turns:
        turn.start()
    ffn_turns = to_mates(9, lambda i: ffn_hbm.at[turned(y, 1 + i)], ffn_came)
    for turn in ffn_turns:
        turn.start()

    def features(h, carry):
        pq[h] = soft_pair(qh[h], f_q[h])
        return carry

    lax.fori_loop(0, HEADS, features, 0)
    for j in range(KEY_HEADS):
        pkey[j] = soft_pair(kv[j][:, :DIM], f_k[j])
    dk[...] = jnp.zeros(dk.shape, F32)
    dv[...] = jnp.zeros(dv.shape, F32)
    pk[...] = jnp.zeros(pk.shape, F32)
    over_pairs(0, 1, big.merge)

    for i in range(3):
        here = gb.at[turned(y, 3 - i)]
        send(here, here, y_sem.at[0, 6 + i], y_sem.at[1, 6 + i], y_mates[i]).wait_recv()
    for load in load_o:
        load.wait()
    grad_low = jnp.zeros((ROWS, 8), F32)
    grad_mixed = jnp.zeros((ROWS, COLS), F32)
    for k in range(4):
        cut = slice(k * COLS, (k + 1) * COLS)
        grad_low = grad_low + mm_nt(gb[k], b_out[:, cut])
        grad_mixed = grad_mixed + mm_nt(gb[k], wide_w[k])
    grad_mixed = grad_mixed + jnp.dot(
        grad_low, a_out[...].astype(F32), precision=HIGH, preferred_element_type=F32
    )
    rounded = grad_mixed.astype(BF16)
    for load in load_q:
        load.start()
    for h in range(HEADS):
        gh[h] = rounded[:, h * DIM : (h + 1) * DIM]
    top, bottom = halves(grad_low)
    gao[...] = mm_tn(top, mixed[...]) + mm_tn(bottom, mixed[...])
    gbo[...] = mm_tn(low_mix[...], gb[y])

    lane = lax.broadcasted_iota(jnp.int32, (ROWS, DIM), 1)
    for h in range(HEADS):
        j = h // 4
        grad = gh[h].astype(F32)
        den = stat[h, :, 1:2]
        inner = -jnp.sum(grad * att[:, h * DIM : (h + 1) * DIM], axis=1, keepdims=True) / den
        ext = jnp.concatenate([grad / den, jnp.where(lane == 0, inner, 0.0)], axis=1)
        dext[h] = ext
        top, bottom = halves(ext * stat[h, :, 2:3])
        phi = pq[h].astype(BF16)
        piece = (mm_tn(top, phi) + mm_tn(bottom, phi))[:STATE]
        scan.own[0, j] = piece if h % 4 == 0 else scan.own[0, j] + piece
    scan.open()

    for i in range(16):
        block = gb[i // 4, :, (i % 4) * 128 : (i % 4 + 1) * 128].T
        xa[1, i // 4, i % 4, :, 0:ROWS] = jnp.where(c == 0, block[:64], block[64:])
        xgb[i // 4, i % 4] = jnp.where(c == 0, block[64:], block[:64])
    for turn in gb_turns:
        turn.wait_send()
    for load in load_n:
        load.start()
    left_gb = send(xgb, xa.at[1, :, :, :, far_rows], sem_att.at[1, 1], sem_att.at[2, 1], sibling)
    left_gb.start()
    for t in (3, 4):
        ya[t, 0:ROWS] = mixed[:, (t - 3) * ATT_WIDTH : (t - 2) * ATT_WIDTH]
        right_att(t).start()
    scan.along_x()
    left_gb.wait()
    for t in (3, 4):
        right_att(t).wait()
        mid.start(t, t % 2)

    def backward(h, carry):
        j = lax.div(h, 4)
        keys, values = kv[j][:, :DIM], kv[j][:, DIM:]
        q, grad, ext = qh[h], gh[h], dext[h]
        top, den, gate = stat[h, :, 0:1], stat[h, :, 1:2], stat[h, :, 2:3]
        soft = pq[h]
        phi, phi_key = soft.astype(BF16), pkey[j].astype(BF16)
        damping = far[...] * jnp.exp(-top)
        weights = jnp.exp(mm_nt(q, keys) * (DIM**-0.5) + near[...] - top)
        grad_weights = mm_nt(grad, values) / den + ext[:, DIM : DIM + 1]
        grad_scores = (weights * grad_weights).astype(BF16)
        grad_linear = (damping * grad_weights).astype(BF16)
        both = weights.astype(BF16).astype(F32) + mm_nt(phi, phi_key) * damping
        high, rest = halves(both / den)
        grad_q = mm(grad_scores, keys) * (DIM**-0.5)
        dk[j] = dk[j] + mm_tn(grad_scores, q) * (DIM**-0.5)
        dv[j] = dv[j] + mm_tn(high, grad) + mm_tn(rest, grad)
        pkey[KEY_HEADS + j] = pkey[KEY_HEADS + j] + mm_tn(grad_linear, phi)
        carried = jnp.dot(
            (ext * gate)[:, :STATE], state[j], precision=HIGH, preferred_element_type=F32
        )
        grad_soft = mm(grad_linear, phi_key) + carried
        high, rest = halves(soft_back(soft, grad_soft))
        qh[h] = (grad_q + mm_nt(high, f_q[h]) + mm_nt(rest, f_q[h])).astype(BF16)
        gfq[h] = mm_tn(q, high) + mm_tn(q, rest)

        @pl.when(h == 1)
        def _():
            scan.along_z()

        @pl.when(h < 5)
        def _():
            big.merge(2 * h + 2, 0)
            big.merge(2 * h + 3, 1)

        @pl.when(h >= 5)
        def _():
            big.cross(2 * h - 10, 0)
            big.cross(2 * h - 9, 1)

        return carry

    for j in range(KEY_HEADS):
        pkey[KEY_HEADS + j] = jnp.zeros((SPAN, 128), F32)
    lax.fori_loop(0, HEADS, backward, 0)

    inside = middle(ROWS, -WINDOW, lengths)
    suffix = scan.close()
    for j in range(KEY_HEADS):
        soft = pkey[j]
        high, rest = halves(suffix[j])
        rows = value_columns(kv[j, :ROWS])[:, :STATE]
        grad_phi = pkey[KEY_HEADS + j]
        carried = (mm(rows, high) + mm(rows, rest)) * inside
        grad_phi = jnp.concatenate([grad_phi[:ROWS] + carried, grad_phi[ROWS:]], axis=0)
        phi = soft[:ROWS].astype(BF16)
        dv[j, :ROWS] = dv[j, :ROWS] + ((mm_nt(phi, high) + mm_nt(phi, rest)) * inside)[:, :DIM]
        high, rest = halves(soft_back(soft, grad_phi))
        dk[j] = dk[j] + mm_nt(high, f_k[j]) + mm_nt(rest, f_k[j])
        keys = kv[j][:, :DIM]
        gfk[j] = mm_tn(keys, high) + mm_tn(keys, rest)
        ret[j] = jnp.concatenate([dk[j, :WINDOW], dv[j, :WINDOW]], axis=1)
    back = send(ret, ret_came, ret_sem.at[0], ret_sem.at[1], leading)
    back.start()
    gq = jnp.concatenate([qh[h] for h in range(HEADS)], axis=1)
    for i in range(2):
        ya[i, 0:ROWS] = gq[:, i * ATT_WIDTH : (i + 1) * ATT_WIDTH]
        right_att(i).start()
    for turn in ffn_turns:
        turn.wait()
    out_block[...] = (
        hidden_in[...]
        + ffn_own[...].astype(F32)
        + ffn_came[0].astype(F32)
        + ffn_came[1].astype(F32)
        + ffn_came[2].astype(F32)
    ).astype(BF16)
    back.wait()
    for j in range(KEY_HEADS):
        dk[j, ROWS:] = dk[j, ROWS:] + ret_came[j][:, :DIM]
        dv[j, ROWS:] = dv[j, ROWS:] + ret_came[j][:, DIM:]
    gk = jnp.concatenate([dk[j, WINDOW:] for j in range(KEY_HEADS)], axis=1).astype(BF16)
    gv = jnp.concatenate([dv[j, WINDOW:] for j in range(KEY_HEADS)], axis=1).astype(BF16)
    gkv[...] = jnp.concatenate([gk, gv], axis=1)
    ya[2, 0:ROWS] = gkv[...]
    right_att(2).start()

    for load in load_q + load_n:
        load.wait()
    glow[...] = jnp.concatenate([mm_nt(gq, b_q[...]), mm_nt(gk, b_k[...]), mm_nt(gv, b_v[...])], axis=1)
    glow_high, glow_rest = halves(glow[...])

    def partial_first(d):
        rows = pl.ds(pl.multiple_of(d * COLS, COLS), COLS)
        down = a_in[rows, :]
        return (
            mm_nt(gq, wide_w[d])
            + mm_nt(gkv[:, :128], wk[rows, :])
            + mm_nt(gkv[:, 128:], wv[rows, :])
            + mm_nt(glow_high, down)
            + mm_nt(glow_rest, down)
        )

    gf_turns = to_mates(12, lambda i: gf_part.at[i], gs_came)
    for i in (1, 0, 2):
        gf_part[i] = partial_first(turned(y, 1 + i)).astype(BF16)
        gf_turns[i].start()
    gsum[...] = partial_first(y)
    for copy in left_att:
        copy.wait()
    for t in range(3):
        right_att(t).wait()
        mid.start(t, t % 2)

    for k in range(4):
        wide[:, k * COLS : (k + 1) * COLS] = mm_tn(glow_high, gb[k]) + mm_tn(glow_rest, gb[k])
    for i in range(16):
        for half in range(2):
            d = 2 * i + half
            pk[d // 16, d // 4 % 4, d % 4, 0:12] = wide[12 * half : 12 * half + 12, i * 128 : (i + 1) * 128]
    for i in range(4):
        for half in range(2):
            d = 2 * i + half
            pk[lax.div(y, 2), lax.rem(y, 2) * 2 + d // 4, d % 4, 12:16] = gbo[
                4 * half : 4 * half + 4, i * 128 : (i + 1) * 128
            ]

    def low_half(d, value):
        pk[d // 16, d // 4 % 4, d % 4, 16 : 16 + value.shape[0]] = value

    for i in range(4):
        pair = jnp.concatenate([gfq[2 * i], gfq[2 * i + 1]], axis=1)
        for part in range(4):
            low_half(4 * i + part, pair[16 * part : 16 * part + 16])
    pair = jnp.concatenate([gfk[0], gfk[1]], axis=1)
    for part in range(4):
        low_half(16 + part, pair[16 * part : 16 * part + 16])
    grad_b = jnp.concatenate(
        [mm_tn(low[:, :8], gq), mm_tn(low[:, 8:16], gkv[:, :128]), mm_tn(low[:, 16:24], gkv[:, 128:])], axis=1
    )
    for i in range(3):
        low_half(20 + i, jnp.concatenate([grad_b[:, 256 * i : 256 * i + 128], grad_b[:, 256 * i + 128 : 256 * i + 256]]))
    for i in range(2):
        low_half(
            23 + i, jnp.concatenate([gao[:, 256 * i : 256 * i + 128], gao[:, 256 * i + 128 : 256 * i + 256]])
        )
    for turn in gf_turns:
        turn.wait()
    total = gsum[...] + gs_came[0].astype(F32) + gs_came[1].astype(F32) + gs_came[2].astype(F32)
    gsum[...] = total
    inputs = x_own[...].astype(F32)
    gain_rows_one = jnp.sum(total * inputs * r1[...], axis=0, keepdims=True)
    low_half(
        25,
        jnp.concatenate([rows[:, i * 128 : (i + 1) * 128] for rows in (gain_rows_one, gain_rows_two) for i in range(4)]),
    )
    pack_far = send(pk.at[1 - c], pk.at[2], sem_pack.at[0], sem_pack.at[1], sibling)
    pack_far.start()
    dot_turns = mean_over(15, total * columns(gain_one, y) * inputs)
    pack_far.wait()
    low_ring.start(0, 0)
    for turn in dot_turns:
        turn.wait()
    scale = r1[...]
    out_inputs[...] = (
        gres[...]
        + scale * (gsum[...] * columns(gain_one, y))
        - x_own[...].astype(F32) * (scale * scale * scale * mean_column())
    )
    for t in (3, 4, 0, 1, 2):
        mid.merge(t, t % 2)
    low_ring.merge(0, 0)
    over_pairs(3, 6, big.cross)
    for t in (3, 4, 0, 1, 2):
        mid.cross(t, t % 2)
    low_ring.cross(0, 0)
    over_pairs(0, 6, big.merge_cross)
    for t in (3, 4, 0, 1, 2):
        mid.merge_cross(t, t % 2)
    low_ring.merge_cross(0, 0)
    low_ring.end(0, 0)
    crown = pl.ds(0, 16)
    turns = to_mates(18, lambda i: out_pack.at[c, z, x, crown], ysum)
    for turn in turns:
        turn.start()
    for turn in turns:
        turn.wait()
    out_pack[c, z, x, crown] = out_pack[c, z, x, crown] + ysum[0] + ysum[1] + ysum[2]

    def spread(base, piece, mates, back_piece):
        turns = [
            send(piece, piece, sem_zx.at[0, base + i], sem_zx.at[1, base + i], mate) for i, mate in enumerate(mates)
        ]
        for turn in turns:
            turn.start()
        return [
            send(back_piece(i), back_piece(i), sem_zx.at[0, base + i], sem_zx.at[1, base + i], mate)
            for i, mate in enumerate(mates)
        ]

    turns = spread(0, out_pack.at[c, z, x], scan.z_mates, lambda i: out_pack.at[c, turned(z, 3 - i), x])
    over_pairs(0, 6, big.end)
    for turn in turns:
        turn.wait()
    turns = spread(3, out_pack.at[c, :, x], scan.x_mates, lambda i: out_pack.at[c, :, turned(x, 3 - i)])
    for t in (3, 4, 0, 1, 2):
        mid.end(t, t % 2)
    for turn in turns:
        turn.wait()
    turns = spread(6, out_pack.at[c], [sibling], lambda i: out_pack.at[1 - c])
    over_pairs(0, 6, big.drain)
    for t in range(ATT_TILES):
        mid.drain(t, t % 2)
    low_ring.drain(0, 0)
    for turn in turns:
        turn.wait()


def back(args, weights):
    anywhere = pl.BlockSpec(memory_space=pl.ANY)
    vmem = pl.BlockSpec(memory_space=pltpu.VMEM)
    shapes = (
        ((ROWS, COLS), BF16),
        ((ROWS, COLS), F32),
        ((FFN_TILES, 64, FFN_WIDTH), F32),
        ((ATT_TILES, 64, ATT_WIDTH), F32),
        ((2, 4, 4, PACK, 128), F32),
    )
    block = (ROWS, COLS)
    return pl.pallas_call(
        back_kernel,
        out_shape=tuple(jax.ShapeDtypeStruct(*shape) for shape in shapes),
        in_specs=[vmem] * 21 + [pl.BlockSpec(memory_space=pltpu.SMEM)] + [anywhere] * 11,
        out_specs=(vmem,) * len(shapes),
        scratch_shapes=[
            pltpu.VMEM((4, 512, 512), BF16),
            pltpu.VMEM((2048, 128), BF16),
            pltpu.VMEM((2048, 128), BF16),
            pltpu.VMEM(block, BF16),
            pltpu.VMEM(block, BF16),
            pltpu.VMEM(block, BF16),
            pltpu.VMEM(block, BF16),
            pltpu.SemaphoreType.DMA((18,)),
            pltpu.VMEM((3, *block), BF16),
            pltpu.VMEM((3, *block), BF16),
            pltpu.VMEM((3, *block), BF16),
            pltpu.VMEM((8, ROWS), F32),
            pltpu.VMEM((3, 8, ROWS), F32),
            pltpu.VMEM((4, *block), BF16),
            pltpu.VMEM(block, F32),
            pltpu.VMEM(block, F32),
            pltpu.SemaphoreType.DMA((2, 21)),
            pltpu.VMEM((2, 4, 4, 64, 512), BF16),
            pltpu.VMEM((FFN_TILES, 512, FFN_WIDTH), BF16),
            pltpu.SemaphoreType.DMA((3, 2 + FFN_TILES)),
            pltpu.VMEM((2, 4, 4, 64, 512), BF16),
            pltpu.VMEM((ATT_TILES, 512, ATT_WIDTH), BF16),
            pltpu.VMEM((4, 4, 64, ROWS), BF16),
            pltpu.SemaphoreType.DMA((3, 2 + ATT_TILES)),
            pltpu.VMEM((3, 4, 4, PACK, 128), F32),
            pltpu.SemaphoreType.DMA((2,)),
            pltpu.VMEM((ROWS, SPAN), F32),
            pltpu.VMEM((ROWS, SPAN), F32),
            pltpu.VMEM((HEADS, ROWS, DIM), BF16),
            pltpu.VMEM((HEADS, ROWS, DIM), BF16),
            pltpu.VMEM((HEADS, ROWS, 128), F32),
            pltpu.VMEM((2 * KEY_HEADS, SPAN, 128), F32),
            pltpu.VMEM((HEADS, ROWS, 128), F32),
            pltpu.VMEM((KEY_HEADS, SPAN, DIM), F32),
            pltpu.VMEM((KEY_HEADS, SPAN, DIM), F32),
            pltpu.VMEM((HEADS, DIM, DIM), F32),
            pltpu.VMEM((KEY_HEADS, DIM, DIM), F32),
            pltpu.VMEM((KEY_HEADS, WINDOW, 128), F32),
            pltpu.VMEM((KEY_HEADS, WINDOW, 128), F32),
            pltpu.SemaphoreType.DMA((2,)),
            pltpu.VMEM((ROWS, 24), F32),
            pltpu.VMEM((ROWS, 256), BF16),
            pltpu.VMEM((24, 2048), F32),
            pltpu.VMEM((8, COLS), F32),
            pltpu.VMEM((8, COLS), F32),
            pltpu.VMEM((3, 16, 128), F32),
            pltpu.SemaphoreType.DMA((2, 7)),
            *Scan.scratch((KEY_HEADS, STATE, 128)),
            *Ring.scratch(FFN_TILES, 64, FFN_WIDTH),
            *Ring.scratch(ATT_TILES, 64, ATT_WIDTH),
            *Ring.scratch(1, PACK, 128),
        ],
        compiler_params=pltpu.CompilerParams(
            collective_id=2, has_side_effects=True, vmem_limit_bytes=63 * 2**20
        ),
        name="back",
    )(*args, *weights)


def body(
    inputs,
    gain_first,
    w_query,
    a_query,
    b_query,
    key_projection_weight,
    a_key,
    key_adapter_second,
    value_projection_weight,
    a_value,
    value_adapter_second,
    feature_query,
    key_hedgehog_map,
    w_out,
    a_out,
    b_out,
    gain_second,
    w_gate,
    w_up,
    w_down,
    lengths,
    cotangent,
):
    gain_one, gain_two = gain_first[None], gain_second[None]
    a_in = jnp.concatenate([a_query, a_key, a_value], axis=1)
    a_out = a_out.T
    projections = (w_query, key_projection_weight, value_projection_weight, w_out)
    normed, low, queries, kv, state, att, stat, mixed, low_mix, hidden_in, ns, r2, r1 = front(
        inputs, gain_one, gain_two, a_in, b_query, key_adapter_second, value_adapter_second,
        feature_query, key_hedgehog_map, a_out, b_out, lengths, *projections,
    )
    y_ffn, gs, ffn_sum, xt = ffn(ns, cotangent, normed, w_gate, w_up, w_down)
    block_out, grad_inputs, out_ffn, out_att, out_pack = back(
        (
            hidden_in, r1, r2, gain_one, gain_two, mixed, low_mix, att, stat, state, queries, kv, low,
            feature_query, key_hedgehog_map, a_in, a_out, b_out, b_query, key_adapter_second,
            value_adapter_second, lengths,
        ),
        (gs, ffn_sum, normed, inputs, cotangent, xt, y_ffn.reshape(FFN_TILES, ROWS, FFN_WIDTH), *projections),
    )
    a_rows, b_out_sum, f_query, f_key, b_rows, a_out_sum, gain_one, gain_two = unpack_small(out_pack)
    a_rows = a_rows.T
    return (
        block_out,
        grad_inputs,
        gain_one,
        untile(out_att[:2]),
        a_rows[:, :8],
        b_rows[:, :512],
        out_att[2, :, :128],
        a_rows[:, 8:16],
        b_rows[:, 512:640],
        out_att[2, :, 128:],
        a_rows[:, 16:],
        b_rows[:, 640:],
        f_query,
        f_key,
        untile(out_att[3:]).T,
        a_out_sum.T,
        b_out_sum,
        gain_two,
        untile(out_ffn[:4]),
        untile(out_ffn[4:8]),
        untile(out_ffn[8:]).T,
    )


def solution(mesh):
    return jax.shard_map(
        body,
        mesh=mesh,
        in_specs=(
            P("seq", None),
            P(),
            P(None, "head"),
            P(),
            P(None, "head"),
            P(None, "head"),
            P(),
            P(None, "head"),
            P(None, "head"),
            P(),
            P(None, "head"),
            P("head", None, None),
            P("head", None, None),
            P("head", None),
            P("head", None),
            P(),
            P(),
            P(None, "head"),
            P(None, "head"),
            P("head", None),
            P(),
            P("seq", None),
        ),
        out_specs=(
            P("seq", "head"),
            P("seq", "head"),
            P("head"),
            P("seq", "head"),
            P(),
            P(None, "head"),
            P("seq", "head"),
            P(),
            P(None, "head"),
            P("seq", "head"),
            P(),
            P(None, "head"),
            P("head", None, None),
            P("head", None, None),
            P("head", "seq"),
            P("head", None),
            P(),
            P("head"),
            P("seq", "head"),
            P("seq", "head"),
            P("head", "seq"),
        ),
        check_vma=False,
    )
```

```python
import jax
import jax.numpy as jnp
from jax import lax
from jax.experimental import pallas as pl
from jax.experimental.pallas import tpu as pltpu
from jax.sharding import PartitionSpec as P

MESH = pl.DeviceIdType.MESH
F32 = jnp.float32
BF16 = jnp.bfloat16


def spot():
    s = lax.axis_index("seq")
    y = lax.axis_index("head")
    return lax.div(s, 8), lax.rem(lax.div(s, 2), 4), lax.rem(s, 2), y


def at(z, x, c, y):
    return ((z * 4 + x) * 2 + c, y)


def turned(p, steps):
    return lax.rem(p + steps, 4)


def greet(partners):
    barrier = pltpu.get_barrier_semaphore()
    for partner in partners:
        pl.semaphore_signal(barrier, inc=1, device_id=partner, device_id_type=MESH)
    pl.semaphore_wait(barrier, len(partners))


def send(src, dst, ss, rs, device):
    return pltpu.make_async_remote_copy(
        src_ref=src, dst_ref=dst, send_sem=ss, recv_sem=rs, device_id=device, device_id_type=MESH
    )


class Ring:
    def __init__(self, refs, rows, term, finish):
        self.sb, self.ra, self.rf, self.ra3, self.rf3, self.ss, self.rs = refs
        self.rows, self.term, self.finish = rows, term, finish
        z, x, c, y = spot()
        self.axes = (
            (x, at(z, turned(x, 1), c, y), at(z, turned(x, 3), c, y)),
            (z, at(turned(z, 1), x, c, y), at(turned(z, 3), x, c, y)),
        )

    @staticmethod
    def scratch(count, rows, width):
        return [
            pltpu.VMEM((count, 2, 4 * rows, width), BF16),
            pltpu.VMEM((count, 2, 2 * rows, width), BF16),
            pltpu.VMEM((count, 2, 4 * rows, width), BF16),
            pltpu.VMEM((count, 2, rows // 2, width), BF16),
            pltpu.VMEM((count, 2, rows, width), BF16),
            pltpu.SemaphoreType.DMA((count, 12)),
            pltpu.SemaphoreType.DMA((count, 12)),
        ]

    def block(self, b, part):
        g = self.rows // 2
        if part is None:
            return pl.ds(pl.multiple_of(b * self.rows, self.rows), self.rows)
        return pl.ds(pl.multiple_of(b * self.rows + part * g, g), g)

    def copy(self, t, k, i):
        p, ahead, behind = self.axes[k]
        q, ahead3, behind3 = self.axes[1 - k]
        h, g = 2 * self.rows, self.rows // 2
        lo, hi, lo3, hi3 = pl.ds(0, h), pl.ds(h, h), pl.ds(0, g), pl.ds(g, g)
        sb, ra, rf, ra3, rf3, block = self.sb, self.ra, self.rf, self.ra3, self.rf3, self.block
        src, dst, device = (
            lambda: (sb.at[t, 0, lo], ra.at[t, 0], ahead),
            lambda: (sb.at[t, 0, hi], ra.at[t, 1], behind),
            lambda: (sb.at[t, 1, hi], rf.at[t, 0, hi], ahead),
            lambda: (sb.at[t, 1, lo], rf.at[t, 1, lo], behind),
            lambda: (ra.at[t, 0], rf.at[t, 0, lo], ahead),
            lambda: (ra.at[t, 1], rf.at[t, 1, hi], behind),
            lambda: (sb.at[t, 0, block(turned(q, 2), 0)], ra3.at[t, 0], ahead3),
            lambda: (sb.at[t, 0, block(turned(q, 2), 1)], ra3.at[t, 1], behind3),
            lambda: (sb.at[t, 0, block(turned(q, 1), 1)], rf3.at[t, 0, hi3], ahead3),
            lambda: (sb.at[t, 0, block(turned(q, 3), 0)], rf3.at[t, 1, lo3], behind3),
            lambda: (ra3.at[t, 0], rf3.at[t, 0, lo3], ahead3),
            lambda: (ra3.at[t, 1], rf3.at[t, 1, hi3], behind3),
        )[i]()
        return send(src, dst, self.ss.at[t, i], self.rs.at[t, i], device)

    def start(self, t, k):
        p = self.axes[k][0]
        h = 2 * self.rows
        self.sb[t, 0] = self.term(t, k, turned(p, 2), 0, 4).astype(BF16)
        self.copy(t, k, 0).start()
        self.copy(t, k, 1).start()
        self.sb[t, 1, h:] = self.term(t, k, turned(p, 1), 2, 4).astype(BF16)
        self.copy(t, k, 2).start()
        self.sb[t, 1, :h] = self.term(t, k, turned(p, 3), 0, 2).astype(BF16)
        self.copy(t, k, 3).start()

    def merge(self, t, k):
        p = self.axes[k][0]
        for way, dest, first in ((0, turned(p, 1), 0), (1, turned(p, 3), 2)):
            self.copy(t, k, way).wait_recv()
            self.ra[t, way] = (self.term(t, k, dest, first, first + 2) + self.ra[t, way].astype(F32)).astype(BF16)
            self.copy(t, k, 4 + way).start()

    def cross(self, t, k):
        p = self.axes[k][0]
        own = self.term(t, k, p, 0, 4)
        for i in (0, 1):
            self.copy(t, k, i).wait_send()
        for i in (2, 3, 4, 5):
            self.copy(t, k, i).wait_recv()
        self.sb[t, 0] = (own + self.rf[t, 0].astype(F32) + self.rf[t, 1].astype(F32)).astype(BF16)
        for i in (6, 7, 8, 9):
            self.copy(t, k, i).start()

    def merge_cross(self, t, k):
        q = self.axes[1 - k][0]
        for way, dest in ((0, turned(q, 1)), (1, turned(q, 3))):
            self.copy(t, k, 6 + way).wait_recv()
            mine = self.sb[t, 0, self.block(dest, way), :]
            self.ra3[t, way] = (mine.astype(F32) + self.ra3[t, way].astype(F32)).astype(BF16)
            self.copy(t, k, 10 + way).start()

    def end(self, t, k):
        q = self.axes[1 - k][0]
        for i in (8, 9, 10, 11):
            self.copy(t, k, i).wait_recv()
        mine = self.sb[t, 0, self.block(q, None), :].astype(F32)
        self.finish(t, k, mine + self.rf3[t, 0].astype(F32) + self.rf3[t, 1].astype(F32))

    def drain(self, t, k):
        for i in range(2, 12):
            self.copy(t, k, i).wait_send()


def over_pairs(first, last, step):
    def both(u, carry):
        step(2 * u, 0)
        step(2 * u + 1, 1)
        return carry

    lax.fori_loop(first, last, both, 0)


FFN_TILES, FFN_WIDTH = 12, 512
ATT_TILES, ATT_WIDTH = 5, 256
PACK = 32


EPS = 1e-05
NEG = -1e30
HIGH = lax.Precision.HIGHEST
ROWS = 256
WINDOW = 64
SPAN = ROWS + WINDOW
COLS = 512
HEADS, KEY_HEADS, DIM = 8, 2, 64
STATE = 72


def mm(a, b):
    return jnp.dot(a, b, preferred_element_type=F32)


def mm_nt(a, b, precision=None):
    return lax.dot_general(a, b, (((1,), (1,)), ((), ())), precision=precision, preferred_element_type=F32)


def mm_tn(a, b, precision=None):
    return lax.dot_general(a, b, (((0,), (0,)), ((), ())), precision=precision, preferred_element_type=F32)


def halves(value):
    top = value.astype(BF16)
    return top, (value - top.astype(F32)).astype(BF16)


def down_rows(a_q, a_k, a_v):
    return jnp.concatenate([a[...].astype(F32) for a in (a_q, a_k, a_v)], axis=0).astype(BF16)


def soft_pair(rows, table):
    both = mm(rows, jnp.concatenate([table, -table], axis=1))
    left = lax.broadcasted_iota(jnp.int32, both.shape, 1) < DIM
    upper = jnp.max(jnp.where(left, both, NEG), axis=1, keepdims=True)
    lower = jnp.max(jnp.where(left, NEG, both), axis=1, keepdims=True)
    grown = jnp.exp(both - jnp.where(left, upper, lower))
    sum_left = jnp.sum(jnp.where(left, grown, 0.0), axis=1, keepdims=True)
    sum_right = jnp.sum(jnp.where(left, 0.0, grown), axis=1, keepdims=True)
    return grown / jnp.where(left, sum_left, sum_right)


def doc_at(positions, lengths):
    first = lengths[0]
    second = first + lengths[1]
    return (
        (positions >= 0).astype(jnp.int32)
        + (positions >= first).astype(jnp.int32)
        + (positions >= second).astype(jnp.int32)
    )


def write_masks(near, far, lengths):
    base = lax.axis_index("seq") * ROWS
    row = lax.broadcasted_iota(jnp.int32, (ROWS, SPAN), 0) + base
    column = lax.broadcasted_iota(jnp.int32, (ROWS, SPAN), 1) + base - WINDOW
    same = doc_at(row, lengths) == doc_at(column, lengths)
    offset = row - column
    near[...] = jnp.where(same & (offset >= 0) & (offset < WINDOW), 0.0, NEG)
    far[...] = jnp.where(same & (offset >= WINDOW), 1.0, 0.0)


def middle(count, first, lengths):
    base = lax.axis_index("seq") * ROWS + first
    position = lax.broadcasted_iota(jnp.int32, (count, 1), 0) + base
    return (doc_at(position, lengths) == 2).astype(F32)


def value_columns(kv):
    lane = lax.broadcasted_iota(jnp.int32, kv.shape, 1)
    v = jnp.concatenate([kv[:, DIM:], kv[:, :DIM]], axis=1)
    return jnp.where(lane < DIM, v, jnp.where(lane == DIM, 1.0, 0.0).astype(kv.dtype))


class Scan:
    def __init__(self, refs, reverse):
        self.own, self.pair, self.line, self.plane, self.sem = refs
        self.reverse = reverse
        z, x, c, y = spot()
        self.z, self.x, self.c = z, x, c
        self.sibling = at(z, x, 1 - c, y)
        self.x_mates = [at(z, turned(x, i), c, y) for i in (1, 2, 3)]
        self.z_mates = [at(turned(z, i), x, c, y) for i in (1, 2, 3)]

    @staticmethod
    def scratch(shape):
        return [
            pltpu.VMEM((3, *shape), F32),
            pltpu.VMEM(shape, F32),
            pltpu.VMEM((3, *shape), F32),
            pltpu.VMEM((3, *shape), F32),
            pltpu.SemaphoreType.DMA((2, 7)),
        ]

    def pair_copy(self):
        return send(self.own.at[0], self.pair, self.sem.at[0, 0], self.sem.at[1, 0], self.sibling)

    def line_copy(self, i):
        return send(self.own.at[1], self.line.at[i], self.sem.at[0, 1 + i], self.sem.at[1, 1 + i], self.x_mates[i])

    def plane_copy(self, i):
        return send(self.own.at[2], self.plane.at[i], self.sem.at[0, 4 + i], self.sem.at[1, 4 + i], self.z_mates[i])

    def counts(self, me, other):
        return ((other > me) if self.reverse else (other < me)).astype(F32)

    def open(self):
        self.pair_copy().start()

    def along_x(self):
        self.pair_copy().wait()
        self.own[1] = self.own[0] + self.pair[...]
        for i in range(3):
            self.line_copy(i).start()

    def along_z(self):
        for i in range(3):
            self.line_copy(i).wait()
        self.own[2] = self.own[1] + self.line[0] + self.line[1] + self.line[2]
        for i in range(3):
            self.plane_copy(i).start()

    def close(self, total):
        for i in range(3):
            self.plane_copy(i).wait()
        for i in range(3):
            total = total + self.line[i] * self.counts(self.x, turned(self.x, 3 - i))
        for i in range(3):
            total = total + self.plane[i] * self.counts(self.z, turned(self.z, 3 - i))
        return total


def front_kernel(
    x_ref, gain_one, gain_two, a_q, a_k, a_v, b_q, b_k, b_v, f_q, f_k, a_out, b_out, lengths, w_q, w_k, w_v, w_o,
    normed_out, low_out, q_out, kv_out, state_out, att_out, stat_out, mixed_out, lowmix_out, hidden_out, g_out, r2_out, r1_out,
    wq, wk, wv, wo, w_sem, qh, phq, phk, num, near, far, brief, tail_sem,
    part, came, y_sem, low_part, square, square_came,
    *scan_refs,
):
    z, x, c, y = spot()
    s = lax.axis_index("seq")
    following, leading = (lax.rem(s + 1, 32), y), (lax.rem(s + 31, 32), y)
    y_mates = [at(z, x, c, turned(y, i)) for i in (1, 2, 3)]
    scan = Scan(scan_refs, False)
    greet([following, leading, scan.sibling] + scan.x_mates + scan.z_mates + y_mates)
    loads = [
        pltpu.make_async_copy(src, dst, w_sem.at[i])
        for i, (src, dst) in enumerate(((w_q, wq), (w_k, wk), (w_v, wv), (w_o, wo)))
    ]
    for load in loads:
        load.start()
    for i in range(4):
        rows = pl.ds(64 * i, 64)
        value = x_ref[rows, :].astype(F32)
        scale = lax.rsqrt(jnp.mean(value * value, axis=1, keepdims=True) + EPS)
        r1_out[rows, :] = scale
        normed_out[rows, :] = (value * scale * gain_one[...]).astype(BF16)
    write_masks(near, far, lengths)
    low_out[...] = mm_nt(normed_out[...], down_rows(a_q, a_k, a_v)).astype(BF16)
    low = low_out[...]
    loads[1].wait()
    loads[2].wait()
    k = (mm(normed_out[...], wk[...]) + mm(low[:, 8:16], b_k[...])).astype(BF16)
    v = (mm(normed_out[...], wv[...]) + mm(low[:, 16:24], b_v[...])).astype(BF16)
    for j in range(KEY_HEADS):
        cut = slice(j * DIM, (j + 1) * DIM)
        kv_out[j, WINDOW:] = jnp.concatenate([k[:, cut], v[:, cut]], axis=1)
    tail = send(
        kv_out.at[:, pl.ds(ROWS, WINDOW)], kv_out.at[:, pl.ds(0, WINDOW)], tail_sem.at[0], tail_sem.at[1], following
    )
    tail.start()
    loads[0].wait()
    for i in range(2):
        cut = slice(i * 256, (i + 1) * 256)
        q_out[:, cut] = (mm(normed_out[...], wq[:, cut]) + mm(low[:, :8], b_q[:, cut])).astype(BF16)
    for h in range(HEADS):
        qh[h] = q_out[:, h * DIM : (h + 1) * DIM]
    inside = middle(ROWS, 0, lengths)
    for j in range(KEY_HEADS):
        phk[j, WINDOW:] = soft_pair(kv_out[j, WINDOW:][:, :DIM], f_k[j]).astype(BF16)
        counted = (phk[j, WINDOW:].astype(F32) * inside).astype(BF16)
        rows = value_columns(kv_out[j, WINDOW:])
        settled = mm_tn(rows[: ROWS - WINDOW], counted[: ROWS - WINDOW])[:STATE]
        brief[0, j] = settled
        scan.own[0, j] = settled + mm_tn(rows[ROWS - WINDOW :], counted[ROWS - WINDOW :])[:STATE]
    brief_turn = send(brief.at[0], brief.at[1], tail_sem.at[2], tail_sem.at[3], scan.sibling)
    brief_turn.start()
    scan.open()

    def features(h, carry):
        phq[h] = soft_pair(qh[h], f_q[h]).astype(BF16)
        return carry

    lax.fori_loop(0, 4, features, 0)
    scan.along_x()
    lax.fori_loop(4, HEADS, features, 0)
    tail.wait()
    inside = middle(WINDOW, -WINDOW, lengths)
    for j in range(KEY_HEADS):
        phk[j, :WINDOW] = soft_pair(kv_out[j, :WINDOW][:, :DIM], f_k[j]).astype(BF16)
        counted = (phk[j, :WINDOW].astype(F32) * inside).astype(BF16)
        brief[2, j] = mm_tn(value_columns(kv_out[j, :WINDOW]), counted)[:STATE]
    brief_turn.wait()

    def inner(h, carry):
        j = lax.div(h, 4)
        kv = kv_out[j]
        scores = mm_nt(qh[h], kv[:, :DIM]) * (DIM**-0.5) + near[...]
        top = jnp.max(scores, axis=1, keepdims=True)
        weights = jnp.exp(scores - top)
        distant = mm_nt(phq[h], phk[j]) * far[...] * jnp.exp(-top)
        total = weights + distant
        high = total.astype(BF16)
        rest = ((total - high.astype(F32)) * far[...]).astype(BF16)
        v = kv[:, DIM:]
        num[h] = mm(high, v) + mm(rest, v)
        stat_out[h, :, 0:1] = top
        stat_out[h, :, 1:2] = jnp.sum(total, axis=1, keepdims=True)
        return carry

    lax.fori_loop(0, 4, inner, 0)
    scan.along_z()
    lax.fori_loop(4, HEADS, inner, 0)
    second = c.astype(F32)
    state_out[...] = scan.close(brief[1] * second - brief[2] * (1.0 - second))
    mine = middle(ROWS, 0, lengths)
    for h in range(HEADS):
        top, rest = halves(state_out[h // 4])
        carried = mm_nt(phq[h], top) + mm_nt(phq[h], rest)
        gate = jnp.exp(-stat_out[h, :, 0:1]) * mine
        total = stat_out[h, :, 1:2] + gate * carried[:, DIM : DIM + 1]
        stat_out[h, :, 1:2] = total
        stat_out[h, :, 2:3] = gate
        cut = slice(h * DIM, (h + 1) * DIM)
        attended = (num[h] + gate * carried[:, :DIM]) / total
        att_out[:, cut] = attended
        mixed_out[:, cut] = attended.astype(BF16)
    mixed = mixed_out[...]
    low_part[y] = mm_nt(a_out[...], mixed)
    low_turns = [send(low_part.at[y], low_part.at[y], y_sem.at[0, i], y_sem.at[1, i], y_mates[i]) for i in range(3)]
    for turn in low_turns:
        turn.start()
    loads[3].wait()

    def columns(ref, d):
        return ref[:, pl.ds(pl.multiple_of(d * COLS, COLS), COLS)]

    turns = [send(part.at[i], came.at[i], y_sem.at[0, 3 + i], y_sem.at[1, 3 + i], y_mates[i]) for i in range(3)]
    for i in (1, 0, 2):
        part[i] = mm(mixed, columns(wo, turned(y, 1 + i))).astype(BF16)
        turns[i].start()
    value = mm(mixed, columns(wo, y)) + columns(x_ref, y).astype(F32)
    for i in range(3):
        here = low_part.at[turned(y, 3 - i)]
        send(here, here, y_sem.at[0, i], y_sem.at[1, i], y_mates[i]).wait()
    low_sum = low_part[0] + low_part[1] + low_part[2] + low_part[3]
    lowmix_out[...] = low_sum.T.astype(BF16)
    value = value + mm(lowmix_out[...], columns(b_out, y))
    for turn in turns:
        turn.wait()
    value = value + came[0].astype(F32) + came[1].astype(F32) + came[2].astype(F32)
    hidden_out[...] = value
    g_out[y] = (value * columns(gain_two, y)).astype(BF16)
    turns = [send(g_out.at[y], g_out.at[y], y_sem.at[0, 9 + i], y_sem.at[1, 9 + i], y_mates[i]) for i in range(3)]
    square[...] = mm_nt(jnp.ones((8, COLS), F32), value * value, HIGH)
    square_turns = [
        send(square, square_came.at[i], y_sem.at[0, 6 + i], y_sem.at[1, 6 + i], y_mates[i]) for i in range(3)
    ]
    for turn in square_turns + turns:
        turn.start()
    for turn in square_turns:
        turn.wait()
    mean = (square[...] + square_came[0] + square_came[1] + square_came[2]) * (1.0 / 2048)
    r2_out[...] = lax.rsqrt(mean + EPS).T[:, 0:1]
    for i in range(3):
        here = g_out.at[turned(y, 3 - i)]
        send(here, here, y_sem.at[0, 9 + i], y_sem.at[1, 9 + i], y_mates[i]).wait_recv()
    for turn in turns:
        turn.wait_send()


def front(*args):
    anywhere = pl.BlockSpec(memory_space=pl.ANY)
    vmem = pl.BlockSpec(memory_space=pltpu.VMEM)
    shapes = (
        ((ROWS, 2048), BF16),
        ((ROWS, 24), BF16),
        ((ROWS, 512), BF16),
        ((KEY_HEADS, SPAN, 128), BF16),
        ((KEY_HEADS, STATE, 128), F32),
        ((ROWS, 512), F32),
        ((HEADS, ROWS, 8), F32),
        ((ROWS, 512), BF16),
        ((ROWS, 8), BF16),
        ((ROWS, COLS), F32),
        ((4, ROWS, COLS), BF16),
        ((ROWS, 1), F32),
        ((ROWS, 1), F32),
    )
    return pl.pallas_call(
        front_kernel,
        out_shape=tuple(jax.ShapeDtypeStruct(*shape) for shape in shapes),
        in_specs=[vmem] * 13 + [pl.BlockSpec(memory_space=pltpu.SMEM)] + [anywhere] * 4,
        out_specs=(vmem,) * len(shapes),
        scratch_shapes=[
            pltpu.VMEM((2048, 512), BF16),
            pltpu.VMEM((2048, 128), BF16),
            pltpu.VMEM((2048, 128), BF16),
            pltpu.VMEM((512, 2048), BF16),
            pltpu.SemaphoreType.DMA((4,)),
            pltpu.VMEM((HEADS, ROWS, DIM), BF16),
            pltpu.VMEM((HEADS, ROWS, 128), BF16),
            pltpu.VMEM((KEY_HEADS, SPAN, 128), BF16),
            pltpu.VMEM((HEADS, ROWS, DIM), F32),
            pltpu.VMEM((ROWS, SPAN), F32),
            pltpu.VMEM((ROWS, SPAN), F32),
            pltpu.VMEM((3, KEY_HEADS, STATE, 128), F32),
            pltpu.SemaphoreType.DMA((4,)),
            pltpu.VMEM((3, ROWS, COLS), BF16),
            pltpu.VMEM((3, ROWS, COLS), BF16),
            pltpu.SemaphoreType.DMA((2, 12)),
            pltpu.VMEM((4, 8, ROWS), F32),
            pltpu.VMEM((8, ROWS), F32),
            pltpu.VMEM((3, 8, ROWS), F32),
            *Scan.scratch((KEY_HEADS, STATE, 128)),
        ],
        compiler_params=pltpu.CompilerParams(
            collective_id=1, has_side_effects=True, vmem_limit_bytes=60 * 2**20
        ),
        name="front",
    )(*args)


def ffn_kernel(g_in, r2, cot, normed, wg, wu, wd, y_out, gs_out, ffn_out, xt_out, dot_out, gs_sum, ffn_sum):
    j = pl.program_id(0)
    gate = jnp.zeros((ROWS, COLS), F32)
    up = jnp.zeros((ROWS, COLS), F32)
    for k in range(4):
        cut = slice(k * COLS, (k + 1) * COLS)
        gate = gate + mm(g_in[k], wg[cut])
        up = up + mm(g_in[k], wu[cut])
    scale = r2[...]
    gate = gate * scale
    up = up * scale
    grad = mm_nt(cot[...], wd[...])
    sigmoid = jax.nn.sigmoid(gate)
    active = gate * sigmoid
    hidden = (active * up).astype(BF16)
    grad = grad * scale
    grad_gate = (grad * up * sigmoid * (1.0 + gate * (1.0 - sigmoid))).astype(BF16)
    grad_up = (grad * active).astype(BF16)
    y_out[0, 0] = grad_gate
    y_out[1, 0] = grad_up
    y_out[2, 0] = hidden
    for k in range(4):
        cut = slice(k * COLS, (k + 1) * COLS)
        back = mm_nt(grad_gate, wg[cut]) + mm_nt(grad_up, wu[cut])
        forth = mm(hidden, wd[:, cut])

        @pl.when(j == 0)
        def _():
            gs_sum[k] = back
            ffn_sum[k] = forth

        @pl.when((j > 0) & (j < 3))
        def _():
            gs_sum[k] = gs_sum[k] + back
            ffn_sum[k] = ffn_sum[k] + forth

        @pl.when(j == 3)
        def _():
            total = (gs_sum[k] + back) / scale
            gs_out[k] = total.astype(BF16)
            gs_sum[k] = total * g_in[k].astype(F32)
            ffn_out[k] = (ffn_sum[k] + forth).astype(BF16)

    @pl.when(j == 3)
    def _():
        product = gs_sum[0] + gs_sum[1] + gs_sum[2] + gs_sum[3]
        dot_out[...] = mm_nt(jnp.ones((8, COLS), F32), product, HIGH)

    def turn(m, block_of):
        for i in range(16):
            block = block_of(i).T
            xt_out[m, 0, i // 4, i % 4] = block[:64]
            xt_out[m, 1, i // 4, i % 4] = block[64:]

    @pl.when(j == 0)
    def _():
        turn(0, lambda i: g_in[i // 4, :, (i % 4) * 128 : (i % 4 + 1) * 128])

    @pl.when(j == 1)
    def _():
        turn(1, lambda i: cot[:, i * 128 : (i + 1) * 128])

    @pl.when(j == 2)
    def _():
        turn(2, lambda i: normed[:, i * 128 : (i + 1) * 128])


def ffn(g_in, r2, cot, normed, w_gate, w_up, w_down):
    def whole(*shape):
        return pl.BlockSpec(shape, lambda j: (0,) * len(shape))

    return pl.pallas_call(
        ffn_kernel,
        grid=(4,),
        out_shape=(
            jax.ShapeDtypeStruct((3, 4, ROWS, COLS), BF16),
            jax.ShapeDtypeStruct((4, ROWS, COLS), BF16),
            jax.ShapeDtypeStruct((4, ROWS, COLS), BF16),
            jax.ShapeDtypeStruct((3, 2, 4, 4, 64, ROWS), BF16),
            jax.ShapeDtypeStruct((8, ROWS), F32),
        ),
        in_specs=[
            whole(4, ROWS, COLS),
            whole(ROWS, 1),
            whole(ROWS, 2048),
            whole(ROWS, 2048),
            pl.BlockSpec((2048, COLS), lambda j: (0, j)),
            pl.BlockSpec((2048, COLS), lambda j: (0, j)),
            pl.BlockSpec((COLS, 2048), lambda j: (j, 0)),
        ],
        out_specs=(
            pl.BlockSpec((3, 1, ROWS, COLS), lambda j: (0, j, 0, 0)),
            whole(4, ROWS, COLS),
            whole(4, ROWS, COLS),
            whole(3, 2, 4, 4, 64, ROWS),
            whole(8, ROWS),
        ),
        scratch_shapes=[pltpu.VMEM((4, ROWS, COLS), F32), pltpu.VMEM((4, ROWS, COLS), F32)],
        compiler_params=pltpu.CompilerParams(vmem_limit_bytes=60 * 2**20),
        name="ffn",
    )(g_in, r2, cot, normed, w_gate, w_up, w_down)


def soft_back(soft, grad):
    left = lax.broadcasted_iota(jnp.int32, soft.shape, 1) < DIM
    part = soft * grad
    sum_left = jnp.sum(jnp.where(left, part, 0.0), axis=1, keepdims=True)
    sum_right = jnp.sum(jnp.where(left, 0.0, part), axis=1, keepdims=True)
    both = part - soft * jnp.where(left, sum_left, sum_right)
    return both[:, :DIM] - both[:, DIM:]


def back_kernel(
    dot_two, hidden_in, r1, r2, gain_one, gain_two, mixed, low_mix, att, stat, state, q_in, kv, low,
    f_q, f_k, a_q, a_k, a_v, a_out, b_out, b_q, b_k, b_v, lengths,
    gs_hbm, ffn_hbm, normed_hbm, x_hbm, cot_hbm, xt_hbm, y_hbm, w_q, w_k, w_v, w_o,
    out_block, out_inputs, out_ffn, out_att, out_pack,
    wide_w, wk, wv, x_all, cot_own, gs_own, ffn_own, w_sem,
    gs_came, ffn_came, gf_part, dot_part, dot_came, gb, gres, gsum, y_sem,
    xf, yf, sem_ffn, xa, ya, xgb, sem_att, pk, sem_pack,
    near, far, qh, gh, pq, pkey, dext, dk, dv, gfq, gfk, ret, ret_came, next_state, ret_sem, glow, gkv, wide, gao, gbo, down_ref,
    first, gain_row, gain_rows_ref, px, px_came, pz, crown, sem_zx,
    *rest,
):
    scan = Scan(rest[0:5], True)
    refs_big, refs_mid = rest[5:12], rest[12:19]
    z, x, c, y = spot()
    s = lax.axis_index("seq")
    following, leading = (lax.rem(s + 1, 32), y), (lax.rem(s + 31, 32), y)
    y_mates = [at(z, x, c, turned(y, i)) for i in (1, 2, 3)]
    sibling = scan.sibling
    greet([following, leading, sibling] + scan.x_mates + scan.z_mates + y_mates)

    def columns(ref, d):
        return ref[:, pl.ds(pl.multiple_of(d * COLS, COLS), COLS)]

    def to_mates(base, pieces, slots):
        return [
            send(pieces(i), slots.at[i], y_sem.at[0, base + i], y_sem.at[1, base + i], y_mates[i]) for i in range(3)
        ]

    own_columns = pl.ds(pl.multiple_of(y * COLS, COLS), COLS)
    gs_turns = to_mates(3, lambda i: dot_two, dot_came) + to_mates(0, lambda i: gs_hbm.at[turned(y, 1 + i)], gs_came)
    for turn in gs_turns:
        turn.start()
    early = [
        pltpu.make_async_copy(src, dst, w_sem.at[i])
        for i, (src, dst) in enumerate(
            (
                (gs_hbm.at[y], gs_own),
                (cot_hbm.at[:, own_columns], cot_own),
                (x_hbm, x_all),
                (ffn_hbm.at[y], ffn_own),
                (w_k, wk),
                (w_v, wv),
            )
        )
    ]

    def quarter(k):
        return pl.ds(k * COLS, COLS)

    load_o = [pltpu.make_async_copy(w_o.at[:, quarter(k)], wide_w.at[k], w_sem.at[6 + k]) for k in range(4)]
    load_q = [pltpu.make_async_copy(w_q.at[quarter(k)], wide_w.at[k], w_sem.at[10 + k]) for k in range(4)]
    load_n = [pltpu.make_async_copy(normed_hbm.at[:, quarter(k)], gb.at[k], w_sem.at[14 + k]) for k in range(4)]
    own_rows, far_rows = pl.ds(0, ROWS), pl.ds(ROWS, ROWS)

    def left_ffn(m):
        return [
            pltpu.make_async_copy(xt_hbm.at[m, c], xf.at[m, :, :, :, own_rows], sem_ffn.at[0, m]),
            send(xt_hbm.at[m, 1 - c], xf.at[m, :, :, :, far_rows], sem_ffn.at[1, m], sem_ffn.at[2, m], sibling),
        ]

    def right_ffn(t):
        return [
            pltpu.make_async_copy(y_hbm.at[t], yf.at[t, own_rows], sem_ffn.at[0, 2 + t]),
            send(y_hbm.at[t], yf.at[t, far_rows], sem_ffn.at[1, 2 + t], sem_ffn.at[2, 2 + t], sibling),
        ]

    left_att = [
        pltpu.make_async_copy(xt_hbm.at[2, c], xa.at[0, :, :, :, own_rows], sem_att.at[0, 0]),
        send(xt_hbm.at[2, 1 - c], xa.at[0, :, :, :, far_rows], sem_att.at[1, 0], sem_att.at[2, 0], sibling),
    ]

    def right_att(t):
        return send(ya.at[t, own_rows], ya.at[t, far_rows], sem_att.at[1, 2 + t], sem_att.at[2, 2 + t], sibling)

    for m in range(2):
        for copy in left_ffn(m):
            copy.start()

    def open_ffn(t, carry):
        for copy in right_ffn(t):
            copy.start()
        return carry

    lax.fori_loop(0, FFN_TILES, open_ffn, 0)
    for load in early + load_o:
        load.start()
    for copy in left_att:
        copy.start()

    def product(xd, yd, kind):
        def term(t, k, dest, first, last):
            m = kind(t)
            rows = xd[m, first:last, dest] if k == 0 else xd[m, dest, first:last]
            return mm(rows.reshape((last - first) * 64, 2 * ROWS), yd[t])

        return term

    def finish_ffn(t, k, value):
        out_ffn[t] = value

    def finish_att(t, k, value):
        out_att[t] = value

    big = Ring(refs_big, 64, product(xf, yf, lambda t: lax.div(t, 8)), finish_ffn)
    mid = Ring(refs_mid, 64, product(xa, ya, lambda t: t // 3), finish_att)

    for m in range(2):
        for copy in left_ffn(m):
            copy.wait()

    def first_ffn(t, k):
        for copy in right_ffn(t):
            copy.wait()
        big.start(t, k)

    over_pairs(0, 6, first_ffn)

    for load in early:
        load.wait()
    for turn in gs_turns:
        turn.wait()
    total = gs_own[...].astype(F32) + gs_came[0].astype(F32) + gs_came[1].astype(F32) + gs_came[2].astype(F32)
    gsum[...] = total
    gain_rows = jnp.sum(total * hidden_in[...] * r2[...], axis=0, keepdims=True)
    gain_rows_ref[...] = jnp.concatenate([gain_rows[:, i * 128 : (i + 1) * 128] for i in range(4)])

    def mean_column(own):
        return ((own + dot_came[0] + dot_came[1] + dot_came[2]) * (1.0 / 2048)).T[:, 0:1]

    scale = r2[...]
    residual = (
        cot_own[...].astype(F32)
        + scale * (gsum[...] * columns(gain_two, y))
        - hidden_in[...] * (scale * scale * scale * mean_column(dot_two[...]))
    )
    gres[...] = residual
    gb[y] = residual.astype(BF16)
    gb_turns = [
        send(gb.at[y], gb.at[y], y_sem.at[0, 6 + i], y_sem.at[1, 6 + i], y_mates[i]) for i in range(3)
    ]
    for turn in gb_turns:
        turn.start()
    ffn_turns = to_mates(9, lambda i: ffn_hbm.at[turned(y, 1 + i)], ffn_came)
    for turn in ffn_turns:
        turn.start()

    write_masks(near, far, lengths)
    for h in range(HEADS):
        qh[h] = q_in[:, h * DIM : (h + 1) * DIM]

    def features(h, carry):
        pq[h] = soft_pair(qh[h], f_q[h])
        return carry

    lax.fori_loop(0, HEADS, features, 0)
    for j in range(KEY_HEADS):
        pkey[j] = soft_pair(kv[j][:, :DIM], f_k[j])
        pkey[KEY_HEADS + j] = jnp.zeros((SPAN, 128), F32)
    dk[...] = jnp.zeros(dk.shape, F32)
    dv[...] = jnp.zeros(dv.shape, F32)
    pk[...] = jnp.zeros(pk.shape, F32)
    over_pairs(0, 3, big.merge)

    for i in range(3):
        here = gb.at[turned(y, 3 - i)]
        send(here, here, y_sem.at[0, 6 + i], y_sem.at[1, 6 + i], y_mates[i]).wait_recv()
    for load in load_o:
        load.wait()
    grad_low = jnp.zeros((ROWS, 8), F32)
    grad_mixed = jnp.zeros((ROWS, COLS), F32)
    for k in range(4):
        cut = slice(k * COLS, (k + 1) * COLS)
        grad_low = grad_low + mm_nt(gb[k], b_out[:, cut])
        grad_mixed = grad_mixed + mm_nt(gb[k], wide_w[k])
    grad_mixed = grad_mixed + jnp.dot(
        grad_low, a_out[...].astype(F32), precision=HIGH, preferred_element_type=F32
    )
    rounded = grad_mixed.astype(BF16)
    for load in load_q:
        load.start()
    for h in range(HEADS):
        gh[h] = rounded[:, h * DIM : (h + 1) * DIM]
    top, bottom = halves(grad_low)
    gao[...] = mm_tn(top, mixed[...]) + mm_tn(bottom, mixed[...])
    for k in range(4):
        gbo[:, k * COLS : (k + 1) * COLS] = mm_tn(low_mix[...], gb[k])

    lane = lax.broadcasted_iota(jnp.int32, (ROWS, DIM), 1)
    for h in range(HEADS):
        j = h // 4
        grad = gh[h].astype(F32)
        den = stat[h, :, 1:2]
        inner = -jnp.sum(grad * att[:, h * DIM : (h + 1) * DIM], axis=1, keepdims=True) / den
        ext = jnp.concatenate([grad / den, jnp.where(lane == 0, inner, 0.0)], axis=1)
        dext[h] = ext
        top, bottom = halves(ext * stat[h, :, 2:3])
        phi = pq[h].astype(BF16)
        piece = (mm_tn(top, phi) + mm_tn(bottom, phi))[:STATE]
        scan.own[0, j] = piece if h % 4 == 0 else scan.own[0, j] + piece
    scan.open()

    for i in range(16):
        block = gb[i // 4, :, (i % 4) * 128 : (i % 4 + 1) * 128].T
        xa[1, i // 4, i % 4, :, 0:ROWS] = jnp.where(c == 0, block[:64], block[64:])
        xgb[i // 4, i % 4] = jnp.where(c == 0, block[64:], block[:64])
    for turn in gb_turns:
        turn.wait_send()
    for load in load_n:
        load.start()
    left_gb = send(xgb, xa.at[1, :, :, :, far_rows], sem_att.at[1, 1], sem_att.at[2, 1], sibling)
    left_gb.start()
    for t in (3, 4):
        ya[t, 0:ROWS] = mixed[:, (t - 3) * ATT_WIDTH : (t - 2) * ATT_WIDTH]
        right_att(t).start()
    scan.along_x()
    left_gb.wait()
    for t in (3, 4):
        right_att(t).wait()
        mid.start(t, t % 2)

    def backward(h, carry):
        j = lax.div(h, 4)
        keys, values = kv[j][:, :DIM], kv[j][:, DIM:]
        q, grad, ext = qh[h], gh[h], dext[h]
        top, den, gate = stat[h, :, 0:1], stat[h, :, 1:2], stat[h, :, 2:3]
        soft = pq[h]
        phi, phi_key = soft.astype(BF16), pkey[j].astype(BF16)
        damping = far[...] * jnp.exp(-top)
        weights = jnp.exp(mm_nt(q, keys) * (DIM**-0.5) + near[...] - top)
        grad_weights = mm_nt(grad, values) / den + ext[:, DIM : DIM + 1]
        grad_scores = (weights * grad_weights).astype(BF16)
        grad_linear = (damping * grad_weights).astype(BF16)
        both = weights.astype(BF16).astype(F32) + mm_nt(phi, phi_key) * damping
        high, rest = halves(both / den)
        grad_q = mm(grad_scores, keys) * (DIM**-0.5)
        dk[j] = dk[j] + mm_tn(grad_scores, q) * (DIM**-0.5)
        dv[j] = dv[j] + mm_tn(high, grad) + mm_tn(rest, grad)
        pkey[KEY_HEADS + j] = pkey[KEY_HEADS + j] + mm_tn(grad_linear, phi)
        carried = jnp.dot(
            (ext * gate)[:, :STATE], state[j], precision=HIGH, preferred_element_type=F32
        )
        grad_soft = mm(grad_linear, phi_key) + carried
        high, rest = halves(soft_back(soft, grad_soft))
        qh[h] = (grad_q + mm_nt(high, f_q[h]) + mm_nt(rest, f_q[h])).astype(BF16)
        gfq[h] = mm_tn(q, high) + mm_tn(q, rest)

        @pl.when(h == 1)
        def _():
            scan.along_z()

        @pl.when((h >= 1) & (h < 4))
        def _():
            big.merge(2 * h + 4, 0)
            big.merge(2 * h + 5, 1)

        @pl.when(h >= 6)
        def _():
            big.cross(2 * h - 12, 0)
            big.cross(2 * h - 11, 1)

        return carry

    lax.fori_loop(0, HEADS, backward, 0)

    for j in range(KEY_HEADS):
        ret[j] = jnp.concatenate([dk[j, :WINDOW], dv[j, :WINDOW], pkey[KEY_HEADS + j, :WINDOW]], axis=1)
    home = [
        send(ret, ret_came, ret_sem.at[0], ret_sem.at[1], leading),
        send(scan.own.at[0], next_state, ret_sem.at[2], ret_sem.at[3], leading),
    ]
    for copy in home:
        copy.start()
    gq = jnp.concatenate([qh[h] for h in range(HEADS)], axis=1)
    for i in range(2):
        ya[i, 0:ROWS] = gq[:, i * ATT_WIDTH : (i + 1) * ATT_WIDTH]
        right_att(i).start()
    down_ref[...] = down_rows(a_q, a_k, a_v)
    for load in load_q + load_n:
        load.wait()
    glow[:, :8] = mm_nt(gq, b_q[...])
    for copy in left_att:
        copy.wait()
    for t in range(2):
        right_att(t).wait()
        mid.start(t, t % 2)
    for k in range(4):
        first[k] = mm_nt(gq, wide_w[k])

    inside = middle(ROWS, 0, lengths)
    suffix = scan.close(scan.pair[...] * (1.0 - c.astype(F32)))
    for copy in home:
        copy.wait()
    joined = (s < 31).astype(F32)
    late_row = lax.broadcasted_iota(jnp.int32, (ROWS, 128), 0) >= ROWS - WINDOW
    for j in range(KEY_HEADS):
        soft = pkey[j, WINDOW:]
        phi = soft.astype(BF16)
        keys = kv[j, WINDOW:][:, :DIM]
        rows = value_columns(kv[j, WINDOW:])[:, :STATE]
        high, rest = halves(suffix[j])
        high_next, rest_next = halves(suffix[j] - joined * next_state[j])
        grad_phi = jnp.where(late_row, mm(rows, high_next) + mm(rows, rest_next), mm(rows, high) + mm(rows, rest))
        grad_phi = grad_phi * inside + pkey[KEY_HEADS + j, WINDOW:]
        grad_v = jnp.where(
            late_row[:, :STATE], mm_nt(phi, high_next) + mm_nt(phi, rest_next), mm_nt(phi, high) + mm_nt(phi, rest)
        )
        grad_v = (grad_v * inside)[:, :DIM] + dv[j, WINDOW:]
        last = ROWS - WINDOW
        grad_phi = jnp.concatenate([grad_phi[:last], grad_phi[last:] + ret_came[j][:, 2 * DIM :]], axis=0)
        high, rest = halves(soft_back(soft, grad_phi))
        grad_k = dk[j, WINDOW:] + mm_nt(high, f_k[j]) + mm_nt(rest, f_k[j])
        gfk[j] = mm_tn(keys, high) + mm_tn(keys, rest)
        dk[j, WINDOW:] = jnp.concatenate([grad_k[:last], grad_k[last:] + ret_came[j][:, :DIM]], axis=0)
        dv[j, WINDOW:] = jnp.concatenate([grad_v[:last], grad_v[last:] + ret_came[j][:, DIM : 2 * DIM]], axis=0)
    gk = jnp.concatenate([dk[j, WINDOW:] for j in range(KEY_HEADS)], axis=1).astype(BF16)
    gv = jnp.concatenate([dv[j, WINDOW:] for j in range(KEY_HEADS)], axis=1).astype(BF16)
    gkv[...] = jnp.concatenate([gk, gv], axis=1)
    ya[2, 0:ROWS] = gkv[...]
    right_att(2).start()

    glow[:, 8:16] = mm_nt(gk, b_k[...])
    glow[:, 16:24] = mm_nt(gv, b_v[...])
    glow_high, glow_rest = halves(glow[...])
    gf_turns = to_mates(12, lambda i: gf_part.at[i], gs_came)
    dot = jnp.zeros((ROWS, 1), F32)
    for i in (1, 0, 2, 3):
        d = turned(y, 1 + i)
        rows = pl.ds(pl.multiple_of(d * COLS, COLS), COLS)
        down = columns(down_ref, d)
        part = (
            first[d]
            + mm_nt(gkv[:, :128], wk[rows, :])
            + mm_nt(gkv[:, 128:], wv[rows, :])
            + mm(glow_high, down)
            + mm(glow_rest, down)
        )
        if i < 3:
            gf_part[i] = part.astype(BF16)
            gf_turns[i].start()
        else:
            gsum[...] = part
        part = part * columns(x_all, d).astype(F32)
        dot = dot + jnp.sum(part * columns(gain_one, d), axis=1, keepdims=True)
        gain_row[:, rows] = jnp.sum(part * r1[...], axis=0, keepdims=True)
    dot_part[...] = jnp.broadcast_to(dot, (ROWS, 128)).T[:8]
    dot_turns = to_mates(15, lambda i: dot_part, dot_came)
    for turn in dot_turns:
        turn.start()

    for k in range(4):
        wide[:, k * COLS : (k + 1) * COLS] = mm_tn(glow_high, gb[k]) + mm_tn(glow_rest, gb[k])

    def place(d):
        return d // 16, d // 4 % 4, d % 4

    for i in range(16):
        cut = slice(i * 128, (i + 1) * 128)
        for half in range(2):
            d = place(2 * i + half)
            pk[*d, 0:12] = wide[12 * half : 12 * half + 12, cut]
            pk[*d, 13:16] = 0.25 * gbo[3 * half : 3 * half + 3, cut]
        pk[*place(2 * i), 12:13] = gain_row[:, cut]
        pk[*place(26 + i // 8), 16 + 2 * (i % 8) : 18 + 2 * (i % 8)] = gbo[6:8, cut]

    def low_half(d, value):
        pk[*place(d), 16 : 16 + value.shape[0]] = value

    for i in range(4):
        pair = jnp.concatenate([gfq[2 * i], gfq[2 * i + 1]], axis=1)
        for part in range(4):
            low_half(4 * i + part, pair[16 * part : 16 * part + 16])
    pair = jnp.concatenate([gfk[0], gfk[1]], axis=1)
    for part in range(4):
        low_half(16 + part, pair[16 * part : 16 * part + 16])
    grad_b = jnp.concatenate(
        [mm_tn(low[:, :8], gq), mm_tn(low[:, 8:16], gkv[:, :128]), mm_tn(low[:, 16:24], gkv[:, 128:])], axis=1
    )
    for i in range(3):
        low_half(20 + i, jnp.concatenate([grad_b[:, 256 * i : 256 * i + 128], grad_b[:, 256 * i + 128 : 256 * i + 256]]))
    for i in range(2):
        low_half(23 + i, jnp.concatenate([gao[:, 256 * i : 256 * i + 128], gao[:, 256 * i + 128 : 256 * i + 256]]))
    low_half(25, gain_rows_ref[...])
    pack_far = send(pk.at[1 - c], pk.at[2], sem_pack.at[0], sem_pack.at[1], sibling)
    pack_far.start()
    right_att(2).wait()
    mid.start(2, 0)
    pack_far.wait()

    def spread(base, piece, mates, back_piece):
        turns = [
            send(piece, piece, sem_zx.at[0, base + i], sem_zx.at[1, base + i], mate) for i, mate in enumerate(mates)
        ]
        for turn in turns:
            turn.start()
        return [
            send(back_piece(i), back_piece(i), sem_zx.at[0, base + i], sem_zx.at[1, base + i], mate)
            for i, mate in enumerate(mates)
        ]

    def mine(dest):
        return (pk[c, :, dest] + pk[2, :, dest]).astype(BF16)

    x_turns = [send(px.at[i], px_came.at[i], sem_zx.at[0, i], sem_zx.at[1, i], scan.x_mates[i]) for i in range(3)]
    for i in range(3):
        px[i] = mine(turned(x, 1 + i))
        x_turns[i].start()
    own_pack = pk[c, :, x] + pk[2, :, x]
    for t in (3, 4, 0, 1):
        mid.merge(t, t % 2)
    for turn in x_turns:
        turn.wait()
    own_pack = own_pack + px_came[0].astype(F32) + px_came[1].astype(F32) + px_came[2].astype(F32)
    pz[z] = own_pack.astype(BF16)
    z_turns = spread(3, pz.at[z], scan.z_mates, lambda i: pz.at[turned(z, 3 - i)])
    mid.merge(2, 0)
    over_pairs(2, 6, big.cross)
    for turn in z_turns:
        turn.wait()
    own_pack = pz[0].astype(F32) + pz[1].astype(F32) + pz[2].astype(F32) + pz[3].astype(F32)
    crown[y] = own_pack[:, :16]
    y_turns = spread(10, crown.at[y], y_mates, lambda i: crown.at[turned(y, 3 - i)])
    for t in (3, 4, 0, 1, 2):
        mid.cross(t, t % 2)
    for turn in y_turns:
        turn.wait()
    top = crown[0] + crown[1] + crown[2] + crown[3]
    out_pack[c, :, x] = jnp.concatenate([top, own_pack[:, 16:]], axis=1).astype(BF16)

    x_turns = spread(6, out_pack.at[c, :, x], scan.x_mates, lambda i: out_pack.at[c, :, turned(x, 3 - i)])
    over_pairs(0, 6, big.merge_cross)
    for t in (3, 4, 0, 1, 2):
        mid.merge_cross(t, t % 2)
    for turn in gf_turns + dot_turns:
        turn.wait()
    total = gsum[...] + gs_came[0].astype(F32) + gs_came[1].astype(F32) + gs_came[2].astype(F32)
    scale = r1[...]
    out_inputs[...] = (
        gres[...]
        + scale * (total * columns(gain_one, y))
        - columns(x_all, y).astype(F32) * (scale * scale * scale * mean_column(dot_part[...]))
    )
    for turn in x_turns:
        turn.wait()
    last = spread(9, out_pack.at[c], [sibling], lambda i: out_pack.at[1 - c])
    for turn in ffn_turns:
        turn.wait()
    out_block[...] = (
        hidden_in[...]
        + ffn_own[...].astype(F32)
        + ffn_came[0].astype(F32)
        + ffn_came[1].astype(F32)
        + ffn_came[2].astype(F32)
    ).astype(BF16)
    over_pairs(0, 6, big.end)
    for t in (3, 4, 0, 1, 2):
        mid.end(t, t % 2)
    for turn in last:
        turn.wait()
    over_pairs(0, 6, big.drain)
    for t in range(ATT_TILES):
        mid.drain(t, t % 2)


def back(args, weights):
    anywhere = pl.BlockSpec(memory_space=pl.ANY)
    vmem = pl.BlockSpec(memory_space=pltpu.VMEM)
    shapes = (
        ((ROWS, COLS), BF16),
        ((ROWS, COLS), F32),
        ((FFN_TILES, 64, FFN_WIDTH), F32),
        ((ATT_TILES, 64, ATT_WIDTH), F32),
        ((2, 4, 4, PACK, 128), BF16),
    )
    block = (ROWS, COLS)
    return pl.pallas_call(
        back_kernel,
        out_shape=tuple(jax.ShapeDtypeStruct(*shape) for shape in shapes),
        in_specs=[vmem] * 24 + [pl.BlockSpec(memory_space=pltpu.SMEM)] + [anywhere] * 11,
        out_specs=(vmem,) * len(shapes),
        scratch_shapes=[
            pltpu.VMEM((4, 512, 512), BF16),
            pltpu.VMEM((2048, 128), BF16),
            pltpu.VMEM((2048, 128), BF16),
            pltpu.VMEM((ROWS, 2048), BF16),
            pltpu.VMEM(block, BF16),
            pltpu.VMEM(block, BF16),
            pltpu.VMEM(block, BF16),
            pltpu.SemaphoreType.DMA((18,)),
            pltpu.VMEM((3, *block), BF16),
            pltpu.VMEM((3, *block), BF16),
            pltpu.VMEM((3, *block), BF16),
            pltpu.VMEM((8, ROWS), F32),
            pltpu.VMEM((3, 8, ROWS), F32),
            pltpu.VMEM((4, *block), BF16),
            pltpu.VMEM(block, F32),
            pltpu.VMEM(block, F32),
            pltpu.SemaphoreType.DMA((2, 18)),
            pltpu.VMEM((2, 4, 4, 64, 512), BF16),
            pltpu.VMEM((FFN_TILES, 512, FFN_WIDTH), BF16),
            pltpu.SemaphoreType.DMA((3, 2 + FFN_TILES)),
            pltpu.VMEM((2, 4, 4, 64, 512), BF16),
            pltpu.VMEM((ATT_TILES, 512, ATT_WIDTH), BF16),
            pltpu.VMEM((4, 4, 64, ROWS), BF16),
            pltpu.SemaphoreType.DMA((3, 2 + ATT_TILES)),
            pltpu.VMEM((3, 4, 4, PACK, 128), F32),
            pltpu.SemaphoreType.DMA((2,)),
            pltpu.VMEM((ROWS, SPAN), F32),
            pltpu.VMEM((ROWS, SPAN), F32),
            pltpu.VMEM((HEADS, ROWS, DIM), BF16),
            pltpu.VMEM((HEADS, ROWS, DIM), BF16),
            pltpu.VMEM((HEADS, ROWS, 128), F32),
            pltpu.VMEM((2 * KEY_HEADS, SPAN, 128), F32),
            pltpu.VMEM((HEADS, ROWS, 128), F32),
            pltpu.VMEM((KEY_HEADS, SPAN, DIM), F32),
            pltpu.VMEM((KEY_HEADS, SPAN, DIM), F32),
            pltpu.VMEM((HEADS, DIM, DIM), F32),
            pltpu.VMEM((KEY_HEADS, DIM, DIM), F32),
            pltpu.VMEM((KEY_HEADS, WINDOW, 256), F32),
            pltpu.VMEM((KEY_HEADS, WINDOW, 256), F32),
            pltpu.VMEM((KEY_HEADS, STATE, 128), F32),
            pltpu.SemaphoreType.DMA((4,)),
            pltpu.VMEM((ROWS, 24), F32),
            pltpu.VMEM((ROWS, 256), BF16),
            pltpu.VMEM((24, 2048), F32),
            pltpu.VMEM((8, COLS), F32),
            pltpu.VMEM((8, 2048), F32),
            pltpu.VMEM((24, 2048), BF16),
            pltpu.VMEM((4, *block), F32),
            pltpu.VMEM((1, 2048), F32),
            pltpu.VMEM((4, 128), F32),
            pltpu.VMEM((3, 4, PACK, 128), BF16),
            pltpu.VMEM((3, 4, PACK, 128), BF16),
            pltpu.VMEM((4, 4, PACK, 128), BF16),
            pltpu.VMEM((4, 4, 16, 128), F32),
            pltpu.SemaphoreType.DMA((2, 13)),
            *Scan.scratch((KEY_HEADS, STATE, 128)),
            *Ring.scratch(FFN_TILES, 64, FFN_WIDTH),
            *Ring.scratch(ATT_TILES, 64, ATT_WIDTH),
        ],
        compiler_params=pltpu.CompilerParams(
            collective_id=2, has_side_effects=True, vmem_limit_bytes=63 * 2**20
        ),
        name="back",
    )(*args, *weights)


def finish_kernel(
    block, inputs, ffn_sums, att_sums, packed,
    block_out, inputs_out, gain_one, w_q, a_q, b_q, w_k, a_k, b_k, w_v, a_v, b_v, f_q, f_k, w_o, a_o, b_o, gain_two,
    w_gate, w_up, w_down,
):
    block_out[...] = block[...]
    pack = packed[...].astype(F32)
    inputs_out[...] = inputs[...]
    for i in range(4):
        cut = slice(i * FFN_WIDTH, (i + 1) * FFN_WIDTH)
        w_gate[:, cut] = ffn_sums[i]
        w_up[:, cut] = ffn_sums[4 + i]
        w_down[:, cut] = ffn_sums[8 + i]
    for i in range(2):
        cut = slice(i * ATT_WIDTH, (i + 1) * ATT_WIDTH)
        w_q[:, cut] = att_sums[i]
        w_o[:, cut] = att_sums[3 + i]
    w_k[...] = att_sums[2, :, :128]
    w_v[...] = att_sums[2, :, 128:]
    for i in range(16):
        cut = slice(i * 128, (i + 1) * 128)
        rows = jnp.concatenate([pack[2 * i, :12], pack[2 * i + 1, :12]], axis=0)
        a_q[:, cut] = rows[:8]
        a_k[:, cut] = rows[8:16]
        a_v[:, cut] = rows[16:]
        last = 16 + 2 * (i % 8)
        b_o[:, cut] = jnp.concatenate(
            [pack[2 * i, 13:16], pack[2 * i + 1, 13:16], pack[26 + i // 8, last : last + 2]], axis=0
        )

    def tile(i):
        return pack[20 + i // 2, 16 + 8 * (i % 2) : 24 + 8 * (i % 2)]

    for i in range(4):
        cut = slice(i * 128, (i + 1) * 128)
        for part in range(4):
            rows = pack[4 * i + part, 16:]
            f_q[2 * i, 16 * part : 16 * part + 16] = rows[:, :DIM]
            f_q[2 * i + 1, 16 * part : 16 * part + 16] = rows[:, DIM:]
        rows = pack[16 + i, 16:]
        f_k[0, 16 * i : 16 * i + 16] = rows[:, :DIM]
        f_k[1, 16 * i : 16 * i + 16] = rows[:, DIM:]
        b_q[:, cut] = tile(i)
        a_o[:, cut] = tile(6 + i)
        gain_two[:, cut] = pack[25, 16 + i : 17 + i]
        gain_one[:, cut] = packed[8 * lax.axis_index("head") + 2 * i].astype(F32)[12:13]
    b_k[...] = tile(4)
    b_v[...] = tile(5)


def finish(block, inputs, ffn_sums, att_sums, pack):
    vmem = pl.BlockSpec(memory_space=pltpu.VMEM)
    shapes = (
        (ROWS, COLS), (ROWS, COLS), (1, COLS), (64, COLS), (8, 2048), (8, COLS), (64, 128), (8, 2048), (8, 128),
        (64, 128), (8, 2048), (8, 128), (HEADS, DIM, DIM), (KEY_HEADS, DIM, DIM), (64, COLS), (8, COLS), (8, 2048),
        (1, COLS), (64, 2048), (64, 2048), (64, 2048),
    )
    outs = pl.pallas_call(
        finish_kernel,
        out_shape=tuple(jax.ShapeDtypeStruct(shape, F32 if i else BF16) for i, shape in enumerate(shapes)),
        in_specs=[vmem] * 5,
        out_specs=(vmem,) * len(shapes),
        compiler_params=pltpu.CompilerParams(vmem_limit_bytes=32 * 2**20),
        name="finish",
    )(block, inputs, ffn_sums, att_sums, pack.reshape(32, 32, 128))
    return tuple(
        out[0] if i in (2, 17) else out.T if i in (4, 7, 10, 14, 15, 20) else out for i, out in enumerate(outs)
    )


def body(
    inputs,
    gain_first,
    w_query,
    a_query,
    b_query,
    key_projection_weight,
    a_key,
    key_adapter_second,
    value_projection_weight,
    a_value,
    value_adapter_second,
    feature_query,
    key_hedgehog_map,
    w_out,
    a_out,
    b_out,
    gain_second,
    w_gate,
    w_up,
    w_down,
    lengths,
    cotangent,
):
    gain_one, gain_two = gain_first[None], gain_second[None]
    a_in = (a_query.T, a_key.T, a_value.T)
    a_out = a_out.T
    projections = (w_query, key_projection_weight, value_projection_weight, w_out)
    normed, low, queries, kv, state, att, stat, mixed, low_mix, hidden_in, g, r2, r1 = front(
        inputs, gain_one, gain_two, *a_in, b_query, key_adapter_second, value_adapter_second,
        feature_query, key_hedgehog_map, a_out, b_out, lengths, *projections,
    )
    y_ffn, gs, ffn_sum, xt, dot_two = ffn(g, r2, cotangent, normed, w_gate, w_up, w_down)
    block_out, grad_inputs, out_ffn, out_att, out_pack = back(
        (
            dot_two, hidden_in, r1, r2, gain_one, gain_two, mixed, low_mix, att, stat, state, queries, kv, low,
            feature_query, key_hedgehog_map, *a_in, a_out, b_out, b_query, key_adapter_second,
            value_adapter_second, lengths,
        ),
        (gs, ffn_sum, normed, inputs, cotangent, xt, y_ffn.reshape(FFN_TILES, ROWS, FFN_WIDTH), *projections),
    )
    return finish(block_out, grad_inputs, out_ffn, out_att, out_pack)


def solution(mesh):
    return jax.shard_map(
        body,
        mesh=mesh,
        in_specs=(
            P("seq", None),
            P(),
            P(None, "head"),
            P(),
            P(None, "head"),
            P(None, "head"),
            P(),
            P(None, "head"),
            P(None, "head"),
            P(),
            P(None, "head"),
            P("head", None, None),
            P("head", None, None),
            P("head", None),
            P("head", None),
            P(),
            P(),
            P(None, "head"),
            P(None, "head"),
            P("head", None),
            P(),
            P("seq", None),
        ),
        out_specs=(
            P("seq", "head"),
            P("seq", "head"),
            P("head"),
            P("seq", "head"),
            P(),
            P(None, "head"),
            P("seq", "head"),
            P(),
            P(None, "head"),
            P("seq", "head"),
            P(),
            P(None, "head"),
            P("head", None, None),
            P("head", None, None),
            P("head", "seq"),
            P("head", None),
            P(),
            P("head"),
            P("seq", "head"),
            P("seq", "head"),
            P("head", "seq"),
        ),
        check_vma=False,
    )
```

```python
import jax
import jax.numpy as jnp
from jax import lax
from jax.experimental import pallas as pl
from jax.experimental.pallas import tpu as pltpu
from jax.sharding import PartitionSpec as P

MESH = pl.DeviceIdType.MESH
F32 = jnp.float32
BF16 = jnp.bfloat16


def spot():
    s = lax.axis_index("seq")
    y = lax.axis_index("head")
    return lax.div(s, 8), lax.rem(lax.div(s, 2), 4), lax.rem(s, 2), y


def at(z, x, c, y):
    return ((z * 4 + x) * 2 + c, y)


def turned(p, steps):
    return lax.rem(p + steps, 4)


def greet(partners):
    barrier = pltpu.get_barrier_semaphore()
    for partner in partners:
        pl.semaphore_signal(barrier, inc=1, device_id=partner, device_id_type=MESH)
    pl.semaphore_wait(barrier, len(partners))


def send(src, dst, ss, rs, device):
    return pltpu.make_async_remote_copy(
        src_ref=src, dst_ref=dst, send_sem=ss, recv_sem=rs, device_id=device, device_id_type=MESH
    )


def took(ref, sem):
    pltpu.make_async_copy(ref, ref, sem).wait()


class Ring:
    def __init__(self, refs, rows, pieces, term, finish):
        self.sb, self.ra, self.rf, self.ra3, self.rf3, self.ss, self.rs = refs
        self.rows, self.pieces, self.term, self.finish = rows, pieces, term, finish
        z, x, c, y = spot()
        self.axes = (
            (x, at(z, turned(x, 1), c, y), at(z, turned(x, 3), c, y)),
            (z, at(turned(z, 1), x, c, y), at(turned(z, 3), x, c, y)),
        )

    @staticmethod
    def scratch(count, pieces, rows, width):
        return [
            pltpu.VMEM((count, 2, pieces, 4 * rows, width), BF16),
            pltpu.VMEM((count, 2, pieces, 2 * rows, width), BF16),
            pltpu.VMEM((count, 2, pieces, 4 * rows, width), BF16),
            pltpu.VMEM((count, 2, pieces, rows // 2, width), BF16),
            pltpu.VMEM((count, 2, pieces, rows, width), BF16),
            pltpu.SemaphoreType.DMA((count, 4)),
            pltpu.SemaphoreType.DMA((count, 6)),
        ]

    def each(self, step):
        if self.pieces == 1:
            step(0)
        else:

            def one(p, carry):
                step(p)
                return carry

            lax.fori_loop(0, self.pieces, one, 0)

    def block(self, b, part):
        g = self.rows // 2
        if part is None:
            return pl.ds(pl.multiple_of(b * self.rows, self.rows), self.rows)
        return pl.ds(pl.multiple_of(b * self.rows + part * g, g), g)

    def copy(self, t, k, i):
        p, ahead, behind = self.axes[k]
        q, ahead3, behind3 = self.axes[1 - k]
        h, g = 2 * self.rows, self.rows // 2
        lo, hi, lo3, hi3 = pl.ds(0, h), pl.ds(h, h), pl.ds(0, g), pl.ds(g, g)
        sb, ra, rf, ra3, rf3, block = self.sb, self.ra, self.rf, self.ra3, self.rf3, self.block
        src, dst, device = (
            lambda: (sb.at[t, 0, :, lo], ra.at[t, 0], ahead),
            lambda: (sb.at[t, 0, :, hi], ra.at[t, 1], behind),
            lambda: (sb.at[t, 1, :, hi], rf.at[t, 0, :, hi], ahead),
            lambda: (sb.at[t, 1, :, lo], rf.at[t, 1, :, lo], behind),
            lambda: (ra.at[t, 0], rf.at[t, 0, :, lo], ahead),
            lambda: (ra.at[t, 1], rf.at[t, 1, :, hi], behind),
            lambda: (sb.at[t, 0, :, block(turned(q, 2), 0)], ra3.at[t, 0], ahead3),
            lambda: (sb.at[t, 0, :, block(turned(q, 2), 1)], ra3.at[t, 1], behind3),
            lambda: (sb.at[t, 0, :, block(turned(q, 1), 1)], rf3.at[t, 0, :, hi3], ahead3),
            lambda: (sb.at[t, 0, :, block(turned(q, 3), 0)], rf3.at[t, 1, :, lo3], behind3),
            lambda: (ra3.at[t, 0], rf3.at[t, 0, :, lo3], ahead3),
            lambda: (ra3.at[t, 1], rf3.at[t, 1, :, hi3], behind3),
        )[i]()
        here = (0, 0, 0, 0, 1, 1, 2, 2, 2, 2, 3, 3)[i]
        there = (0, 1, 2, 2, 2, 2, 3, 4, 5, 5, 5, 5)[i]
        return send(src, dst, self.ss.at[t, here], self.rs.at[t, there], device)

    def sent(self, t, group):
        took((self.sb, self.ra, self.rf3, self.ra3)[group].at[t], self.ss.at[t, group])

    def arrived(self, t, group):
        ref = (self.ra.at[t, 0], self.ra.at[t, 1], self.rf.at[t], self.ra3.at[t, 0], self.ra3.at[t, 1], self.rf3.at[t])
        took(ref[group], self.rs.at[t, group])

    def start(self, t, k):
        p = self.axes[k][0]
        h = 2 * self.rows

        def far(i):
            self.sb[t, 0, i] = self.term(t, i, k, turned(p, 2), 0, 4).astype(BF16)

        def near(i):
            self.sb[t, 1, i, h:] = self.term(t, i, k, turned(p, 1), 2, 4).astype(BF16)
            self.sb[t, 1, i, :h] = self.term(t, i, k, turned(p, 3), 0, 2).astype(BF16)

        self.each(far)
        self.copy(t, k, 0).start()
        self.copy(t, k, 1).start()
        self.each(near)
        self.copy(t, k, 2).start()
        self.copy(t, k, 3).start()

    def merge(self, t, k):
        p = self.axes[k][0]
        for way, dest, first in ((0, turned(p, 1), 0), (1, turned(p, 3), 2)):
            self.arrived(t, way)

            def one(i):
                mine = self.term(t, i, k, dest, first, first + 2)
                self.ra[t, way, i] = (mine + self.ra[t, way, i].astype(F32)).astype(BF16)

            self.each(one)
            self.copy(t, k, 4 + way).start()

    def cross(self, t, k):
        p = self.axes[k][0]
        self.sent(t, 0)
        self.arrived(t, 2)

        def one(i):
            own = self.term(t, i, k, p, 0, 4)
            self.sb[t, 0, i] = (own + self.rf[t, 0, i].astype(F32) + self.rf[t, 1, i].astype(F32)).astype(BF16)

        self.each(one)
        for i in (6, 7, 8, 9):
            self.copy(t, k, i).start()

    def merge_cross(self, t, k):
        q = self.axes[1 - k][0]
        for way, dest in ((0, turned(q, 1)), (1, turned(q, 3))):
            self.arrived(t, 3 + way)

            def one(i):
                mine = self.sb[t, 0, i, self.block(dest, way), :]
                self.ra3[t, way, i] = (mine.astype(F32) + self.ra3[t, way, i].astype(F32)).astype(BF16)

            self.each(one)
            self.copy(t, k, 10 + way).start()

    def end(self, t, k):
        q = self.axes[1 - k][0]
        self.arrived(t, 5)

        def one(i):
            mine = self.sb[t, 0, i, self.block(q, None), :].astype(F32)
            self.finish(t, i, k, mine + self.rf3[t, 0, i].astype(F32) + self.rf3[t, 1, i].astype(F32))

        self.each(one)

    def drain(self, t, k):
        for group in (1, 2, 3):
            self.sent(t, group)


FFN_TILES, FFN_PARTS, FFN_WIDTH = 4, 3, 512
ATT_TILES, ATT_WIDTH = 5, 256
PACK = 32


EPS = 1e-05
NEG = -1e30
HIGH = lax.Precision.HIGHEST
ROWS = 256
WINDOW = 64
SPAN = ROWS + WINDOW
COLS = 512
HEADS, KEY_HEADS, DIM = 8, 2, 64
STATE = 72


def mm(a, b):
    return jnp.dot(a, b, preferred_element_type=F32)


def mm_nt(a, b, precision=None):
    return lax.dot_general(a, b, (((1,), (1,)), ((), ())), precision=precision, preferred_element_type=F32)


def mm_tn(a, b, precision=None):
    return lax.dot_general(a, b, (((0,), (0,)), ((), ())), precision=precision, preferred_element_type=F32)


def halves(value):
    top = value.astype(BF16)
    return top, (value - top.astype(F32)).astype(BF16)


def down_rows(a_q, a_k, a_v):
    return jnp.concatenate([a[...].astype(F32) for a in (a_q, a_k, a_v)], axis=0).astype(BF16)


def soft_pair(rows, table):
    both = mm(rows, jnp.concatenate([table, -table], axis=1))
    left = lax.broadcasted_iota(jnp.int32, both.shape, 1) < DIM
    upper = jnp.max(jnp.where(left, both, NEG), axis=1, keepdims=True)
    lower = jnp.max(jnp.where(left, NEG, both), axis=1, keepdims=True)
    grown = jnp.exp(both - jnp.where(left, upper, lower))
    sum_left = jnp.sum(jnp.where(left, grown, 0.0), axis=1, keepdims=True)
    sum_right = jnp.sum(jnp.where(left, 0.0, grown), axis=1, keepdims=True)
    return grown / jnp.where(left, sum_left, sum_right)


def doc_at(positions, lengths):
    first = lengths[0]
    second = first + lengths[1]
    return (
        (positions >= 0).astype(jnp.int32)
        + (positions >= first).astype(jnp.int32)
        + (positions >= second).astype(jnp.int32)
    )


def write_mask(mask, lengths):
    base = lax.axis_index("seq") * ROWS
    row = lax.broadcasted_iota(jnp.int32, (ROWS, SPAN), 0) + base
    column = lax.broadcasted_iota(jnp.int32, (ROWS, SPAN), 1) + base - WINDOW
    same = doc_at(row, lengths) == doc_at(column, lengths)
    offset = row - column
    here = jnp.where(offset < WINDOW, 0.0, NEG)
    mask[...] = jnp.where(same & (offset >= 0), here, 2.0 * NEG)


def middle(count, first, lengths):
    base = lax.axis_index("seq") * ROWS + first
    position = lax.broadcasted_iota(jnp.int32, (count, 1), 0) + base
    return (doc_at(position, lengths) == 2).astype(F32)


def value_columns(kv):
    lane = lax.broadcasted_iota(jnp.int32, kv.shape, 1)
    v = jnp.concatenate([kv[:, DIM:], kv[:, :DIM]], axis=1)
    return jnp.where(lane < DIM, v, jnp.where(lane == DIM, 1.0, 0.0).astype(kv.dtype))


class Scan:
    def __init__(self, refs, reverse):
        self.own, self.pair, self.line, self.plane, self.sem = refs
        self.reverse = reverse
        z, x, c, y = spot()
        self.z, self.x, self.c = z, x, c
        self.sibling = at(z, x, 1 - c, y)
        self.x_mates = [at(z, turned(x, i), c, y) for i in (1, 2, 3)]
        self.z_mates = [at(turned(z, i), x, c, y) for i in (1, 2, 3)]

    @staticmethod
    def scratch(shape):
        return [
            pltpu.VMEM((3, *shape), F32),
            pltpu.VMEM(shape, F32),
            pltpu.VMEM((3, *shape), F32),
            pltpu.VMEM((3, *shape), F32),
            pltpu.SemaphoreType.DMA((2, 7)),
        ]

    def pair_copy(self):
        return send(self.own.at[0], self.pair, self.sem.at[0, 0], self.sem.at[1, 0], self.sibling)

    def line_copy(self, i):
        return send(self.own.at[1], self.line.at[i], self.sem.at[0, 1 + i], self.sem.at[1, 1 + i], self.x_mates[i])

    def plane_copy(self, i):
        return send(self.own.at[2], self.plane.at[i], self.sem.at[0, 4 + i], self.sem.at[1, 4 + i], self.z_mates[i])

    def counts(self, me, other):
        return ((other > me) if self.reverse else (other < me)).astype(F32)

    def open(self):
        self.pair_copy().start()

    def along_x(self):
        self.pair_copy().wait()
        self.own[1] = self.own[0] + self.pair[...]
        for i in range(3):
            self.line_copy(i).start()

    def along_z(self):
        for i in range(3):
            self.line_copy(i).wait()
        self.own[2] = self.own[1] + self.line[0] + self.line[1] + self.line[2]
        for i in range(3):
            self.plane_copy(i).start()

    def close(self, total):
        for i in range(3):
            self.plane_copy(i).wait()
        for i in range(3):
            total = total + self.line[i] * self.counts(self.x, turned(self.x, 3 - i))
        for i in range(3):
            total = total + self.plane[i] * self.counts(self.z, turned(self.z, 3 - i))
        return total


def front_kernel(
    x_ref, gain_one, gain_two, a_q, a_k, a_v, b_q, b_k, b_v, f_q, f_k, a_out, b_out, lengths, w_q, w_k, w_v, w_o, cot_hbm,
    normed_out, low_out, qh, kv_out, state_out, att_out, stat_out, mixed_out, lowmix_out, hidden_out, g_out, scales_out, xt_out,
    wq, wk, wv, wo, cot, w_sem, phq, phk, num, mask, q_rows, stat, brief, tail_sem,
    part, came, y_sem, low_part, square, square_came,
    *scan_refs,
):
    z, x, c, y = spot()
    s = lax.axis_index("seq")
    following, leading = (lax.rem(s + 1, 32), y), (lax.rem(s + 31, 32), y)
    y_mates = [at(z, x, c, turned(y, i)) for i in (1, 2, 3)]
    scan = Scan(scan_refs, False)
    greet([following, leading, scan.sibling] + scan.x_mates + scan.z_mates + y_mates)
    loads = [
        pltpu.make_async_copy(src, dst, w_sem.at[i])
        for i, (src, dst) in enumerate(((w_q, wq), (w_k, wk), (w_v, wv), (w_o, wo), (cot_hbm, cot)))
    ]
    for load in loads:
        load.start()
    for i in range(4):
        rows = pl.ds(64 * i, 64)
        value = x_ref[rows, :].astype(F32)
        scale = lax.rsqrt(jnp.mean(value * value, axis=1, keepdims=True) + EPS)
        scales_out[rows, 0:1] = scale
        normed_out[rows, :] = (value * scale * gain_one[...]).astype(BF16)
    write_mask(mask, lengths)
    low_out[...] = mm_nt(normed_out[...], down_rows(a_q, a_k, a_v)).astype(BF16)
    low = low_out[...]
    loads[1].wait()
    loads[2].wait()
    k = (mm(normed_out[...], wk[...]) + mm(low[:, 8:16], b_k[...])).astype(BF16)
    v = (mm(normed_out[...], wv[...]) + mm(low[:, 16:24], b_v[...])).astype(BF16)
    for j in range(KEY_HEADS):
        cut = slice(j * DIM, (j + 1) * DIM)
        kv_out[j, WINDOW:] = jnp.concatenate([k[:, cut], v[:, cut]], axis=1)
    tail = send(
        kv_out.at[:, pl.ds(ROWS, WINDOW)], kv_out.at[:, pl.ds(0, WINDOW)], tail_sem.at[0], tail_sem.at[1], following
    )
    tail.start()
    loads[0].wait()
    for i in range(2):
        cut = slice(i * 256, (i + 1) * 256)
        q_rows[:, cut] = (mm(normed_out[...], wq[:, cut]) + mm(low[:, :8], b_q[:, cut])).astype(BF16)
    for h in range(HEADS):
        qh[h] = q_rows[:, h * DIM : (h + 1) * DIM]
    inside = middle(ROWS, 0, lengths)
    for j in range(KEY_HEADS):
        phk[j, WINDOW:] = soft_pair(kv_out[j, WINDOW:][:, :DIM], f_k[j]).astype(BF16)
        counted = (phk[j, WINDOW:].astype(F32) * inside).astype(BF16)
        rows = value_columns(kv_out[j, WINDOW:])
        settled = mm_tn(rows[: ROWS - WINDOW], counted[: ROWS - WINDOW])[:STATE]
        brief[0, j] = settled
        scan.own[0, j] = settled + mm_tn(rows[ROWS - WINDOW :], counted[ROWS - WINDOW :])[:STATE]
    brief_turn = send(brief.at[0], brief.at[1], tail_sem.at[2], tail_sem.at[3], scan.sibling)
    brief_turn.start()
    scan.open()

    def features(h, carry):
        phq[h] = soft_pair(qh[h], f_q[h]).astype(BF16)
        return carry

    lax.fori_loop(0, 4, features, 0)
    scan.along_x()
    lax.fori_loop(4, HEADS, features, 0)
    tail.wait()
    inside = middle(WINDOW, -WINDOW, lengths)
    for j in range(KEY_HEADS):
        phk[j, :WINDOW] = soft_pair(kv_out[j, :WINDOW][:, :DIM], f_k[j]).astype(BF16)
        counted = (phk[j, :WINDOW].astype(F32) * inside).astype(BF16)
        brief[2, j] = mm_tn(value_columns(kv_out[j, :WINDOW]), counted)[:STATE]
    brief_turn.wait()

    def inner(h, carry):
        j = lax.div(h, 4)
        kv = kv_out[j]
        distant = mask[...] == NEG
        scores = mm_nt(qh[h], kv[:, :DIM]) * (DIM**-0.5) + mask[...]
        top = jnp.max(scores, axis=1, keepdims=True)
        weights = jnp.exp(scores - top)
        total = weights + jnp.where(distant, mm_nt(phq[h], phk[j]) * jnp.exp(-top), 0.0)
        high = total.astype(BF16)
        rest = jnp.where(distant, total - high.astype(F32), 0.0).astype(BF16)
        v = kv[:, DIM:]
        num[h] = mm(high, v) + mm(rest, v)
        stat[h, :, 0:1] = top
        stat[h, :, 1:2] = jnp.sum(total, axis=1, keepdims=True)
        return carry

    lax.fori_loop(0, 4, inner, 0)
    scan.along_z()
    lax.fori_loop(4, HEADS, inner, 0)
    second = c.astype(F32)
    state_out[...] = scan.close(brief[1] * second - brief[2] * (1.0 - second))
    mine = middle(ROWS, 0, lengths)
    for h in range(HEADS):
        top, rest = halves(state_out[h // 4])
        carried = mm_nt(phq[h], top) + mm_nt(phq[h], rest)
        gate = jnp.exp(-stat[h, :, 0:1]) * mine
        total = stat[h, :, 1:2] + gate * carried[:, DIM : DIM + 1]
        stat[h, :, 1:2] = total
        stat[h, :, 2:3] = gate
        cut = slice(h * DIM, (h + 1) * DIM)
        attended = (num[h] + gate * carried[:, :DIM]) / total
        att_out[:, cut] = attended
        mixed_out[:, cut] = attended.astype(BF16)
        stat_out[h] = stat[h].T
    mixed = mixed_out[...]
    low_part[y] = mm_nt(a_out[...], mixed)
    low_turns = [send(low_part.at[y], low_part.at[y], y_sem.at[0, i], y_sem.at[1, i], y_mates[i]) for i in range(3)]
    for turn in low_turns:
        turn.start()
    loads[3].wait()

    def columns(ref, d):
        return ref[:, pl.ds(pl.multiple_of(d * COLS, COLS), COLS)]

    turns = [send(part.at[i], came.at[i], y_sem.at[0, 3 + i], y_sem.at[1, 3 + i], y_mates[i]) for i in range(3)]
    for i in (1, 0, 2):
        part[i] = mm(mixed, columns(wo, turned(y, 1 + i))).astype(BF16)
        turns[i].start()
    value = mm(mixed, columns(wo, y)) + columns(x_ref, y).astype(F32)

    def by_owner(m, rows):
        for i in range(16):
            flat = rows[:, i * 128 : (i + 1) * 128].T
            xt_out[m, 0, i // 4, i % 4] = flat[:64]
            xt_out[m, 1, i // 4, i % 4] = flat[64:]

    by_owner(0, normed_out)
    for i in range(3):
        here = low_part.at[turned(y, 3 - i)]
        send(here, here, y_sem.at[0, i], y_sem.at[1, i], y_mates[i]).wait()
    low_sum = low_part[0] + low_part[1] + low_part[2] + low_part[3]
    lowmix_out[...] = low_sum.T.astype(BF16)
    value = value + mm(lowmix_out[...], columns(b_out, y))
    for turn in turns:
        turn.wait()
    value = value + came[0].astype(F32) + came[1].astype(F32) + came[2].astype(F32)
    hidden_out[...] = value
    g_out[y] = (value * columns(gain_two, y)).astype(BF16)
    turns = [send(g_out.at[y], g_out.at[y], y_sem.at[0, 9 + i], y_sem.at[1, 9 + i], y_mates[i]) for i in range(3)]
    square[...] = mm_nt(jnp.ones((8, COLS), F32), value * value, HIGH)
    square_turns = [
        send(square, square_came.at[i], y_sem.at[0, 6 + i], y_sem.at[1, 6 + i], y_mates[i]) for i in range(3)
    ]
    for turn in square_turns + turns:
        turn.start()
    loads[4].wait()
    by_owner(1, cot)
    for turn in square_turns:
        turn.wait()
    mean = (square[...] + square_came[0] + square_came[1] + square_came[2]) * (1.0 / 2048)
    scales_out[:, 1:2] = lax.rsqrt(mean + EPS).T[:, 0:1]
    for i in range(3):
        here = g_out.at[turned(y, 3 - i)]
        send(here, here, y_sem.at[0, 9 + i], y_sem.at[1, 9 + i], y_mates[i]).wait_recv()
    for turn in turns:
        turn.wait_send()


def front(*args):
    anywhere = pl.BlockSpec(memory_space=pl.ANY)
    vmem = pl.BlockSpec(memory_space=pltpu.VMEM)
    shapes = (
        ((ROWS, 2048), BF16),
        ((ROWS, 24), BF16),
        ((HEADS, ROWS, DIM), BF16),
        ((KEY_HEADS, SPAN, 128), BF16),
        ((KEY_HEADS, STATE, 128), F32),
        ((ROWS, 512), F32),
        ((HEADS, 8, ROWS), F32),
        ((ROWS, 512), BF16),
        ((ROWS, 8), BF16),
        ((ROWS, COLS), F32),
        ((4, ROWS, COLS), BF16),
        ((ROWS, 2), F32),
        ((2, 2, 4, 4, 64, ROWS), BF16),
    )
    return pl.pallas_call(
        front_kernel,
        out_shape=tuple(jax.ShapeDtypeStruct(*shape) for shape in shapes),
        in_specs=[vmem] * 13 + [pl.BlockSpec(memory_space=pltpu.SMEM)] + [anywhere] * 5,
        out_specs=(vmem,) * len(shapes),
        scratch_shapes=[
            pltpu.VMEM((2048, 512), BF16),
            pltpu.VMEM((2048, 128), BF16),
            pltpu.VMEM((2048, 128), BF16),
            pltpu.VMEM((512, 2048), BF16),
            pltpu.VMEM((ROWS, 2048), BF16),
            pltpu.SemaphoreType.DMA((5,)),
            pltpu.VMEM((HEADS, ROWS, 128), BF16),
            pltpu.VMEM((KEY_HEADS, SPAN, 128), BF16),
            pltpu.VMEM((HEADS, ROWS, DIM), F32),
            pltpu.VMEM((ROWS, SPAN), F32),
            pltpu.VMEM((ROWS, 512), BF16),
            pltpu.VMEM((HEADS, ROWS, 8), F32),
            pltpu.VMEM((3, KEY_HEADS, STATE, 128), F32),
            pltpu.SemaphoreType.DMA((4,)),
            pltpu.VMEM((3, ROWS, COLS), BF16),
            pltpu.VMEM((3, ROWS, COLS), BF16),
            pltpu.SemaphoreType.DMA((2, 12)),
            pltpu.VMEM((4, 8, ROWS), F32),
            pltpu.VMEM((8, ROWS), F32),
            pltpu.VMEM((3, 8, ROWS), F32),
            *Scan.scratch((KEY_HEADS, STATE, 128)),
        ],
        compiler_params=pltpu.CompilerParams(
            collective_id=1, has_side_effects=True, vmem_limit_bytes=60 * 2**20
        ),
        name="front",
    )(*args)


def soft_back(soft, grad):
    left = lax.broadcasted_iota(jnp.int32, soft.shape, 1) < DIM
    part = soft * grad
    sum_left = jnp.sum(jnp.where(left, part, 0.0), axis=1, keepdims=True)
    sum_right = jnp.sum(jnp.where(left, 0.0, part), axis=1, keepdims=True)
    both = part - soft * jnp.where(left, sum_left, sum_right)
    return both[:, :DIM] - both[:, DIM:]


def late_kernel(
    hidden_in, scales, gain_one, gain_two, mixed, low_mix, att, stat, state, qh, kv, low,
    f_q, f_k, a_q, a_k, a_v, a_out, b_out, b_q, b_k, b_v, lengths,
    g_hbm, normed_hbm, x_hbm, cot_hbm, xt_hbm, w_q, w_k, w_v, w_o, w_gate, w_up, w_down,
    out_block, out_inputs, out_ffn, out_att, out_pack, out_gain,
    wb, x_all, w_sem,
    gs_came, ffn_came, gf_part, dot_part, dot_came, gb, gres, gsum, y_sem,
    xf, yf, xs, sem_ffn, xa, ya, sem_att, pk, sem_pack,
    mask, gh, pq, pkey, dext, dkv, gfq, gfk, ret, ret_came, next_state, ret_sem, glow, gkv, wide, gao, gbo, down_ref,
    first, gain_row, gain_rows_ref, px, px_came, pz, crown, sem_zx, stage, sem_stage, gain_c, gain_x, gain_z, gain_y, sem_gain,
    *rest,
):
    scan = Scan(rest[0:5], True)
    refs_big, refs_mid = rest[5:12], rest[12:19]
    z, x, c, y = spot()
    s = lax.axis_index("seq")
    following, leading = (lax.rem(s + 1, 32), y), (lax.rem(s + 31, 32), y)
    y_mates = [at(z, x, c, turned(y, i)) for i in (1, 2, 3)]
    sibling = scan.sibling
    greet([following, leading, sibling] + scan.x_mates + scan.z_mates + y_mates)

    def columns(ref, d):
        return ref[:, pl.ds(pl.multiple_of(d * COLS, COLS), COLS)]

    def to_mates(base, pieces, slots):
        return [
            send(pieces(i), slots.at[i], y_sem.at[0, base + i], y_sem.at[1, base + i], y_mates[i]) for i in range(3)
        ]

    own_rows, far_rows = pl.ds(0, ROWS), pl.ds(ROWS, ROWS)

    def local(i, src, dst):
        return pltpu.make_async_copy(src, dst, w_sem.at[i])

    def turn_at(n):
        return turned(y, 1 + n)

    def part(n):
        return pl.ds(pl.multiple_of(n * COLS, COLS), COLS)

    def held(slot):
        local(slot, w_o.at[:, part(0)], wb.at[slot]).wait()

    def load_forward(u, slot):
        i = slot % 4
        src = (
            lambda: w_gate.at[part(i), part(u)],
            lambda: w_up.at[part(i), part(u)],
            lambda: w_down.at[part(u), part(i)],
        )[slot // 4]()
        local(slot, src, wb.at[slot]).start()

    def load_later(b):
        slot = b % 12
        if b < 32:
            src = (w_gate, w_up)[b % 8 // 4].at[part(turn_at(b // 8)), part(b % 4)]
        elif b < 48:
            src = w_down.at[part(b % 4), part(turn_at((b - 32) // 4))]
        elif b < 52:
            src = w_o.at[:, part(slot)]
        elif b < 56:
            src = w_q.at[part(slot - 4)]
        else:
            rows = part(slot - 8)
            local(slot, w_k.at[rows], wb.at[slot, :, pl.ds(0, 128)]).start()
            local(slot + 4, w_v.at[rows], wb.at[slot, :, pl.ds(128, 128)]).start()
            return
        local(slot, src, wb.at[slot]).start()

    def held_pair(slot):
        rows = part(slot - 8)
        local(slot, w_k.at[rows], wb.at[slot, :, pl.ds(0, 128)]).wait()
        local(slot + 4, w_v.at[rows], wb.at[slot, :, pl.ds(128, 128)]).wait()

    load_g = local(16, g_hbm, gb)
    load_cot = local(17, cot_hbm, x_all)
    load_x = local(18, x_hbm, x_all)
    load_n = [local(19 + i, normed_hbm.at[:, pl.ds(i * COLS, COLS)], gb.at[i]) for i in range(4)]
    load_g.start()
    for slot in range(12):
        load_forward(0, slot)
    load_cot.start()

    left_cot = [
        pltpu.make_async_copy(xt_hbm.at[1, c], xf.at[1, :, :, :, own_rows], w_sem.at[23]),
        send(xt_hbm.at[1, 1 - c], xf.at[1, :, :, :, far_rows], sem_ffn.at[0, 0], sem_ffn.at[1, 0], sibling),
    ]
    left_g = send(xs, xf.at[0, :, :, :, far_rows], sem_ffn.at[0, 1], sem_ffn.at[1, 1], sibling)

    def right_ffn(t):
        return send(yf.at[t, :, own_rows], yf.at[t, :, far_rows], sem_ffn.at[0, 2 + t], sem_ffn.at[1, 2 + t], sibling)

    left_att = [
        pltpu.make_async_copy(xt_hbm.at[0, c], xa.at[0, :, :, :, own_rows], w_sem.at[24]),
        send(xt_hbm.at[0, 1 - c], xa.at[0, :, :, :, far_rows], sem_att.at[0, 0], sem_att.at[1, 0], sibling),
    ]
    left_gb = send(xs, xa.at[1, :, :, :, far_rows], sem_att.at[0, 1], sem_att.at[1, 1], sibling)

    def right_att(t):
        return send(ya.at[t, own_rows], ya.at[t, far_rows], sem_att.at[0, 2 + t], sem_att.at[1, 2 + t], sibling)

    def by_owner(m, xd):
        for i in range(16):
            block = gb[i // 4, :, (i % 4) * 128 : (i % 4 + 1) * 128].T
            xd[m, i // 4, i % 4, :, 0:ROWS] = jnp.where(c == 0, block[:64], block[64:])
            xs[i // 4, i % 4] = jnp.where(c == 0, block[64:], block[:64])

    for copy in left_cot:
        copy.start()
    load_g.wait()
    by_owner(0, xf)
    left_g.start()

    def product(xd, right):
        def term(t, i, k, dest, first, last):
            m, yd = right(t, i)
            rows = xd[m, first:last, dest] if k == 0 else xd[m, dest, first:last]
            return mm(rows.reshape((last - first) * 64, 2 * ROWS), yd)

        return term

    def finish_ffn(t, i, k, value):
        stage[k, i] = value

    def write_ffn(t, k):
        return pltpu.make_async_copy(stage.at[k], out_ffn.at[:, t], sem_stage.at[k])

    def close_ffn(t):
        if t >= 2:
            write_ffn(t - 2, t % 2).wait()
        big.end(t, t % 2)
        write_ffn(t, t % 2).start()

    def finish_att(t, i, k, value):
        out_att[t] = value

    big = Ring(refs_big, 64, FFN_PARTS, product(xf, lambda t, i: (lax.div(i, 2), yf[t, i])), finish_ffn)
    mid = Ring(refs_mid, 64, 1, product(xa, lambda t, i: (t // 3, ya[t])), finish_att)

    def begin(u):
        right_ffn(u).wait()
        big.start(u, u % 2)

    def feed(u, carry):
        def through(first_slot, term):
            value = jnp.zeros((ROWS, COLS), F32)
            for i in range(4):
                slot = first_slot + i
                held(slot)
                value = value + term(i, slot)

                @pl.when(u < 3)
                def _():
                    load_forward(u + 1, slot)

                @pl.when(u == 3)
                def _():
                    load_later(slot)

            return value * scales[:, 1:2]

        gate = through(0, lambda i, slot: mm(gb[i], wb[slot]))
        up = through(4, lambda i, slot: mm(gb[i], wb[slot]))

        @pl.when(u == 0)
        def _():
            load_cot.wait()

        grad = through(8, lambda i, slot: mm_nt(x_all[:, i * COLS : (i + 1) * COLS], wb[slot]))
        sigmoid = jax.nn.sigmoid(gate)
        active = gate * sigmoid
        yf[u, 0, own_rows] = (grad * up * sigmoid * (1.0 + gate * (1.0 - sigmoid))).astype(BF16)
        yf[u, 1, own_rows] = (grad * active).astype(BF16)
        yf[u, 2, own_rows] = (active * up).astype(BF16)
        right_ffn(u).start()

        @pl.when(u == 1)
        def _():
            for copy in left_cot:
                copy.wait()
            left_g.wait()
            begin(0)

        @pl.when(u == 3)
        def _():
            begin(1)

        return carry

    lax.fori_loop(0, FFN_TILES, feed, 0)
    for copy in left_att:
        copy.start()
    inverse = 1.0 / scales[:, 1:2]
    gs_turns = to_mates(0, lambda i: gf_part.at[i], gs_came)
    dot = jnp.zeros((ROWS, 1), F32)
    for n in range(4):
        value = jnp.zeros((ROWS, COLS), F32)
        for b in range(8 * n, 8 * n + 8):
            held(b % 12)
            value = value + mm_nt(yf[b % 4, b % 8 // 4, 0:ROWS], wb[b % 12])
            load_later(b + 12)
        value = value * inverse
        dot = dot + jnp.sum(value * gb[turn_at(n)].astype(F32), axis=1, keepdims=True)
        if n < 3:
            gf_part[n] = value.astype(BF16)
            gs_turns[n].start()
        else:
            gsum[...] = value
    dot_part[...] = jnp.broadcast_to(dot, (ROWS, 128)).T[:8]
    gs_dots = to_mates(3, lambda i: dot_part, dot_came)
    for turn in gs_dots:
        turn.start()
    begin(2)

    for turn in gs_turns + gs_dots:
        turn.wait()
    total = gsum[...] + gs_came[0].astype(F32) + gs_came[1].astype(F32) + gs_came[2].astype(F32)
    gsum[...] = total
    gain_rows = jnp.sum(total * hidden_in[...] * scales[:, 1:2], axis=0, keepdims=True)
    gain_rows_ref[...] = jnp.concatenate([gain_rows[:, i * 128 : (i + 1) * 128] for i in range(4)])

    def mean_column(own):
        return ((own + dot_came[0] + dot_came[1] + dot_came[2]) * (1.0 / 2048)).T[:, 0:1]

    scale = scales[:, 1:2]
    residual = (
        columns(x_all, y).astype(F32)
        + scale * (gsum[...] * columns(gain_two, y))
        - hidden_in[...] * (scale * scale * scale * mean_column(dot_part[...]))
    )
    gres[...] = residual
    gb[y] = residual.astype(BF16)
    gb_turns = [
        send(gb.at[y], gb.at[y], y_sem.at[0, 6 + i], y_sem.at[1, 6 + i], y_mates[i]) for i in range(3)
    ]
    for turn in gb_turns:
        turn.start()
    load_x.start()

    ffn_turns = to_mates(9, lambda i: gf_part.at[i], ffn_came)
    for n in range(4):
        value = jnp.zeros((ROWS, COLS), F32)
        for b in range(32 + 4 * n, 36 + 4 * n):
            held(b % 12)
            value = value + mm(yf[b % 4, 2, 0:ROWS], wb[b % 12])
            load_later(b + 12)
        if n < 3:
            gf_part[n] = value.astype(BF16)
            ffn_turns[n].start()
        else:
            out_inputs[...] = value
    begin(3)
    write_mask(mask, lengths)
    def features(h, carry):
        pq[h] = soft_pair(qh[h], f_q[h])
        return carry

    lax.fori_loop(0, HEADS, features, 0)
    for j in range(KEY_HEADS):
        pkey[j] = soft_pair(kv[j][:, :DIM], f_k[j])
        pkey[KEY_HEADS + j] = jnp.zeros((SPAN, 128), F32)
    dkv[...] = jnp.zeros(dkv.shape, F32)
    pk[...] = jnp.zeros(pk.shape, F32)
    big.merge(0, 0)

    for i in range(3):
        here = gb.at[turned(y, 3 - i)]
        send(here, here, y_sem.at[0, 6 + i], y_sem.at[1, 6 + i], y_mates[i]).wait_recv()
    for slot in range(4):
        held(slot)
    grad_low = jnp.zeros((ROWS, 8), F32)
    grad_mixed = jnp.zeros((ROWS, COLS), F32)
    for k in range(4):
        cut = slice(k * COLS, (k + 1) * COLS)
        grad_low = grad_low + mm_nt(gb[k], b_out[:, cut])
        grad_mixed = grad_mixed + mm_nt(gb[k], wb[k])
    grad_mixed = grad_mixed + jnp.dot(
        grad_low, a_out[...].astype(F32), precision=HIGH, preferred_element_type=F32
    )
    rounded = grad_mixed.astype(BF16)
    for h in range(HEADS):
        gh[h] = rounded[:, h * DIM : (h + 1) * DIM]
    top, bottom = halves(grad_low)
    gao[...] = mm_tn(top, mixed[...]) + mm_tn(bottom, mixed[...])
    for k in range(4):
        gbo[:, k * COLS : (k + 1) * COLS] = mm_tn(low_mix[...], gb[k])

    lane = lax.broadcasted_iota(jnp.int32, (ROWS, DIM), 1)
    for h in range(HEADS):
        j = h // 4
        grad = gh[h].astype(F32)
        column = stat[h].T
        den = column[:, 1:2]
        inner = -jnp.sum(grad * att[:, h * DIM : (h + 1) * DIM], axis=1, keepdims=True) / den
        ext = jnp.concatenate([grad / den, jnp.where(lane == 0, inner, 0.0)], axis=1)
        dext[h] = ext
        top, bottom = halves(ext * column[:, 2:3])
        phi = pq[h].astype(BF16)
        piece = (mm_tn(top, phi) + mm_tn(bottom, phi))[:STATE]
        scan.own[0, j] = piece if h % 4 == 0 else scan.own[0, j] + piece
    scan.open()

    by_owner(1, xa)
    for turn in gb_turns:
        turn.wait_send()
    for load in load_n:
        load.start()
    left_gb.start()
    for t in (3, 4):
        ya[t, 0:ROWS] = mixed[:, (t - 3) * ATT_WIDTH : (t - 2) * ATT_WIDTH]
        right_att(t).start()
    scan.along_x()
    left_gb.wait()
    for t in (3, 4):
        right_att(t).wait()
        mid.start(t, t % 2)

    def backward(h, carry):
        j = lax.div(h, 4)
        keys, values = kv[j][:, :DIM], kv[j][:, DIM:]
        q, grad, ext = qh[h], gh[h], dext[h]
        column = stat[h].T
        top, den, gate = column[:, 0:1], column[:, 1:2], column[:, 2:3]
        distant = mask[...] == NEG
        soft = pq[h]
        phi, phi_key = soft.astype(BF16), pkey[j].astype(BF16)
        damping = jnp.where(distant, jnp.exp(-top), 0.0)
        weights = jnp.exp(mm_nt(q, keys) * (DIM**-0.5) + mask[...] - top)
        grad_weights = mm_nt(grad, values) / den + ext[:, DIM : DIM + 1]
        grad_scores = (weights * grad_weights).astype(BF16)
        grad_linear = (damping * grad_weights).astype(BF16)
        both = weights.astype(BF16).astype(F32) + mm_nt(phi, phi_key) * damping
        high, rest = halves(both / den)
        grad_q = mm(grad_scores, keys) * (DIM**-0.5)
        grad_k = mm_tn(grad_scores, q) * (DIM**-0.5)
        dkv[j] = dkv[j] + jnp.concatenate([grad_k, mm_tn(high, grad) + mm_tn(rest, grad)], axis=1)
        pkey[KEY_HEADS + j] = pkey[KEY_HEADS + j] + mm_tn(grad_linear, phi)
        carried = jnp.dot(
            (ext * gate)[:, :STATE], state[j], precision=HIGH, preferred_element_type=F32
        )
        grad_soft = mm(grad_linear, phi_key) + carried
        high, rest = halves(soft_back(soft, grad_soft))
        gh[h] = (grad_q + mm_nt(high, f_q[h]) + mm_nt(rest, f_q[h])).astype(BF16)
        gfq[h] = mm_tn(q, high) + mm_tn(q, rest)

        @pl.when(h == 1)
        def _():
            scan.along_z()

        @pl.when(h == 0)
        def _():
            big.merge(1, 1)

        @pl.when(h == 4)
        def _():
            big.merge(2, 0)

        @pl.when(h == 6)
        def _():
            big.cross(0, 0)

        @pl.when(h == 7)
        def _():
            big.merge(3, 1)

        return carry

    lax.fori_loop(0, HEADS, backward, 0)

    for j in range(KEY_HEADS):
        ret[j] = jnp.concatenate([dkv[j, :WINDOW], pkey[KEY_HEADS + j, :WINDOW]], axis=1)
    home = [
        send(ret, ret_came, ret_sem.at[0], ret_sem.at[1], leading),
        send(scan.own.at[0], next_state, ret_sem.at[2], ret_sem.at[3], leading),
    ]
    for copy in home:
        copy.start()
    gq = jnp.concatenate([gh[h] for h in range(HEADS)], axis=1)
    for i in range(2):
        ya[i, 0:ROWS] = gq[:, i * ATT_WIDTH : (i + 1) * ATT_WIDTH]
        right_att(i).start()
    down_ref[...] = down_rows(a_q, a_k, a_v)
    for slot in range(4, 8):
        held(slot)
    for slot in range(8, 12):
        held_pair(slot)
    for load in load_n + [load_x]:
        load.wait()
    glow[:, :8] = mm_nt(gq, b_q[...])
    for copy in left_att:
        copy.wait()
    for t in range(2):
        right_att(t).wait()
        mid.start(t, t % 2)
    for k in range(4):
        first[k] = mm_nt(gq, wb[4 + k])

    inside = middle(ROWS, 0, lengths)
    suffix = scan.close(scan.pair[...] * (1.0 - c.astype(F32)))
    for copy in home:
        copy.wait()
    joined = (s < 31).astype(F32)
    late_row = lax.broadcasted_iota(jnp.int32, (ROWS, 128), 0) >= ROWS - WINDOW
    for j in range(KEY_HEADS):
        soft = pkey[j, WINDOW:]
        phi = soft.astype(BF16)
        keys = kv[j, WINDOW:][:, :DIM]
        rows = value_columns(kv[j, WINDOW:])[:, :STATE]
        high, rest = halves(suffix[j])
        high_next, rest_next = halves(suffix[j] - joined * next_state[j])
        grad_phi = jnp.where(late_row, mm(rows, high_next) + mm(rows, rest_next), mm(rows, high) + mm(rows, rest))
        grad_phi = grad_phi * inside + pkey[KEY_HEADS + j, WINDOW:]
        grad_v = jnp.where(
            late_row[:, :STATE], mm_nt(phi, high_next) + mm_nt(phi, rest_next), mm_nt(phi, high) + mm_nt(phi, rest)
        )
        grad_v = (grad_v * inside)[:, :DIM]
        last = ROWS - WINDOW
        grad_phi = jnp.concatenate([grad_phi[:last], grad_phi[last:] + ret_came[j][:, 2 * DIM :]], axis=0)
        high, rest = halves(soft_back(soft, grad_phi))
        grad_k = mm_nt(high, f_k[j]) + mm_nt(rest, f_k[j])
        gfk[j] = mm_tn(keys, high) + mm_tn(keys, rest)
        dkv[j, WINDOW:] = dkv[j, WINDOW:] + jnp.concatenate([grad_k, grad_v], axis=1)
        dkv[j, ROWS:] = dkv[j, ROWS:] + ret_came[j][:, : 2 * DIM]
    gk = jnp.concatenate([dkv[j, WINDOW:][:, :DIM] for j in range(KEY_HEADS)], axis=1).astype(BF16)
    gv = jnp.concatenate([dkv[j, WINDOW:][:, DIM:] for j in range(KEY_HEADS)], axis=1).astype(BF16)
    gkv[...] = jnp.concatenate([gk, gv], axis=1)
    ya[2, 0:ROWS] = gkv[...]
    right_att(2).start()

    glow[:, 8:16] = mm_nt(gk, b_k[...])
    glow[:, 16:24] = mm_nt(gv, b_v[...])
    glow_high, glow_rest = halves(glow[...])
    for k in range(4):
        wide[:, k * COLS : (k + 1) * COLS] = mm_tn(glow_high, gb[k]) + mm_tn(glow_rest, gb[k])

    def place(d):
        return d // 16, d // 4 % 4, d % 4

    for i in range(16):
        cut = slice(i * 128, (i + 1) * 128)
        for half in range(2):
            d = place(2 * i + half)
            pk[*d, 0:12] = wide[12 * half : 12 * half + 12, cut]
            pk[*d, 13:16] = 0.25 * gbo[3 * half : 3 * half + 3, cut]
        pk[*place(26 + i // 8), 16 + 2 * (i % 8) : 18 + 2 * (i % 8)] = gbo[6:8, cut]

    def low_half(d, value):
        pk[*place(d), 16 : 16 + value.shape[0]] = value

    for i in range(4):
        pair = jnp.concatenate([gfq[2 * i], gfq[2 * i + 1]], axis=1)
        for part in range(4):
            low_half(4 * i + part, pair[16 * part : 16 * part + 16])
    pair = jnp.concatenate([gfk[0], gfk[1]], axis=1)
    for part in range(4):
        low_half(16 + part, pair[16 * part : 16 * part + 16])
    grad_b = jnp.concatenate(
        [mm_tn(low[:, :8], gq), mm_tn(low[:, 8:16], gkv[:, :128]), mm_tn(low[:, 16:24], gkv[:, 128:])], axis=1
    )
    for i in range(3):
        low_half(20 + i, jnp.concatenate([grad_b[:, 256 * i : 256 * i + 128], grad_b[:, 256 * i + 128 : 256 * i + 256]]))
    for i in range(2):
        low_half(23 + i, jnp.concatenate([gao[:, 256 * i : 256 * i + 128], gao[:, 256 * i + 128 : 256 * i + 256]]))
    low_half(25, gain_rows_ref[...])
    pack_far = send(pk.at[1 - c], pk.at[2], sem_pack.at[0], sem_pack.at[1], sibling)
    pack_far.start()

    for turn in ffn_turns:
        turn.wait()
    out_block[...] = (
        hidden_in[...]
        + out_inputs[...]
        + ffn_came[0].astype(F32)
        + ffn_came[1].astype(F32)
        + ffn_came[2].astype(F32)
    ).astype(BF16)
    gf_turns = to_mates(12, lambda i: gf_part.at[i], gs_came)

    def partial_first(d, dot):
        rows = pl.ds(pl.multiple_of(d * COLS, COLS), COLS)
        down = columns(down_ref, d)
        part = first[d] + mm_nt(gkv[...], wb[8 + d, :, 0:256]) + mm(glow_high, down) + mm(glow_rest, down)
        shaped = part * columns(x_all, d).astype(F32)
        gain_row[:, rows] = jnp.sum(shaped * scales[:, 0:1], axis=0, keepdims=True)
        return part, dot + jnp.sum(shaped * columns(gain_one, d), axis=1, keepdims=True)

    def spread(sems, base, piece, mates, back_piece):
        turns = [send(piece, piece, sems.at[0, base + i], sems.at[1, base + i], mate) for i, mate in enumerate(mates)]
        for turn in turns:
            turn.start()
        return [
            send(back_piece(i), back_piece(i), sems.at[0, base + i], sems.at[1, base + i], mate)
            for i, mate in enumerate(mates)
        ]

    def settle(turns):
        for turn in turns:
            turn.wait()

    dot = jnp.zeros((ROWS, 1), F32)
    for i in (1, 0):
        chunk, dot = partial_first(turned(y, 1 + i), dot)
        gf_part[i] = chunk.astype(BF16)
        gf_turns[i].start()

    pack_far.wait()
    x_turns = [send(px.at[i], px_came.at[i], sem_zx.at[0, i], sem_zx.at[1, i], scan.x_mates[i]) for i in range(3)]
    for i in range(3):
        dest = turned(x, 1 + i)
        px[i] = (pk[c, :, dest] + pk[2, :, dest]).astype(BF16)
        x_turns[i].start()
    chunk, dot = partial_first(turned(y, 3), dot)
    gf_part[2] = chunk.astype(BF16)
    gf_turns[2].start()
    chunk, dot = partial_first(y, dot)
    gsum[...] = chunk
    dot_part[...] = jnp.broadcast_to(dot, (ROWS, 128)).T[:8]
    dot_turns = to_mates(15, lambda i: dot_part, dot_came)
    for turn in dot_turns:
        turn.start()
    for i in range(16):
        gain_c[c, i : i + 1] = gain_row[:, i * 128 : (i + 1) * 128]
    gain_turns = spread(sem_gain, 0, gain_c.at[c], [sibling], lambda i: gain_c.at[1 - c])
    own_pack = pk[c, :, x] + pk[2, :, x]
    right_att(2).wait()
    mid.start(2, 0)
    settle(x_turns)
    own_pack = own_pack + px_came[0].astype(F32) + px_came[1].astype(F32) + px_came[2].astype(F32)
    pz[z] = own_pack.astype(BF16)
    z_turns = spread(sem_zx, 3, pz.at[z], scan.z_mates, lambda i: pz.at[turned(z, 3 - i)])
    settle(gain_turns)
    gain_x[x] = gain_c[0] + gain_c[1]
    gain_turns = spread(sem_gain, 1, gain_x.at[x], scan.x_mates, lambda i: gain_x.at[turned(x, 3 - i)])
    for t in (3, 4, 0, 1):
        mid.merge(t, t % 2)
    settle(z_turns)
    own_pack = pz[0].astype(F32) + pz[1].astype(F32) + pz[2].astype(F32) + pz[3].astype(F32)
    crown[y] = own_pack[:, :16]
    y_turns = spread(sem_zx, 10, crown.at[y], y_mates, lambda i: crown.at[turned(y, 3 - i)])
    settle(gain_turns)
    gain_z[z] = gain_x[0] + gain_x[1] + gain_x[2] + gain_x[3]
    gain_turns = spread(sem_gain, 4, gain_z.at[z], scan.z_mates, lambda i: gain_z.at[turned(z, 3 - i)])
    big.cross(1, 1)
    mid.merge(2, 0)
    settle(y_turns)
    top = crown[0] + crown[1] + crown[2] + crown[3]
    out_pack[c, :, x] = jnp.concatenate([top, own_pack[:, 16:]], axis=1).astype(BF16)
    x_turns = spread(sem_zx, 6, out_pack.at[c, :, x], scan.x_mates, lambda i: out_pack.at[c, :, turned(x, 3 - i)])
    settle(gain_turns)
    gain_y[y] = gain_z[0] + gain_z[1] + gain_z[2] + gain_z[3]
    gain_turns = spread(sem_gain, 7, gain_y.at[y], y_mates, lambda i: gain_y.at[turned(y, 3 - i)])
    big.cross(2, 0)
    for t in (3, 4, 0, 1, 2):
        mid.cross(t, t % 2)
    settle(gf_turns + dot_turns)
    total = gsum[...] + gs_came[0].astype(F32) + gs_came[1].astype(F32) + gs_came[2].astype(F32)
    scale = scales[:, 0:1]
    out_inputs[...] = (
        gres[...]
        + scale * (total * columns(gain_one, y))
        - columns(x_all, y).astype(F32) * (scale * scale * scale * mean_column(dot_part[...]))
    )
    settle(x_turns)
    last = spread(sem_zx, 9, out_pack.at[c], [sibling], lambda i: out_pack.at[1 - c])
    settle(gain_turns)
    out_gain[...] = gain_y[0] + gain_y[1] + gain_y[2] + gain_y[3]
    big.cross(3, 1)
    for t in range(FFN_TILES):
        big.merge_cross(t, t % 2)
    for t in (3, 4, 0, 1, 2):
        mid.merge_cross(t, t % 2)
    for t in range(FFN_TILES):
        close_ffn(t)
    for t in (3, 4, 0, 1, 2):
        mid.end(t, t % 2)
    settle(last)
    for i in range(2):
        write_ffn(FFN_TILES - 2 + i, i).wait()
    for t in range(FFN_TILES):
        big.drain(t, t % 2)
    for t in range(ATT_TILES):
        mid.drain(t, t % 2)


def late(args, weights):
    anywhere = pl.BlockSpec(memory_space=pl.ANY)
    vmem = pl.BlockSpec(memory_space=pltpu.VMEM)
    shapes = (
        ((ROWS, COLS), BF16),
        ((ROWS, COLS), F32),
        ((FFN_PARTS, FFN_TILES, 64, FFN_WIDTH), F32),
        ((ATT_TILES, 64, ATT_WIDTH), F32),
        ((2, 4, 4, PACK, 128), BF16),
        ((16, 128), F32),
    )
    block = (ROWS, COLS)
    return pl.pallas_call(
        late_kernel,
        out_shape=tuple(jax.ShapeDtypeStruct(*shape) for shape in shapes),
        in_specs=[vmem] * 22 + [pl.BlockSpec(memory_space=pltpu.SMEM)] + [anywhere] * 12,
        out_specs=(vmem, vmem, anywhere, vmem, vmem, vmem),
        scratch_shapes=[
            pltpu.VMEM((12, COLS, COLS), BF16),
            pltpu.VMEM((ROWS, 2048), BF16),
            pltpu.SemaphoreType.DMA((25,)),
            pltpu.VMEM((3, *block), BF16),
            pltpu.VMEM((3, *block), BF16),
            pltpu.VMEM((3, *block), BF16),
            pltpu.VMEM((8, ROWS), F32),
            pltpu.VMEM((3, 8, ROWS), F32),
            pltpu.VMEM((4, *block), BF16),
            pltpu.VMEM(block, F32),
            pltpu.VMEM(block, F32),
            pltpu.SemaphoreType.DMA((2, 18)),
            pltpu.VMEM((2, 4, 4, 64, 512), BF16),
            pltpu.VMEM((FFN_TILES, FFN_PARTS, 512, FFN_WIDTH), BF16),
            pltpu.VMEM((4, 4, 64, ROWS), BF16),
            pltpu.SemaphoreType.DMA((2, 2 + FFN_TILES)),
            pltpu.VMEM((2, 4, 4, 64, 512), BF16),
            pltpu.VMEM((ATT_TILES, 512, ATT_WIDTH), BF16),
            pltpu.SemaphoreType.DMA((2, 2 + ATT_TILES)),
            pltpu.VMEM((3, 4, 4, PACK, 128), F32),
            pltpu.SemaphoreType.DMA((2,)),
            pltpu.VMEM((ROWS, SPAN), F32),
            pltpu.VMEM((HEADS, ROWS, DIM), BF16),
            pltpu.VMEM((HEADS, ROWS, 128), F32),
            pltpu.VMEM((2 * KEY_HEADS, SPAN, 128), F32),
            pltpu.VMEM((HEADS, ROWS, 128), F32),
            pltpu.VMEM((KEY_HEADS, SPAN, 128), F32),
            pltpu.VMEM((HEADS, DIM, DIM), F32),
            pltpu.VMEM((KEY_HEADS, DIM, DIM), F32),
            pltpu.VMEM((KEY_HEADS, WINDOW, 256), F32),
            pltpu.VMEM((KEY_HEADS, WINDOW, 256), F32),
            pltpu.VMEM((KEY_HEADS, STATE, 128), F32),
            pltpu.SemaphoreType.DMA((4,)),
            pltpu.VMEM((ROWS, 24), F32),
            pltpu.VMEM((ROWS, 256), BF16),
            pltpu.VMEM((24, 2048), F32),
            pltpu.VMEM((8, COLS), F32),
            pltpu.VMEM((8, 2048), F32),
            pltpu.VMEM((24, 2048), BF16),
            pltpu.VMEM((4, *block), F32),
            pltpu.VMEM((1, 2048), F32),
            pltpu.VMEM((4, 128), F32),
            pltpu.VMEM((3, 4, PACK, 128), BF16),
            pltpu.VMEM((3, 4, PACK, 128), BF16),
            pltpu.VMEM((4, 4, PACK, 128), BF16),
            pltpu.VMEM((4, 4, 16, 128), F32),
            pltpu.SemaphoreType.DMA((2, 13)),
            pltpu.VMEM((2, FFN_PARTS, 64, FFN_WIDTH), F32),
            pltpu.SemaphoreType.DMA((2,)),
            pltpu.VMEM((2, 16, 128), F32),
            pltpu.VMEM((4, 16, 128), F32),
            pltpu.VMEM((4, 16, 128), F32),
            pltpu.VMEM((4, 16, 128), F32),
            pltpu.SemaphoreType.DMA((2, 10)),
            *Scan.scratch((KEY_HEADS, STATE, 128)),
            *Ring.scratch(FFN_TILES, FFN_PARTS, 64, FFN_WIDTH),
            *Ring.scratch(ATT_TILES, 1, 64, ATT_WIDTH),
        ],
        compiler_params=pltpu.CompilerParams(
            collective_id=2, has_side_effects=True, vmem_limit_bytes=63 * 2**20 + 2**19
        ),
        name="late",
    )(*args, *weights)


def finish_kernel(
    block, inputs, ffn_sums, att_sums, packed, gains,
    block_out, inputs_out, gain_one, w_q, a_q, b_q, w_k, a_k, b_k, w_v, a_v, b_v, f_q, f_k, w_o, a_o, b_o, gain_two,
    w_gate, w_up, w_down,
):
    block_out[...] = block[...]
    pack = packed[...].astype(F32)
    inputs_out[...] = inputs[...]
    for i in range(4):
        cut = slice(i * FFN_WIDTH, (i + 1) * FFN_WIDTH)
        w_gate[:, cut] = ffn_sums[0, i]
        w_up[:, cut] = ffn_sums[1, i]
        w_down[:, cut] = ffn_sums[2, i]
    for i in range(2):
        cut = slice(i * ATT_WIDTH, (i + 1) * ATT_WIDTH)
        w_q[:, cut] = att_sums[i]
        w_o[:, cut] = att_sums[3 + i]
    w_k[...] = att_sums[2, :, :128]
    w_v[...] = att_sums[2, :, 128:]
    for i in range(16):
        cut = slice(i * 128, (i + 1) * 128)
        rows = jnp.concatenate([pack[2 * i, :12], pack[2 * i + 1, :12]], axis=0)
        a_q[:, cut] = rows[:8]
        a_k[:, cut] = rows[8:16]
        a_v[:, cut] = rows[16:]
        last = 16 + 2 * (i % 8)
        b_o[:, cut] = jnp.concatenate(
            [pack[2 * i, 13:16], pack[2 * i + 1, 13:16], pack[26 + i // 8, last : last + 2]], axis=0
        )

    def tile(i):
        return pack[20 + i // 2, 16 + 8 * (i % 2) : 24 + 8 * (i % 2)]

    for i in range(4):
        cut = slice(i * 128, (i + 1) * 128)
        for part in range(4):
            rows = pack[4 * i + part, 16:]
            f_q[2 * i, 16 * part : 16 * part + 16] = rows[:, :DIM]
            f_q[2 * i + 1, 16 * part : 16 * part + 16] = rows[:, DIM:]
        rows = pack[16 + i, 16:]
        f_k[0, 16 * i : 16 * i + 16] = rows[:, :DIM]
        f_k[1, 16 * i : 16 * i + 16] = rows[:, DIM:]
        b_q[:, cut] = tile(i)
        a_o[:, cut] = tile(6 + i)
        gain_two[:, cut] = pack[25, 16 + i : 17 + i]
        gain_one[:, cut] = gains[pl.ds(4 * lax.axis_index("head") + i, 1), :]
    b_k[...] = tile(4)
    b_v[...] = tile(5)


def finish(block, inputs, ffn_sums, att_sums, pack, gains):
    vmem = pl.BlockSpec(memory_space=pltpu.VMEM)
    shapes = (
        (ROWS, COLS), (ROWS, COLS), (1, COLS), (64, COLS), (8, 2048), (8, COLS), (64, 128), (8, 2048), (8, 128),
        (64, 128), (8, 2048), (8, 128), (HEADS, DIM, DIM), (KEY_HEADS, DIM, DIM), (64, COLS), (8, COLS), (8, 2048),
        (1, COLS), (64, 2048), (64, 2048), (64, 2048),
    )
    outs = pl.pallas_call(
        finish_kernel,
        out_shape=tuple(jax.ShapeDtypeStruct(shape, F32 if i else BF16) for i, shape in enumerate(shapes)),
        in_specs=[vmem] * 6,
        out_specs=(vmem,) * len(shapes),
        compiler_params=pltpu.CompilerParams(vmem_limit_bytes=32 * 2**20),
        name="finish",
    )(block, inputs, ffn_sums, att_sums, pack.reshape(32, 32, 128), gains)
    return tuple(
        out[0] if i in (2, 17) else out.T if i in (4, 7, 10, 14, 15, 20) else out for i, out in enumerate(outs)
    )


def body(
    inputs,
    gain_first,
    w_query,
    a_query,
    b_query,
    key_projection_weight,
    a_key,
    key_adapter_second,
    value_projection_weight,
    a_value,
    value_adapter_second,
    feature_query,
    key_hedgehog_map,
    w_out,
    a_out,
    b_out,
    gain_second,
    w_gate,
    w_up,
    w_down,
    lengths,
    cotangent,
):
    gain_one, gain_two = gain_first[None], gain_second[None]
    a_in = (a_query.T, a_key.T, a_value.T)
    a_out = a_out.T
    projections = (w_query, key_projection_weight, value_projection_weight, w_out)
    normed, low, queries, kv, state, att, stat, mixed, low_mix, hidden_in, g, scales, xt = front(
        inputs, gain_one, gain_two, *a_in, b_query, key_adapter_second, value_adapter_second,
        feature_query, key_hedgehog_map, a_out, b_out, lengths, *projections, cotangent,
    )
    block_out, grad_inputs, out_ffn, out_att, out_pack, out_gain = late(
        (
            hidden_in, scales, gain_one, gain_two, mixed, low_mix, att, stat, state, queries, kv, low,
            feature_query, key_hedgehog_map, *a_in, a_out, b_out, b_query, key_adapter_second,
            value_adapter_second, lengths,
        ),
        (g, normed, inputs, cotangent, xt, *projections, w_gate, w_up, w_down),
    )
    return finish(block_out, grad_inputs, out_ffn, out_att, out_pack, out_gain)


def solution(mesh):
    return jax.shard_map(
        body,
        mesh=mesh,
        in_specs=(
            P("seq", None),
            P(),
            P(None, "head"),
            P(),
            P(None, "head"),
            P(None, "head"),
            P(),
            P(None, "head"),
            P(None, "head"),
            P(),
            P(None, "head"),
            P("head", None, None),
            P("head", None, None),
            P("head", None),
            P("head", None),
            P(),
            P(),
            P(None, "head"),
            P(None, "head"),
            P("head", None),
            P(),
            P("seq", None),
        ),
        out_specs=(
            P("seq", "head"),
            P("seq", "head"),
            P("head"),
            P("seq", "head"),
            P(),
            P(None, "head"),
            P("seq", "head"),
            P(),
            P(None, "head"),
            P("seq", "head"),
            P(),
            P(None, "head"),
            P("head", None, None),
            P("head", None, None),
            P("head", "seq"),
            P("head", None),
            P(),
            P("head"),
            P("seq", "head"),
            P("seq", "head"),
            P("head", "seq"),
        ),
        check_vma=False,
    )
```

```python
import jax
import jax.numpy as jnp
from jax import lax
from jax.experimental import pallas as pl
from jax.experimental.pallas import tpu as pltpu
from jax.sharding import PartitionSpec as P

MESH = pl.DeviceIdType.MESH
F32 = jnp.float32
BF16 = jnp.bfloat16


def spot():
    s = lax.axis_index("seq")
    y = lax.axis_index("head")
    return lax.div(s, 8), lax.rem(lax.div(s, 2), 4), lax.rem(s, 2), y


def at(z, x, c, y):
    return ((z * 4 + x) * 2 + c, y)


def turned(p, steps):
    return lax.rem(p + steps, 4)


def greet(partners):
    barrier = pltpu.get_barrier_semaphore()
    for partner in partners:
        pl.semaphore_signal(barrier, inc=1, device_id=partner, device_id_type=MESH)


def greeted(partners):
    pl.semaphore_wait(pltpu.get_barrier_semaphore(), len(partners))


def send(src, dst, ss, rs, device):
    return pltpu.make_async_remote_copy(
        src_ref=src, dst_ref=dst, send_sem=ss, recv_sem=rs, device_id=device, device_id_type=MESH
    )


def took(ref, sem):
    pltpu.make_async_copy(ref, ref, sem).wait()


class Ring:
    def __init__(self, refs, rows, pieces, term, finish):
        self.sb, self.ra, self.rf, self.ra3, self.rf3, self.ss, self.rs = refs
        self.rows, self.pieces, self.term, self.finish = rows, pieces, term, finish
        z, x, c, y = spot()
        self.axes = (
            (x, at(z, turned(x, 1), c, y), at(z, turned(x, 3), c, y)),
            (z, at(turned(z, 1), x, c, y), at(turned(z, 3), x, c, y)),
        )

    @staticmethod
    def scratch(count, pieces, rows, width):
        return [
            pltpu.VMEM((count, 2, pieces, 4 * rows, width), BF16),
            pltpu.VMEM((count, 2, pieces, 2 * rows, width), BF16),
            pltpu.VMEM((count, 2, pieces, 4 * rows, width), BF16),
            pltpu.VMEM((count, 2, pieces, rows // 2, width), BF16),
            pltpu.VMEM((count, 2, pieces, rows, width), BF16),
            pltpu.SemaphoreType.DMA((count, 4)),
            pltpu.SemaphoreType.DMA((count, 6)),
        ]

    def each(self, step):
        if self.pieces == 1:
            step(0)
        else:

            def one(p, carry):
                step(p)
                return carry

            lax.fori_loop(0, self.pieces, one, 0)

    def block(self, b, part):
        g = self.rows // 2
        if part is None:
            return pl.ds(pl.multiple_of(b * self.rows, self.rows), self.rows)
        return pl.ds(pl.multiple_of(b * self.rows + part * g, g), g)

    def copy(self, t, k, i):
        p, ahead, behind = self.axes[k]
        q, ahead3, behind3 = self.axes[1 - k]
        h, g = 2 * self.rows, self.rows // 2
        lo, hi, lo3, hi3 = pl.ds(0, h), pl.ds(h, h), pl.ds(0, g), pl.ds(g, g)
        sb, ra, rf, ra3, rf3, block = self.sb, self.ra, self.rf, self.ra3, self.rf3, self.block
        src, dst, device = (
            lambda: (sb.at[t, 0, :, lo], ra.at[t, 0], ahead),
            lambda: (sb.at[t, 0, :, hi], ra.at[t, 1], behind),
            lambda: (sb.at[t, 1, :, hi], rf.at[t, 0, :, hi], ahead),
            lambda: (sb.at[t, 1, :, lo], rf.at[t, 1, :, lo], behind),
            lambda: (ra.at[t, 0], rf.at[t, 0, :, lo], ahead),
            lambda: (ra.at[t, 1], rf.at[t, 1, :, hi], behind),
            lambda: (sb.at[t, 0, :, block(turned(q, 2), 0)], ra3.at[t, 0], ahead3),
            lambda: (sb.at[t, 0, :, block(turned(q, 2), 1)], ra3.at[t, 1], behind3),
            lambda: (sb.at[t, 0, :, block(turned(q, 1), 1)], rf3.at[t, 0, :, hi3], ahead3),
            lambda: (sb.at[t, 0, :, block(turned(q, 3), 0)], rf3.at[t, 1, :, lo3], behind3),
            lambda: (ra3.at[t, 0], rf3.at[t, 0, :, lo3], ahead3),
            lambda: (ra3.at[t, 1], rf3.at[t, 1, :, hi3], behind3),
        )[i]()
        here = (0, 0, 0, 0, 1, 1, 2, 2, 2, 2, 3, 3)[i]
        there = (0, 1, 2, 2, 2, 2, 3, 4, 5, 5, 5, 5)[i]
        return send(src, dst, self.ss.at[t, here], self.rs.at[t, there], device)

    def sent(self, t, group):
        took((self.sb, self.ra, self.rf3, self.ra3)[group].at[t], self.ss.at[t, group])

    def arrived(self, t, group):
        ref = (self.ra.at[t, 0], self.ra.at[t, 1], self.rf.at[t], self.ra3.at[t, 0], self.ra3.at[t, 1], self.rf3.at[t])
        took(ref[group], self.rs.at[t, group])

    def start(self, t, k):
        p = self.axes[k][0]
        h = 2 * self.rows
        pieces = ((turned(p, 2), 0, 4), (turned(p, 3), 0, 2), (turned(p, 1), 2, 4))

        def one(i):
            value = self.term(t, i, k, *pieces).astype(BF16)
            self.sb[t, 0, i] = value[: 2 * h]
            self.sb[t, 1, i] = value[2 * h :]

        self.each(one)
        for i in range(4):
            self.copy(t, k, i).start()

    def merge(self, t, k):
        p = self.axes[k][0]
        h = 2 * self.rows
        for way in range(2):
            self.arrived(t, way)

        def one(i):
            mine = self.term(t, i, k, (turned(p, 1), 0, 2), (turned(p, 3), 2, 4))
            for way in range(2):
                part = mine[way * h : (way + 1) * h]
                self.ra[t, way, i] = (part + self.ra[t, way, i].astype(F32)).astype(BF16)

        self.each(one)
        for way in range(2):
            self.copy(t, k, 4 + way).start()

    def cross(self, t, k):
        p = self.axes[k][0]
        self.sent(t, 0)
        self.arrived(t, 2)

        def one(i):
            own = self.term(t, i, k, (p, 0, 4))
            self.sb[t, 0, i] = (own + self.rf[t, 0, i].astype(F32) + self.rf[t, 1, i].astype(F32)).astype(BF16)

        self.each(one)
        for i in (6, 7, 8, 9):
            self.copy(t, k, i).start()

    def merge_cross(self, t, k):
        q = self.axes[1 - k][0]
        for way, dest in ((0, turned(q, 1)), (1, turned(q, 3))):
            self.arrived(t, 3 + way)

            def one(i):
                mine = self.sb[t, 0, i, self.block(dest, way), :]
                self.ra3[t, way, i] = (mine.astype(F32) + self.ra3[t, way, i].astype(F32)).astype(BF16)

            self.each(one)
            self.copy(t, k, 10 + way).start()

    def end(self, t, k):
        q = self.axes[1 - k][0]
        self.arrived(t, 5)

        def one(i):
            mine = self.sb[t, 0, i, self.block(q, None), :].astype(F32)
            self.finish(t, i, k, mine + self.rf3[t, 0, i].astype(F32) + self.rf3[t, 1, i].astype(F32))

        self.each(one)

    def drain(self, t, k):
        for group in (1, 2, 3):
            self.sent(t, group)


LO, HI = pl.ds(0, 128), pl.ds(128, 128)


class Line:
    def __init__(self, part, came, sems, base):
        z, x, c, y = spot()
        ahead, behind = at(z, x, c, turned(y, 1)), at(z, x, c, turned(y, 3))
        self.part, self.came = part, came
        ways = (
            (part.at[1, LO], came.at[2, LO], ahead),
            (part.at[1, HI], came.at[2, HI], behind),
            (part.at[0, HI], came.at[0, HI], ahead),
            (part.at[2, LO], came.at[1, LO], behind),
            (came.at[2, LO], came.at[0, LO], ahead),
            (came.at[2, HI], came.at[1, HI], behind),
        )
        self.copies = [send(src, dst, sems.at[0, base + i], sems.at[1, base + i], to) for i, (src, dst, to) in enumerate(ways)]

    def start(self, *which):
        for i in which:
            self.copies[i].start()

    def merge(self):
        for i, piece, rows in ((0, 0, LO), (1, 2, HI)):
            self.copies[i].wait_recv()
            self.came[2, rows] = (self.came[2, rows].astype(F32) + self.part[piece, rows].astype(F32)).astype(BF16)
            self.copies[4 + i].start()

    def total(self, own):
        for copy in self.copies[2:]:
            copy.wait_recv()
        for copy in self.copies:
            copy.wait_send()
        return own + self.came[0].astype(F32) + self.came[1].astype(F32)


class Share:
    def __init__(self, ref, sems, base):
        z, x, c, y = spot()
        ahead, behind = at(z, x, c, turned(y, 1)), at(z, x, c, turned(y, 3))
        next_y, last_y, far_y = turned(y, 1), turned(y, 3), turned(y, 2)
        out = (
            (ref.at[y, LO], ahead),
            (ref.at[y, HI], behind),
            (ref.at[y, HI], ahead),
            (ref.at[y, LO], behind),
            (ref.at[last_y, LO], ahead),
            (ref.at[next_y, HI], behind),
        )
        into = (
            ref.at[last_y, LO],
            ref.at[next_y, HI],
            ref.at[last_y, HI],
            ref.at[next_y, LO],
            ref.at[far_y, LO],
            ref.at[far_y, HI],
        )
        self.copies = [send(src, src, sems.at[0, base + i], sems.at[1, base + i], to) for i, (src, to) in enumerate(out)]
        self.arrivals = [send(dst, dst, sems.at[0, base + i], sems.at[1, base + i], ahead) for i, dst in enumerate(into)]

    def start(self):
        for copy in self.copies[:4]:
            copy.start()

    def pass_on(self):
        for i in range(2):
            self.arrivals[i].wait_recv()
            self.copies[4 + i].start()

    def finish(self):
        for arrival in self.arrivals[2:]:
            arrival.wait_recv()
        for copy in self.copies:
            copy.wait_send()


FFN_TILES, FFN_PARTS, FFN_WIDTH, FFN_HALF = 4, 3, 512, 256
ATT_TILES, ATT_WIDTH = 5, 256
PACK = 32


EPS = 1e-05
NEG = -1e30
HIGH = lax.Precision.HIGHEST
ROWS = 256
WINDOW = 64
SPAN = ROWS + WINDOW
COLS = 512
HEADS, KEY_HEADS, DIM = 8, 2, 64
STATE = 72


def mm(a, b):
    return jnp.dot(a, b, preferred_element_type=F32)


def mm_nt(a, b, precision=None):
    return lax.dot_general(a, b, (((1,), (1,)), ((), ())), precision=precision, preferred_element_type=F32)


def mm_tn(a, b, precision=None):
    return lax.dot_general(a, b, (((0,), (0,)), ((), ())), precision=precision, preferred_element_type=F32)


def halves(value):
    top = value.astype(BF16)
    return top, (value - top.astype(F32)).astype(BF16)


def down_rows(a_q, a_k, a_v):
    return jnp.concatenate([a[...].astype(F32) for a in (a_q, a_k, a_v)], axis=0).astype(BF16)


def soft_pair(rows, table):
    both = mm(rows, jnp.concatenate([table, -table], axis=1))
    left = lax.broadcasted_iota(jnp.int32, both.shape, 1) < DIM
    upper = jnp.max(jnp.where(left, both, NEG), axis=1, keepdims=True)
    lower = jnp.max(jnp.where(left, NEG, both), axis=1, keepdims=True)
    grown = jnp.exp(both - jnp.where(left, upper, lower))
    sum_left = jnp.sum(jnp.where(left, grown, 0.0), axis=1, keepdims=True)
    sum_right = jnp.sum(jnp.where(left, 0.0, grown), axis=1, keepdims=True)
    return grown * jnp.where(left, 1.0 / sum_left, 1.0 / sum_right)


def doc_at(positions, lengths):
    first = lengths[0]
    second = first + lengths[1]
    return (
        (positions >= 0).astype(jnp.int32)
        + (positions >= first).astype(jnp.int32)
        + (positions >= second).astype(jnp.int32)
    )


def write_mask(mask, lengths):
    base = lax.axis_index("seq") * ROWS
    row = lax.broadcasted_iota(jnp.int32, (ROWS, SPAN), 0) + base
    column = lax.broadcasted_iota(jnp.int32, (ROWS, SPAN), 1) + base - WINDOW
    same = doc_at(row, lengths) == doc_at(column, lengths)
    offset = row - column
    here = jnp.where(offset < WINDOW, 0.0, NEG)
    mask[...] = jnp.where(same & (offset >= 0), here, 2.0 * NEG)


def middle(count, first, lengths):
    base = lax.axis_index("seq") * ROWS + first
    position = lax.broadcasted_iota(jnp.int32, (count, 1), 0) + base
    return (doc_at(position, lengths) == 2).astype(F32)


def value_columns(kv):
    lane = lax.broadcasted_iota(jnp.int32, kv.shape, 1)
    v = jnp.concatenate([kv[:, DIM:], kv[:, :DIM]], axis=1)
    return jnp.where(lane < DIM, v, jnp.where(lane == DIM, 1.0, 0.0).astype(kv.dtype))


class Scan:
    def __init__(self, refs, reverse):
        self.own, self.pair, self.line, self.plane, self.sem = refs
        self.reverse = reverse
        z, x, c, y = spot()
        self.z, self.x, self.c = z, x, c
        self.sibling = at(z, x, 1 - c, y)
        self.x_mates = [at(z, turned(x, i), c, y) for i in (1, 2, 3)]
        self.z_mates = [at(turned(z, i), x, c, y) for i in (1, 2, 3)]

    @staticmethod
    def scratch(shape):
        return [
            pltpu.VMEM((3, *shape), F32),
            pltpu.VMEM(shape, F32),
            pltpu.VMEM((3, *shape), F32),
            pltpu.VMEM((3, *shape), F32),
            pltpu.SemaphoreType.DMA((2, 7)),
        ]

    def pair_copy(self):
        return send(self.own.at[0], self.pair, self.sem.at[0, 0], self.sem.at[1, 0], self.sibling)

    def line_copy(self, i):
        return send(self.own.at[1], self.line.at[i], self.sem.at[0, 1 + i], self.sem.at[1, 1 + i], self.x_mates[i])

    def plane_copy(self, i):
        return send(self.own.at[2], self.plane.at[i], self.sem.at[0, 4 + i], self.sem.at[1, 4 + i], self.z_mates[i])

    def counts(self, me, other):
        return ((other > me) if self.reverse else (other < me)).astype(F32)

    def open(self):
        self.pair_copy().start()

    def along_x(self):
        self.pair_copy().wait()
        self.own[1] = self.own[0] + self.pair[...]
        for i in range(3):
            self.line_copy(i).start()

    def along_z(self):
        for i in range(3):
            self.line_copy(i).wait()
        self.own[2] = self.own[1] + self.line[0] + self.line[1] + self.line[2]
        for i in range(3):
            self.plane_copy(i).start()

    def close(self, total):
        for i in range(3):
            self.plane_copy(i).wait()
        for i in range(3):
            total = total + self.line[i] * self.counts(self.x, turned(self.x, 3 - i))
        for i in range(3):
            total = total + self.plane[i] * self.counts(self.z, turned(self.z, 3 - i))
        return total


def front_kernel(
    x_ref, gain_one, gain_two, a_q, a_k, a_v, b_q, b_k, b_v, f_q, f_k, a_out, b_out, lengths, w_q, w_k, w_v, w_o, cot_hbm,
    normed_out, low_out, qh, kv_out, state_out, att_out, stat_out, mixed_out, lowmix_out, hidden_out, g_out, scales_out, xt_out,
    wq, wk, wv, wo, cot, w_sem, phq, phk, num, mask, q_rows, stat, brief, tail_sem,
    part, came, y_sem, low_part, square, square_came,
    *scan_refs,
):
    z, x, c, y = spot()
    s = lax.axis_index("seq")
    following, leading = (lax.rem(s + 1, 32), y), (lax.rem(s + 31, 32), y)
    y_mates = [at(z, x, c, turned(y, i)) for i in (1, 2, 3)]
    scan = Scan(scan_refs, False)
    partners = [following, leading, scan.sibling] + scan.x_mates + scan.z_mates + y_mates
    greet(partners)
    loads = [
        pltpu.make_async_copy(src, dst, w_sem.at[i])
        for i, (src, dst) in enumerate(((w_q, wq), (w_k, wk), (w_v, wv), (w_o, wo), (cot_hbm, cot)))
    ]
    for load in loads:
        load.start()
    for i in range(4):
        rows = pl.ds(64 * i, 64)
        value = x_ref[rows, :].astype(F32)
        scale = lax.rsqrt(jnp.mean(value * value, axis=1, keepdims=True) + EPS)
        scales_out[rows, 0:1] = scale
        normed_out[rows, :] = (value * scale * gain_one[...]).astype(BF16)
    write_mask(mask, lengths)
    low_out[...] = mm_nt(normed_out[...], down_rows(a_q, a_k, a_v)).astype(BF16)
    low = low_out[...]
    loads[1].wait()
    loads[2].wait()
    k = (mm(normed_out[...], wk[...]) + mm(low[:, 8:16], b_k[...])).astype(BF16)
    v = (mm(normed_out[...], wv[...]) + mm(low[:, 16:24], b_v[...])).astype(BF16)
    for j in range(KEY_HEADS):
        cut = slice(j * DIM, (j + 1) * DIM)
        kv_out[j, WINDOW:] = jnp.concatenate([k[:, cut], v[:, cut]], axis=1)
    tail = send(
        kv_out.at[:, pl.ds(ROWS, WINDOW)], kv_out.at[:, pl.ds(0, WINDOW)], tail_sem.at[0], tail_sem.at[1], following
    )
    greeted(partners)
    tail.start()
    loads[0].wait()
    for i in range(2):
        cut = slice(i * 256, (i + 1) * 256)
        q_rows[:, cut] = (mm(normed_out[...], wq[:, cut]) + mm(low[:, :8], b_q[:, cut])).astype(BF16)
    for h in range(HEADS):
        qh[h] = q_rows[:, h * DIM : (h + 1) * DIM]
    inside = middle(ROWS, 0, lengths)
    for j in range(KEY_HEADS):
        phk[j, WINDOW:] = soft_pair(kv_out[j, WINDOW:][:, :DIM], f_k[j]).astype(BF16)
        counted = (phk[j, WINDOW:].astype(F32) * inside).astype(BF16)
        rows = value_columns(kv_out[j, WINDOW:])
        settled = mm_tn(rows[: ROWS - WINDOW], counted[: ROWS - WINDOW])[:STATE]
        brief[0, j] = settled
        scan.own[0, j] = settled + mm_tn(rows[ROWS - WINDOW :], counted[ROWS - WINDOW :])[:STATE]
    brief_turn = send(brief.at[0], brief.at[1], tail_sem.at[2], tail_sem.at[3], scan.sibling)
    brief_turn.start()
    scan.open()

    def features(h, carry):
        phq[h] = soft_pair(qh[h], f_q[h]).astype(BF16)
        return carry

    lax.fori_loop(0, 4, features, 0)
    scan.along_x()
    lax.fori_loop(4, HEADS, features, 0)
    tail.wait()
    inside = middle(WINDOW, -WINDOW, lengths)
    for j in range(KEY_HEADS):
        phk[j, :WINDOW] = soft_pair(kv_out[j, :WINDOW][:, :DIM], f_k[j]).astype(BF16)
        counted = (phk[j, :WINDOW].astype(F32) * inside).astype(BF16)
        brief[2, j] = mm_tn(value_columns(kv_out[j, :WINDOW]), counted)[:STATE]
    brief_turn.wait()

    def inner(h, carry):
        j = lax.div(h, 4)
        kv = kv_out[j]
        distant = mask[...] == NEG
        scores = mm_nt(qh[h], kv[:, :DIM]) * (DIM**-0.5) + mask[...]
        top = jnp.max(scores, axis=1, keepdims=True)
        weights = jnp.exp(scores - top)
        total = weights + jnp.where(distant, mm_nt(phq[h], phk[j]) * jnp.exp(-top), 0.0)
        high = total.astype(BF16)
        rest = jnp.where(distant, total - high.astype(F32), 0.0).astype(BF16)
        v = kv[:, DIM:]
        num[h] = mm(high, v) + mm(rest, v)
        stat[h, :, 0:1] = top
        stat[h, :, 1:2] = jnp.sum(total, axis=1, keepdims=True)
        return carry

    lax.fori_loop(0, 4, inner, 0)
    scan.along_z()
    lax.fori_loop(4, HEADS, inner, 0)
    second = c.astype(F32)
    state_out[...] = scan.close(brief[1] * second - brief[2] * (1.0 - second))
    mine = middle(ROWS, 0, lengths)
    for h in range(HEADS):
        top, rest = halves(state_out[h // 4])
        carried = mm_nt(phq[h], top) + mm_nt(phq[h], rest)
        gate = jnp.exp(-stat[h, :, 0:1]) * mine
        total = stat[h, :, 1:2] + gate * carried[:, DIM : DIM + 1]
        stat[h, :, 1:2] = total
        stat[h, :, 2:3] = gate
        cut = slice(h * DIM, (h + 1) * DIM)
        attended = (num[h] + gate * carried[:, :DIM]) * (1.0 / total)
        att_out[:, cut] = attended
        mixed_out[:, cut] = attended.astype(BF16)
        stat_out[h] = stat[h].T
    mixed = mixed_out[...]
    low_part[y] = mm_nt(a_out[...], mixed)
    low_turns = [send(low_part.at[y], low_part.at[y], y_sem.at[0, i], y_sem.at[1, i], y_mates[i]) for i in range(3)]
    for turn in low_turns:
        turn.start()
    loads[3].wait()

    def columns(ref, d):
        return ref[:, pl.ds(pl.multiple_of(d * COLS, COLS), COLS)]

    line = Line(part, came, y_sem, 3)
    for i, which in ((1, (0, 1)), (0, (2,)), (2, (3,))):
        part[i] = mm(mixed, columns(wo, turned(y, 1 + i))).astype(BF16)
        line.start(*which)
    value = mm(mixed, columns(wo, y)) + columns(x_ref, y).astype(F32)

    def by_owner(m, rows):
        for i in range(16):
            flat = rows[:, i * 128 : (i + 1) * 128].T
            xt_out[m, 0, i // 4, i % 4] = flat[:64]
            xt_out[m, 1, i // 4, i % 4] = flat[64:]

    by_owner(0, normed_out)
    for i in range(3):
        here = low_part.at[turned(y, 3 - i)]
        send(here, here, y_sem.at[0, i], y_sem.at[1, i], y_mates[i]).wait()
    low_sum = low_part[0] + low_part[1] + low_part[2] + low_part[3]
    lowmix_out[...] = low_sum.T.astype(BF16)
    value = value + mm(lowmix_out[...], columns(b_out, y))
    line.merge()
    loads[4].wait()
    by_owner(1, cot)
    value = line.total(value)
    hidden_out[...] = value
    g_out[y] = (value * columns(gain_two, y)).astype(BF16)
    share = Share(g_out, y_sem, 12)
    square[...] = mm_nt(jnp.ones((8, COLS), F32), value * value, HIGH)
    square_turns = [
        send(square, square_came.at[i], y_sem.at[0, 9 + i], y_sem.at[1, 9 + i], y_mates[i]) for i in range(3)
    ]
    for turn in square_turns:
        turn.start()
    share.start()
    for turn in square_turns:
        turn.wait()
    mean = (square[...] + square_came[0] + square_came[1] + square_came[2]) * (1.0 / 2048)
    scales_out[:, 1:2] = lax.rsqrt(mean + EPS).T[:, 0:1]
    share.pass_on()
    share.finish()


def front(*args):
    anywhere = pl.BlockSpec(memory_space=pl.ANY)
    vmem = pl.BlockSpec(memory_space=pltpu.VMEM)
    shapes = (
        ((ROWS, 2048), BF16),
        ((ROWS, 24), BF16),
        ((HEADS, ROWS, DIM), BF16),
        ((KEY_HEADS, SPAN, 128), BF16),
        ((KEY_HEADS, STATE, 128), F32),
        ((ROWS, 512), F32),
        ((HEADS, 8, ROWS), F32),
        ((ROWS, 512), BF16),
        ((ROWS, 8), BF16),
        ((ROWS, COLS), F32),
        ((4, ROWS, COLS), BF16),
        ((ROWS, 2), F32),
        ((2, 2, 4, 4, 64, ROWS), BF16),
    )
    return pl.pallas_call(
        front_kernel,
        out_shape=tuple(jax.ShapeDtypeStruct(*shape) for shape in shapes),
        in_specs=[vmem] * 13 + [pl.BlockSpec(memory_space=pltpu.SMEM)] + [anywhere] * 5,
        out_specs=(vmem,) * len(shapes),
        scratch_shapes=[
            pltpu.VMEM((2048, 512), BF16),
            pltpu.VMEM((2048, 128), BF16),
            pltpu.VMEM((2048, 128), BF16),
            pltpu.VMEM((512, 2048), BF16),
            pltpu.VMEM((ROWS, 2048), BF16),
            pltpu.SemaphoreType.DMA((5,)),
            pltpu.VMEM((HEADS, ROWS, 128), BF16),
            pltpu.VMEM((KEY_HEADS, SPAN, 128), BF16),
            pltpu.VMEM((HEADS, ROWS, DIM), F32),
            pltpu.VMEM((ROWS, SPAN), F32),
            pltpu.VMEM((ROWS, 512), BF16),
            pltpu.VMEM((HEADS, ROWS, 8), F32),
            pltpu.VMEM((3, KEY_HEADS, STATE, 128), F32),
            pltpu.SemaphoreType.DMA((4,)),
            pltpu.VMEM((3, ROWS, COLS), BF16),
            pltpu.VMEM((3, ROWS, COLS), BF16),
            pltpu.SemaphoreType.DMA((2, 18)),
            pltpu.VMEM((4, 8, ROWS), F32),
            pltpu.VMEM((8, ROWS), F32),
            pltpu.VMEM((3, 8, ROWS), F32),
            *Scan.scratch((KEY_HEADS, STATE, 128)),
        ],
        compiler_params=pltpu.CompilerParams(
            collective_id=1, has_side_effects=True, vmem_limit_bytes=60 * 2**20
        ),
        name="front",
    )(*args)


def soft_back(soft, grad):
    left = lax.broadcasted_iota(jnp.int32, soft.shape, 1) < DIM
    part = soft * grad
    sum_left = jnp.sum(jnp.where(left, part, 0.0), axis=1, keepdims=True)
    sum_right = jnp.sum(jnp.where(left, 0.0, part), axis=1, keepdims=True)
    both = part - soft * jnp.where(left, sum_left, sum_right)
    return both[:, :DIM] - both[:, DIM:]


def late_kernel(
    hidden_in, scales, gain_one, gain_two, mixed, low_mix, att, stat, state, qh, kv, low,
    f_q, f_k, a_q, a_k, a_v, a_out, b_out, b_q, b_k, b_v, lengths,
    g_hbm, normed_hbm, x_hbm, cot_hbm, xt_hbm, w_q, w_k, w_v, w_o, w_gate, w_up, w_down,
    out_block, out_inputs, out_ffn, out_att, out_pack, out_gain,
    wb, x_all, w_sem,
    gs_came, ffn_came, gf_part, dot_part, dot_came, gb, gres, gsum, y_sem,
    xf, yf, xs, sem_ffn, xa, ya, sem_att, pk, sem_pack,
    mask, gh, pq, pkey, dext, dkv, gfq, gfk, ret, ret_came, next_state, ret_sem, glow, gkv, wide, gao, gbo, down_ref,
    first, gain_row, gain_rows_ref, px, px_came, pz, crown, sem_zx, stage, sem_stage, gain_c, gain_x, gain_z, gain_y, sem_gain,
    *rest,
):
    scan = Scan(rest[0:5], True)
    refs_big, refs_mid = rest[5:12], rest[12:19]
    z, x, c, y = spot()
    s = lax.axis_index("seq")
    following, leading = (lax.rem(s + 1, 32), y), (lax.rem(s + 31, 32), y)
    y_mates = [at(z, x, c, turned(y, i)) for i in (1, 2, 3)]
    sibling = scan.sibling
    partners = [following, leading, sibling] + scan.x_mates + scan.z_mates + y_mates
    greet(partners)

    def columns(ref, d):
        return ref[:, pl.ds(pl.multiple_of(d * COLS, COLS), COLS)]

    def to_mates(base, pieces, slots):
        return [
            send(pieces(i), slots.at[i], y_sem.at[0, base + i], y_sem.at[1, base + i], y_mates[i]) for i in range(3)
        ]

    own_rows, far_rows = pl.ds(0, ROWS), pl.ds(ROWS, ROWS)

    def local(i, src, dst):
        return pltpu.make_async_copy(src, dst, w_sem.at[i])

    def turn_at(n):
        return turned(y, (2, 1, 3, 0)[n])

    def part(n):
        return pl.ds(pl.multiple_of(n * COLS, COLS), COLS)

    def held(slot):
        local(slot, w_o.at[:, part(0)], wb.at[slot]).wait()

    def load_forward(u, slot):
        i = slot % 4
        src = (
            lambda: w_gate.at[part(i), part(u)],
            lambda: w_up.at[part(i), part(u)],
            lambda: w_down.at[part(u), part(i)],
        )[slot // 4]()
        local(slot, src, wb.at[slot]).start()

    def load_later(b):
        slot = b % 12
        if b < 32:
            src = (w_gate, w_up)[b % 8 // 4].at[part(turn_at(b // 8)), part(b % 4)]
        elif b < 48:
            src = w_down.at[part(b % 4), part(turn_at((b - 32) // 4))]
        elif b < 52:
            src = w_o.at[:, part(slot)]
        elif b < 56:
            src = w_q.at[part(slot - 4)]
        else:
            rows = part(slot - 8)
            local(slot, w_k.at[rows], wb.at[slot, :, pl.ds(0, 128)]).start()
            local(slot + 4, w_v.at[rows], wb.at[slot, :, pl.ds(128, 128)]).start()
            return
        local(slot, src, wb.at[slot]).start()

    def held_pair(slot):
        rows = part(slot - 8)
        local(slot, w_k.at[rows], wb.at[slot, :, pl.ds(0, 128)]).wait()
        local(slot + 4, w_v.at[rows], wb.at[slot, :, pl.ds(128, 128)]).wait()

    load_g = local(16, g_hbm, gb)
    load_cot = local(17, cot_hbm, x_all)
    load_x = local(18, x_hbm, x_all)
    load_n = [local(19 + i, normed_hbm.at[:, pl.ds(i * COLS, COLS)], gb.at[i]) for i in range(4)]
    load_g.start()
    for slot in range(12):
        load_forward(0, slot)
    load_cot.start()

    left_cot = [
        pltpu.make_async_copy(xt_hbm.at[1, c], xf.at[1, :, :, :, own_rows], w_sem.at[23]),
        send(xt_hbm.at[1, 1 - c], xf.at[1, :, :, :, far_rows], sem_ffn.at[0, 0], sem_ffn.at[1, 0], sibling),
    ]
    left_g = send(xs, xf.at[0, :, :, :, far_rows], sem_ffn.at[0, 1], sem_ffn.at[1, 1], sibling)

    def right_ffn(t):
        return send(yf.at[t, :, own_rows], yf.at[t, :, far_rows], sem_ffn.at[0, 2 + t], sem_ffn.at[1, 2 + t], sibling)

    left_att = [
        pltpu.make_async_copy(xt_hbm.at[0, c], xa.at[0, :, :, :, own_rows], w_sem.at[24]),
        send(xt_hbm.at[0, 1 - c], xa.at[0, :, :, :, far_rows], sem_att.at[0, 0], sem_att.at[1, 0], sibling),
    ]
    left_gb = send(xs, xa.at[1, :, :, :, far_rows], sem_att.at[0, 1], sem_att.at[1, 1], sibling)

    def right_att(t):
        return send(ya.at[t, own_rows], ya.at[t, far_rows], sem_att.at[0, 2 + t], sem_att.at[1, 2 + t], sibling)

    def by_owner(m, xd):
        for i in range(16):
            block = gb[i // 4, :, (i % 4) * 128 : (i % 4 + 1) * 128].T
            xd[m, i // 4, i % 4, :, 0:ROWS] = jnp.where(c == 0, block[:64], block[64:])
            xs[i // 4, i % 4] = jnp.where(c == 0, block[64:], block[:64])

    load_g.wait()
    by_owner(0, xf)
    greeted(partners)
    for copy in left_cot + [left_g]:
        copy.start()

    def product(xd, right):
        def term(t, i, k, *pieces):
            m, yd = right(t, i, k)
            rows = []
            for dest, first, last in pieces:
                piece = xd[m, first:last, dest] if k == 0 else xd[m, dest, first:last]
                rows.append(piece.reshape((last - first) * 64, 2 * ROWS))
            return mm(jnp.concatenate(rows, axis=0), yd)

        return term

    def half_of(k):
        return slice(k * FFN_HALF, (k + 1) * FFN_HALF)

    def finish_ffn(t, i, k, value):
        stage[t // 2 % 2, i, :, half_of(k)] = value

    def write_ffn(u):
        return pltpu.make_async_copy(stage.at[u % 2], out_ffn.at[:, u], sem_stage.at[u % 2])

    def sides(step, u):
        step(2 * u, 0)
        step(2 * u + 1, 1)

    def close_ffn(u):
        if u >= 2:
            write_ffn(u - 2).wait()
        sides(big.end, u)
        write_ffn(u).start()

    def finish_att(t, i, k, value):
        out_att[t] = value

    big = Ring(refs_big, 64, FFN_PARTS, product(xf, lambda t, i, k: (lax.div(i, 2), yf[t // 2, i, :, half_of(k)])), finish_ffn)
    mid = Ring(refs_mid, 64, 1, product(xa, lambda t, i, k: (t // 3, ya[t])), finish_att)

    def begin(u):
        right_ffn(u).wait()
        sides(big.start, u)

    def feed(u, carry):
        def through(first_slot, term):
            value = jnp.zeros((ROWS, COLS), F32)
            for i in range(4):
                slot = first_slot + i
                held(slot)
                value = value + term(i, slot)

                @pl.when(u < 3)
                def _():
                    load_forward(u + 1, slot)

                @pl.when(u == 3)
                def _():
                    load_later(slot)

            return value * scales[:, 1:2]

        gate = through(0, lambda i, slot: mm(gb[i], wb[slot]))
        up = through(4, lambda i, slot: mm(gb[i], wb[slot]))

        @pl.when(u == 0)
        def _():
            load_cot.wait()

        grad = through(8, lambda i, slot: mm_nt(x_all[:, i * COLS : (i + 1) * COLS], wb[slot]))
        sigmoid = jax.nn.sigmoid(gate)
        active = gate * sigmoid
        yf[u, 0, own_rows] = (grad * up * sigmoid * (1.0 + gate * (1.0 - sigmoid))).astype(BF16)
        yf[u, 1, own_rows] = (grad * active).astype(BF16)
        yf[u, 2, own_rows] = (active * up).astype(BF16)
        right_ffn(u).start()

        @pl.when(u == 1)
        def _():
            for copy in left_cot:
                copy.wait()
            left_g.wait()
            begin(0)

        @pl.when(u == 2)
        def _():
            begin(1)

        @pl.when(u == 3)
        def _():
            begin(2)

        return carry

    lax.fori_loop(0, FFN_TILES, feed, 0)
    for copy in left_att:
        copy.start()
    inverse = 1.0 / scales[:, 1:2]
    gs_line = Line(gf_part, gs_came, y_sem, 0)
    dot = jnp.zeros((ROWS, 1), F32)
    for n in range(4):
        value = jnp.zeros((ROWS, COLS), F32)
        for b in range(8 * n, 8 * n + 8):
            held(b % 12)
            value = value + mm_nt(yf[b % 4, b % 8 // 4, 0:ROWS], wb[b % 12])
            load_later(b + 12)
        value = value * inverse
        dot = dot + jnp.sum(value * gb[turn_at(n)].astype(F32), axis=1, keepdims=True)
        if n < 3:
            gf_part[(1, 0, 2)[n]] = value.astype(BF16)
            gs_line.start(*((0, 1), (2,), (3,))[n])
        else:
            gsum[...] = value
    dot_part[...] = jnp.broadcast_to(dot, (ROWS, 128)).T[:8]
    gs_dots = to_mates(6, lambda i: dot_part, dot_came)
    for turn in gs_dots:
        turn.start()
    gs_line.merge()
    begin(3)
    sides(big.merge, 0)

    for turn in gs_dots:
        turn.wait()
    total = gs_line.total(gsum[...])
    gsum[...] = total
    gain_rows = jnp.sum(total * hidden_in[...] * scales[:, 1:2], axis=0, keepdims=True)
    gain_rows_ref[...] = jnp.concatenate([gain_rows[:, i * 128 : (i + 1) * 128] for i in range(4)])

    def mean_column(own):
        return ((own + dot_came[0] + dot_came[1] + dot_came[2]) * (1.0 / 2048)).T[:, 0:1]

    scale = scales[:, 1:2]
    residual = (
        columns(x_all, y).astype(F32)
        + scale * (gsum[...] * columns(gain_two, y))
        - hidden_in[...] * (scale * scale * scale * mean_column(dot_part[...]))
    )
    gres[...] = residual
    gb[y] = residual.astype(BF16)
    gb_share = Share(gb, y_sem, 9)
    gb_share.start()
    load_x.start()

    ffn_turns = to_mates(15, lambda i: gf_part.at[i], ffn_came)
    for n in range(4):
        value = jnp.zeros((ROWS, COLS), F32)
        for b in range(32 + 4 * n, 36 + 4 * n):
            held(b % 12)
            value = value + mm(yf[b % 4, 2, 0:ROWS], wb[b % 12])
            load_later(b + 12)
        if n < 3:
            gf_part[(1, 0, 2)[n]] = value.astype(BF16)
        else:
            out_inputs[...] = value
    gb_share.pass_on()
    sides(big.merge, 1)
    write_mask(mask, lengths)
    def features(h, carry):
        pq[h] = soft_pair(qh[h], f_q[h])
        return carry

    lax.fori_loop(0, HEADS, features, 0)
    for j in range(KEY_HEADS):
        pkey[j] = soft_pair(kv[j][:, :DIM], f_k[j])
        pkey[KEY_HEADS + j] = jnp.zeros((SPAN, 128), F32)
    dkv[...] = jnp.zeros(dkv.shape, F32)
    pk[...] = jnp.zeros(pk.shape, F32)
    sides(big.merge, 2)

    gb_share.finish()
    for turn in ffn_turns:
        turn.start()
    for slot in range(4):
        held(slot)
    grad_low = jnp.zeros((ROWS, 8), F32)
    grad_mixed = jnp.zeros((ROWS, COLS), F32)
    for k in range(4):
        cut = slice(k * COLS, (k + 1) * COLS)
        grad_low = grad_low + mm_nt(gb[k], b_out[:, cut])
        grad_mixed = grad_mixed + mm_nt(gb[k], wb[k])
    grad_mixed = grad_mixed + jnp.dot(
        grad_low, a_out[...].astype(F32), precision=HIGH, preferred_element_type=F32
    )
    rounded = grad_mixed.astype(BF16)
    for h in range(HEADS):
        gh[h] = rounded[:, h * DIM : (h + 1) * DIM]
    top, bottom = halves(grad_low)
    gao[...] = mm_tn(top, mixed[...]) + mm_tn(bottom, mixed[...])
    for k in range(4):
        gbo[:, k * COLS : (k + 1) * COLS] = mm_tn(low_mix[...], gb[k])

    lane = lax.broadcasted_iota(jnp.int32, (ROWS, DIM), 1)
    for h in range(HEADS):
        j = h // 4
        grad = gh[h].astype(F32)
        column = stat[h].T
        inverse = 1.0 / column[:, 1:2]
        inner = -jnp.sum(grad * att[:, h * DIM : (h + 1) * DIM], axis=1, keepdims=True) * inverse
        ext = jnp.concatenate([grad * inverse, jnp.where(lane == 0, inner, 0.0)], axis=1)
        dext[h] = ext
        top, bottom = halves(ext * column[:, 2:3])
        phi = pq[h].astype(BF16)
        piece = (mm_tn(top, phi) + mm_tn(bottom, phi))[:STATE]
        scan.own[0, j] = piece if h % 4 == 0 else scan.own[0, j] + piece
    scan.open()

    by_owner(1, xa)
    for load in load_n:
        load.start()
    left_gb.start()
    for t in (3, 4):
        ya[t, 0:ROWS] = mixed[:, (t - 3) * ATT_WIDTH : (t - 2) * ATT_WIDTH]
        right_att(t).start()
    scan.along_x()
    left_gb.wait()
    for t in (3, 4):
        right_att(t).wait()
        mid.start(t, t % 2)

    def backward(h, carry):
        j = lax.div(h, 4)
        keys, values = kv[j][:, :DIM], kv[j][:, DIM:]
        q, grad, ext = qh[h], gh[h], dext[h]
        column = stat[h].T
        top, inverse, gate = column[:, 0:1], 1.0 / column[:, 1:2], column[:, 2:3]
        distant = mask[...] == NEG
        soft = pq[h]
        phi, phi_key = soft.astype(BF16), pkey[j].astype(BF16)
        damping = jnp.where(distant, jnp.exp(-top), 0.0)
        weights = jnp.exp(mm_nt(q, keys) * (DIM**-0.5) + mask[...] - top)
        grad_weights = mm_nt(grad, values) * inverse + ext[:, DIM : DIM + 1]
        grad_scores = (weights * grad_weights).astype(BF16)
        grad_linear = (damping * grad_weights).astype(BF16)
        both = weights.astype(BF16).astype(F32) + mm_nt(phi, phi_key) * damping
        held_weights = (both * inverse).astype(BF16)
        grad_q = mm(grad_scores, keys) * (DIM**-0.5)
        grad_k = mm_tn(grad_scores, q) * (DIM**-0.5)
        dkv[j] = dkv[j] + jnp.concatenate([grad_k, mm_tn(held_weights, grad)], axis=1)
        pkey[KEY_HEADS + j] = pkey[KEY_HEADS + j] + mm_tn(grad_linear, phi)
        carried = jnp.dot(
            (ext * gate)[:, :STATE], state[j], precision=HIGH, preferred_element_type=F32
        )
        grad_soft = mm(grad_linear, phi_key) + carried
        high, rest = halves(soft_back(soft, grad_soft))
        gh[h] = (grad_q + mm_nt(high, f_q[h]) + mm_nt(rest, f_q[h])).astype(BF16)
        gfq[h] = mm_tn(q, high) + mm_tn(q, rest)

        @pl.when(h == 1)
        def _():
            scan.along_z()

        @pl.when(h == 2)
        def _():
            sides(big.cross, 0)

        @pl.when(h == 3)
        def _():
            sides(big.merge, 3)

        @pl.when(h == 5)
        def _():
            sides(big.cross, 1)

        @pl.when(h == 7)
        def _():
            sides(big.cross, 2)

        return carry

    lax.fori_loop(0, HEADS, backward, 0)

    for j in range(KEY_HEADS):
        ret[j] = jnp.concatenate([dkv[j, :WINDOW], pkey[KEY_HEADS + j, :WINDOW]], axis=1)
    home = [
        send(ret, ret_came, ret_sem.at[0], ret_sem.at[1], leading),
        send(scan.own.at[0], next_state, ret_sem.at[2], ret_sem.at[3], leading),
    ]
    for copy in home:
        copy.start()
    gq = jnp.concatenate([gh[h] for h in range(HEADS)], axis=1)
    for i in range(2):
        ya[i, 0:ROWS] = gq[:, i * ATT_WIDTH : (i + 1) * ATT_WIDTH]
        right_att(i).start()
    down_ref[...] = down_rows(a_q, a_k, a_v)
    for slot in range(4, 8):
        held(slot)
    for slot in range(8, 12):
        held_pair(slot)
    for load in load_n + [load_x]:
        load.wait()
    glow[:, :8] = mm_nt(gq, b_q[...])
    for copy in left_att:
        copy.wait()
    for t in range(2):
        right_att(t).wait()
        mid.start(t, t % 2)
    for k in range(4):
        first[k] = mm_nt(gq, wb[4 + k])

    inside = middle(ROWS, 0, lengths)
    suffix = scan.close(scan.pair[...] * (1.0 - c.astype(F32)))
    for copy in home:
        copy.wait()
    joined = (s < 31).astype(F32)
    late_row = lax.broadcasted_iota(jnp.int32, (ROWS, 128), 0) >= ROWS - WINDOW
    for j in range(KEY_HEADS):
        soft = pkey[j, WINDOW:]
        phi = soft.astype(BF16)
        keys = kv[j, WINDOW:][:, :DIM]
        rows = value_columns(kv[j, WINDOW:])[:, :STATE]
        high, rest = halves(suffix[j])
        high_next, rest_next = halves(suffix[j] - joined * next_state[j])
        grad_phi = jnp.where(late_row, mm(rows, high_next) + mm(rows, rest_next), mm(rows, high) + mm(rows, rest))
        grad_phi = grad_phi * inside + pkey[KEY_HEADS + j, WINDOW:]
        grad_v = jnp.where(
            late_row[:, :STATE], mm_nt(phi, high_next) + mm_nt(phi, rest_next), mm_nt(phi, high) + mm_nt(phi, rest)
        )
        grad_v = (grad_v * inside)[:, :DIM]
        last = ROWS - WINDOW
        grad_phi = jnp.concatenate([grad_phi[:last], grad_phi[last:] + ret_came[j][:, 2 * DIM :]], axis=0)
        high, rest = halves(soft_back(soft, grad_phi))
        grad_k = mm_nt(high, f_k[j]) + mm_nt(rest, f_k[j])
        gfk[j] = mm_tn(keys, high) + mm_tn(keys, rest)
        dkv[j, WINDOW:] = dkv[j, WINDOW:] + jnp.concatenate([grad_k, grad_v], axis=1)
        dkv[j, ROWS:] = dkv[j, ROWS:] + ret_came[j][:, : 2 * DIM]
    gk = jnp.concatenate([dkv[j, WINDOW:][:, :DIM] for j in range(KEY_HEADS)], axis=1).astype(BF16)
    gv = jnp.concatenate([dkv[j, WINDOW:][:, DIM:] for j in range(KEY_HEADS)], axis=1).astype(BF16)
    gkv[...] = jnp.concatenate([gk, gv], axis=1)
    ya[2, 0:ROWS] = gkv[...]
    right_att(2).start()

    glow[:, 8:16] = mm_nt(gk, b_k[...])
    glow[:, 16:24] = mm_nt(gv, b_v[...])
    glow_high, glow_rest = halves(glow[...])
    for k in range(4):
        wide[:, k * COLS : (k + 1) * COLS] = mm_tn(glow_high, gb[k]) + mm_tn(glow_rest, gb[k])

    def place(d):
        return d // 16, d // 4 % 4, d % 4

    for i in range(16):
        cut = slice(i * 128, (i + 1) * 128)
        for half in range(2):
            d = place(2 * i + half)
            pk[*d, 0:12] = wide[12 * half : 12 * half + 12, cut]
            pk[*d, 13:16] = 0.25 * gbo[3 * half : 3 * half + 3, cut]
        pk[*place(26 + i // 8), 16 + 2 * (i % 8) : 18 + 2 * (i % 8)] = gbo[6:8, cut]

    def low_half(d, value):
        pk[*place(d), 16 : 16 + value.shape[0]] = value

    for i in range(4):
        pair = jnp.concatenate([gfq[2 * i], gfq[2 * i + 1]], axis=1)
        for part in range(4):
            low_half(4 * i + part, pair[16 * part : 16 * part + 16])
    pair = jnp.concatenate([gfk[0], gfk[1]], axis=1)
    for part in range(4):
        low_half(16 + part, pair[16 * part : 16 * part + 16])
    grad_b = jnp.concatenate(
        [mm_tn(low[:, :8], gq), mm_tn(low[:, 8:16], gkv[:, :128]), mm_tn(low[:, 16:24], gkv[:, 128:])], axis=1
    )
    for i in range(3):
        low_half(20 + i, jnp.concatenate([grad_b[:, 256 * i : 256 * i + 128], grad_b[:, 256 * i + 128 : 256 * i + 256]]))
    for i in range(2):
        low_half(23 + i, jnp.concatenate([gao[:, 256 * i : 256 * i + 128], gao[:, 256 * i + 128 : 256 * i + 256]]))
    low_half(25, gain_rows_ref[...])
    pack_far = send(pk.at[1 - c], pk.at[2], sem_pack.at[0], sem_pack.at[1], sibling)
    pack_far.start()

    for turn in ffn_turns:
        turn.wait()
    out_block[...] = (
        hidden_in[...]
        + out_inputs[...]
        + ffn_came[0].astype(F32)
        + ffn_came[1].astype(F32)
        + ffn_came[2].astype(F32)
    ).astype(BF16)
    gf_line = Line(gf_part, gs_came, y_sem, 18)

    def partial_first(d, dot):
        rows = pl.ds(pl.multiple_of(d * COLS, COLS), COLS)
        down = columns(down_ref, d)
        part = first[d] + mm_nt(gkv[...], wb[8 + d, :, 0:256]) + mm(glow_high, down) + mm(glow_rest, down)
        shaped = part * columns(x_all, d).astype(F32)
        gain_row[:, rows] = jnp.sum(shaped * scales[:, 0:1], axis=0, keepdims=True)
        return part, dot + jnp.sum(shaped * columns(gain_one, d), axis=1, keepdims=True)

    def spread(sems, base, piece, mates, back_piece):
        turns = [send(piece, piece, sems.at[0, base + i], sems.at[1, base + i], mate) for i, mate in enumerate(mates)]
        for turn in turns:
            turn.start()
        return [
            send(back_piece(i), back_piece(i), sems.at[0, base + i], sems.at[1, base + i], mate)
            for i, mate in enumerate(mates)
        ]

    def settle(turns):
        for turn in turns:
            turn.wait()

    dot = jnp.zeros((ROWS, 1), F32)
    for i in (1, 0):
        chunk, dot = partial_first(turned(y, 1 + i), dot)
        gf_part[i] = chunk.astype(BF16)
        gf_line.start(*((2,), (0, 1))[i])

    pack_far.wait()
    x_turns = [send(px.at[i], px_came.at[i], sem_zx.at[0, i], sem_zx.at[1, i], scan.x_mates[i]) for i in range(3)]
    for i in range(3):
        dest = turned(x, 1 + i)
        px[i] = (pk[c, :, dest] + pk[2, :, dest]).astype(BF16)
        x_turns[i].start()
    chunk, dot = partial_first(turned(y, 3), dot)
    gf_part[2] = chunk.astype(BF16)
    gf_line.start(3)
    chunk, dot = partial_first(y, dot)
    gsum[...] = chunk
    dot_part[...] = jnp.broadcast_to(dot, (ROWS, 128)).T[:8]
    dot_turns = to_mates(24, lambda i: dot_part, dot_came)
    for turn in dot_turns:
        turn.start()
    for i in range(16):
        gain_c[c, i : i + 1] = gain_row[:, i * 128 : (i + 1) * 128]
    gain_turns = spread(sem_gain, 0, gain_c.at[c], [sibling], lambda i: gain_c.at[1 - c])
    own_pack = pk[c, :, x] + pk[2, :, x]
    right_att(2).wait()
    mid.start(2, 0)
    gf_line.merge()
    settle(x_turns)
    own_pack = own_pack + px_came[0].astype(F32) + px_came[1].astype(F32) + px_came[2].astype(F32)
    pz[z] = own_pack.astype(BF16)
    z_turns = spread(sem_zx, 3, pz.at[z], scan.z_mates, lambda i: pz.at[turned(z, 3 - i)])
    settle(gain_turns)
    gain_x[x] = gain_c[0] + gain_c[1]
    gain_turns = spread(sem_gain, 1, gain_x.at[x], scan.x_mates, lambda i: gain_x.at[turned(x, 3 - i)])
    for t in (3, 4, 0, 1):
        mid.merge(t, t % 2)
    settle(z_turns)
    own_pack = pz[0].astype(F32) + pz[1].astype(F32) + pz[2].astype(F32) + pz[3].astype(F32)
    crown[y] = own_pack[:, :16]
    y_turns = spread(sem_zx, 10, crown.at[y], y_mates, lambda i: crown.at[turned(y, 3 - i)])
    settle(gain_turns)
    gain_z[z] = gain_x[0] + gain_x[1] + gain_x[2] + gain_x[3]
    gain_turns = spread(sem_gain, 4, gain_z.at[z], scan.z_mates, lambda i: gain_z.at[turned(z, 3 - i)])
    sides(big.cross, 3)
    mid.merge(2, 0)
    settle(y_turns)
    top = crown[0] + crown[1] + crown[2] + crown[3]
    out_pack[c, :, x] = jnp.concatenate([top, own_pack[:, 16:]], axis=1).astype(BF16)
    x_turns = spread(sem_zx, 6, out_pack.at[c, :, x], scan.x_mates, lambda i: out_pack.at[c, :, turned(x, 3 - i)])
    settle(gain_turns)
    gain_y[y] = gain_z[0] + gain_z[1] + gain_z[2] + gain_z[3]
    gain_turns = spread(sem_gain, 7, gain_y.at[y], y_mates, lambda i: gain_y.at[turned(y, 3 - i)])
    for t in (3, 4, 0, 1, 2):
        mid.cross(t, t % 2)
    sides(big.merge_cross, 0)
    sides(big.merge_cross, 1)
    sides(big.merge_cross, 2)
    settle(dot_turns)
    total = gf_line.total(gsum[...])
    scale = scales[:, 0:1]
    out_inputs[...] = (
        gres[...]
        + scale * (total * columns(gain_one, y))
        - columns(x_all, y).astype(F32) * (scale * scale * scale * mean_column(dot_part[...]))
    )
    settle(x_turns)
    last = spread(sem_zx, 9, out_pack.at[c], [sibling], lambda i: out_pack.at[1 - c])
    settle(gain_turns)
    out_gain[...] = gain_y[0] + gain_y[1] + gain_y[2] + gain_y[3]
    for t in (3, 4, 0, 1, 2):
        mid.merge_cross(t, t % 2)
    sides(big.merge_cross, 3)
    for t in range(FFN_TILES):
        close_ffn(t)
    for t in (3, 4, 0, 1, 2):
        mid.end(t, t % 2)
    settle(last)
    write_ffn(2).wait()
    write_ffn(3).wait()
    for u in range(FFN_TILES):
        sides(big.drain, u)
    for t in range(ATT_TILES):
        mid.drain(t, t % 2)


def late(args, weights):
    anywhere = pl.BlockSpec(memory_space=pl.ANY)
    vmem = pl.BlockSpec(memory_space=pltpu.VMEM)
    shapes = (
        ((ROWS, COLS), BF16),
        ((ROWS, COLS), F32),
        ((FFN_PARTS, FFN_TILES, 64, FFN_WIDTH), F32),
        ((ATT_TILES, 64, ATT_WIDTH), F32),
        ((2, 4, 4, PACK, 128), BF16),
        ((16, 128), F32),
    )
    block = (ROWS, COLS)
    return pl.pallas_call(
        late_kernel,
        out_shape=tuple(jax.ShapeDtypeStruct(*shape) for shape in shapes),
        in_specs=[vmem] * 22 + [pl.BlockSpec(memory_space=pltpu.SMEM)] + [anywhere] * 12,
        out_specs=(vmem, vmem, anywhere, vmem, vmem, vmem),
        scratch_shapes=[
            pltpu.VMEM((12, COLS, COLS), BF16),
            pltpu.VMEM((ROWS, 2048), BF16),
            pltpu.SemaphoreType.DMA((25,)),
            pltpu.VMEM((3, *block), BF16),
            pltpu.VMEM((3, *block), BF16),
            pltpu.VMEM((3, *block), BF16),
            pltpu.VMEM((8, ROWS), F32),
            pltpu.VMEM((3, 8, ROWS), F32),
            pltpu.VMEM((4, *block), BF16),
            pltpu.VMEM(block, F32),
            pltpu.VMEM(block, F32),
            pltpu.SemaphoreType.DMA((2, 27)),
            pltpu.VMEM((2, 4, 4, 64, 512), BF16),
            pltpu.VMEM((FFN_TILES, FFN_PARTS, 512, FFN_WIDTH), BF16),
            pltpu.VMEM((4, 4, 64, ROWS), BF16),
            pltpu.SemaphoreType.DMA((2, 2 + FFN_TILES)),
            pltpu.VMEM((2, 4, 4, 64, 512), BF16),
            pltpu.VMEM((ATT_TILES, 512, ATT_WIDTH), BF16),
            pltpu.SemaphoreType.DMA((2, 2 + ATT_TILES)),
            pltpu.VMEM((3, 4, 4, PACK, 128), F32),
            pltpu.SemaphoreType.DMA((2,)),
            pltpu.VMEM((ROWS, SPAN), F32),
            pltpu.VMEM((HEADS, ROWS, DIM), BF16),
            pltpu.VMEM((HEADS, ROWS, 128), F32),
            pltpu.VMEM((2 * KEY_HEADS, SPAN, 128), F32),
            pltpu.VMEM((HEADS, ROWS, 128), F32),
            pltpu.VMEM((KEY_HEADS, SPAN, 128), F32),
            pltpu.VMEM((HEADS, DIM, DIM), F32),
            pltpu.VMEM((KEY_HEADS, DIM, DIM), F32),
            pltpu.VMEM((KEY_HEADS, WINDOW, 256), F32),
            pltpu.VMEM((KEY_HEADS, WINDOW, 256), F32),
            pltpu.VMEM((KEY_HEADS, STATE, 128), F32),
            pltpu.SemaphoreType.DMA((4,)),
            pltpu.VMEM((ROWS, 24), F32),
            pltpu.VMEM((ROWS, 256), BF16),
            pltpu.VMEM((24, 2048), F32),
            pltpu.VMEM((8, COLS), F32),
            pltpu.VMEM((8, 2048), F32),
            pltpu.VMEM((24, 2048), BF16),
            pltpu.VMEM((4, *block), F32),
            pltpu.VMEM((1, 2048), F32),
            pltpu.VMEM((4, 128), F32),
            pltpu.VMEM((3, 4, PACK, 128), BF16),
            pltpu.VMEM((3, 4, PACK, 128), BF16),
            pltpu.VMEM((4, 4, PACK, 128), BF16),
            pltpu.VMEM((4, 4, 16, 128), F32),
            pltpu.SemaphoreType.DMA((2, 13)),
            pltpu.VMEM((2, FFN_PARTS, 64, FFN_WIDTH), F32),
            pltpu.SemaphoreType.DMA((2,)),
            pltpu.VMEM((2, 16, 128), F32),
            pltpu.VMEM((4, 16, 128), F32),
            pltpu.VMEM((4, 16, 128), F32),
            pltpu.VMEM((4, 16, 128), F32),
            pltpu.SemaphoreType.DMA((2, 10)),
            *Scan.scratch((KEY_HEADS, STATE, 128)),
            *Ring.scratch(2 * FFN_TILES, FFN_PARTS, 64, FFN_HALF),
            *Ring.scratch(ATT_TILES, 1, 64, ATT_WIDTH),
        ],
        compiler_params=pltpu.CompilerParams(
            collective_id=2, has_side_effects=True, vmem_limit_bytes=63 * 2**20 + 2**19
        ),
        name="late",
    )(*args, *weights)


def finish_kernel(
    block, inputs, ffn_sums, att_sums, packed, gains,
    block_out, inputs_out, gain_one, w_q, a_q, b_q, w_k, a_k, b_k, w_v, a_v, b_v, f_q, f_k, w_o, a_o, b_o, gain_two,
    w_gate, w_up, w_down,
):
    block_out[...] = block[...]
    pack = packed[...].astype(F32)
    inputs_out[...] = inputs[...]
    for i in range(4):
        cut = slice(i * FFN_WIDTH, (i + 1) * FFN_WIDTH)
        w_gate[:, cut] = ffn_sums[0, i]
        w_up[:, cut] = ffn_sums[1, i]
        w_down[:, cut] = ffn_sums[2, i]
    for i in range(2):
        cut = slice(i * ATT_WIDTH, (i + 1) * ATT_WIDTH)
        w_q[:, cut] = att_sums[i]
        w_o[:, cut] = att_sums[3 + i]
    w_k[...] = att_sums[2, :, :128]
    w_v[...] = att_sums[2, :, 128:]
    for i in range(16):
        cut = slice(i * 128, (i + 1) * 128)
        rows = jnp.concatenate([pack[2 * i, :12], pack[2 * i + 1, :12]], axis=0)
        a_q[:, cut] = rows[:8]
        a_k[:, cut] = rows[8:16]
        a_v[:, cut] = rows[16:]
        last = 16 + 2 * (i % 8)
        b_o[:, cut] = jnp.concatenate(
            [pack[2 * i, 13:16], pack[2 * i + 1, 13:16], pack[26 + i // 8, last : last + 2]], axis=0
        )

    def tile(i):
        return pack[20 + i // 2, 16 + 8 * (i % 2) : 24 + 8 * (i % 2)]

    for i in range(4):
        cut = slice(i * 128, (i + 1) * 128)
        for part in range(4):
            rows = pack[4 * i + part, 16:]
            f_q[2 * i, 16 * part : 16 * part + 16] = rows[:, :DIM]
            f_q[2 * i + 1, 16 * part : 16 * part + 16] = rows[:, DIM:]
        rows = pack[16 + i, 16:]
        f_k[0, 16 * i : 16 * i + 16] = rows[:, :DIM]
        f_k[1, 16 * i : 16 * i + 16] = rows[:, DIM:]
        b_q[:, cut] = tile(i)
        a_o[:, cut] = tile(6 + i)
        gain_two[:, cut] = pack[25, 16 + i : 17 + i]
        gain_one[:, cut] = gains[pl.ds(4 * lax.axis_index("head") + i, 1), :]
    b_k[...] = tile(4)
    b_v[...] = tile(5)


def finish(block, inputs, ffn_sums, att_sums, pack, gains):
    vmem = pl.BlockSpec(memory_space=pltpu.VMEM)
    shapes = (
        (ROWS, COLS), (ROWS, COLS), (1, COLS), (64, COLS), (8, 2048), (8, COLS), (64, 128), (8, 2048), (8, 128),
        (64, 128), (8, 2048), (8, 128), (HEADS, DIM, DIM), (KEY_HEADS, DIM, DIM), (64, COLS), (8, COLS), (8, 2048),
        (1, COLS), (64, 2048), (64, 2048), (64, 2048),
    )
    outs = pl.pallas_call(
        finish_kernel,
        out_shape=tuple(jax.ShapeDtypeStruct(shape, F32 if i else BF16) for i, shape in enumerate(shapes)),
        in_specs=[vmem] * 6,
        out_specs=(vmem,) * len(shapes),
        compiler_params=pltpu.CompilerParams(vmem_limit_bytes=63 * 2**20),
        name="finish",
    )(block, inputs, ffn_sums, att_sums, pack.reshape(32, 32, 128), gains)
    return tuple(
        out[0] if i in (2, 17) else out.T if i in (4, 7, 10, 14, 15, 20) else out for i, out in enumerate(outs)
    )


def body(
    inputs,
    gain_first,
    w_query,
    a_query,
    b_query,
    key_projection_weight,
    a_key,
    key_adapter_second,
    value_projection_weight,
    a_value,
    value_adapter_second,
    feature_query,
    key_hedgehog_map,
    w_out,
    a_out,
    b_out,
    gain_second,
    w_gate,
    w_up,
    w_down,
    lengths,
    cotangent,
):
    gain_one, gain_two = gain_first[None], gain_second[None]
    a_in = (a_query.T, a_key.T, a_value.T)
    a_out = a_out.T
    projections = (w_query, key_projection_weight, value_projection_weight, w_out)
    normed, low, queries, kv, state, att, stat, mixed, low_mix, hidden_in, g, scales, xt = front(
        inputs, gain_one, gain_two, *a_in, b_query, key_adapter_second, value_adapter_second,
        feature_query, key_hedgehog_map, a_out, b_out, lengths, *projections, cotangent,
    )
    block_out, grad_inputs, out_ffn, out_att, out_pack, out_gain = late(
        (
            hidden_in, scales, gain_one, gain_two, mixed, low_mix, att, stat, state, queries, kv, low,
            feature_query, key_hedgehog_map, *a_in, a_out, b_out, b_query, key_adapter_second,
            value_adapter_second, lengths,
        ),
        (g, normed, inputs, cotangent, xt, *projections, w_gate, w_up, w_down),
    )
    return finish(block_out, grad_inputs, out_ffn, out_att, out_pack, out_gain)


def solution(mesh):
    return jax.shard_map(
        body,
        mesh=mesh,
        in_specs=(
            P("seq", None),
            P(),
            P(None, "head"),
            P(),
            P(None, "head"),
            P(None, "head"),
            P(),
            P(None, "head"),
            P(None, "head"),
            P(),
            P(None, "head"),
            P("head", None, None),
            P("head", None, None),
            P("head", None),
            P("head", None),
            P(),
            P(),
            P(None, "head"),
            P(None, "head"),
            P("head", None),
            P(),
            P("seq", None),
        ),
        out_specs=(
            P("seq", "head"),
            P("seq", "head"),
            P("head"),
            P("seq", "head"),
            P(),
            P(None, "head"),
            P("seq", "head"),
            P(),
            P(None, "head"),
            P("seq", "head"),
            P(),
            P(None, "head"),
            P("head", None, None),
            P("head", None, None),
            P("head", "seq"),
            P("head", None),
            P(),
            P("head"),
            P("seq", "head"),
            P("seq", "head"),
            P("head", "seq"),
        ),
        check_vma=False,
    )
```

```python
import jax
import jax.numpy as jnp
from jax import lax
from jax.experimental import pallas as pl
from jax.experimental.pallas import tpu as pltpu
from jax.sharding import PartitionSpec as P

MESH = pl.DeviceIdType.MESH
F32 = jnp.float32
BF16 = jnp.bfloat16


def spot():
    s = lax.axis_index("seq")
    y = lax.axis_index("head")
    return lax.div(s, 8), lax.rem(lax.div(s, 2), 4), lax.rem(s, 2), y


def at(z, x, c, y):
    return ((z * 4 + x) * 2 + c, y)


def turned(p, steps):
    return lax.rem(p + steps, 4)


def greet(partners):
    barrier = pltpu.get_barrier_semaphore()
    for partner in partners:
        pl.semaphore_signal(barrier, inc=1, device_id=partner, device_id_type=MESH)


def greeted(partners):
    pl.semaphore_wait(pltpu.get_barrier_semaphore(), len(partners))


def send(src, dst, ss, rs, device):
    return pltpu.make_async_remote_copy(
        src_ref=src, dst_ref=dst, send_sem=ss, recv_sem=rs, device_id=device, device_id_type=MESH
    )


def took(ref, sem):
    pltpu.make_async_copy(ref, ref, sem).wait()


class Ring:
    def __init__(self, refs, rows, pieces, term, finish):
        self.sb, self.ra, self.rf, self.ra3, self.rf3, self.ss, self.rs = refs
        self.rows, self.pieces, self.term, self.finish = rows, pieces, term, finish
        z, x, c, y = spot()
        self.axes = (
            (x, at(z, turned(x, 1), c, y), at(z, turned(x, 3), c, y)),
            (z, at(turned(z, 1), x, c, y), at(turned(z, 3), x, c, y)),
        )

    @staticmethod
    def scratch(count, pieces, rows, width):
        return [
            pltpu.VMEM((count, 2, pieces, 4 * rows, width), BF16),
            pltpu.VMEM((count, 2, pieces, 2 * rows, width), BF16),
            pltpu.VMEM((count, 2, pieces, 4 * rows, width), BF16),
            pltpu.VMEM((count, 2, pieces, rows // 2, width), BF16),
            pltpu.VMEM((count, 2, pieces, rows, width), BF16),
            pltpu.SemaphoreType.DMA((count, 4)),
            pltpu.SemaphoreType.DMA((count, 6)),
        ]

    def each(self, step):
        if self.pieces == 1:
            step(0)
        else:

            def one(p, carry):
                step(p)
                return carry

            lax.fori_loop(0, self.pieces, one, 0)

    def block(self, b, part):
        g = self.rows // 2
        if part is None:
            return pl.ds(pl.multiple_of(b * self.rows, self.rows), self.rows)
        return pl.ds(pl.multiple_of(b * self.rows + part * g, g), g)

    def copy(self, t, k, i):
        p, ahead, behind = self.axes[k]
        q, ahead3, behind3 = self.axes[1 - k]
        h, g = 2 * self.rows, self.rows // 2
        lo, hi, lo3, hi3 = pl.ds(0, h), pl.ds(h, h), pl.ds(0, g), pl.ds(g, g)
        sb, ra, rf, ra3, rf3, block = self.sb, self.ra, self.rf, self.ra3, self.rf3, self.block
        src, dst, device = (
            lambda: (sb.at[t, 0, :, lo], ra.at[t, 0], ahead),
            lambda: (sb.at[t, 0, :, hi], ra.at[t, 1], behind),
            lambda: (sb.at[t, 1, :, hi], rf.at[t, 0, :, hi], ahead),
            lambda: (sb.at[t, 1, :, lo], rf.at[t, 1, :, lo], behind),
            lambda: (ra.at[t, 0], rf.at[t, 0, :, lo], ahead),
            lambda: (ra.at[t, 1], rf.at[t, 1, :, hi], behind),
            lambda: (sb.at[t, 0, :, block(turned(q, 2), 0)], ra3.at[t, 0], ahead3),
            lambda: (sb.at[t, 0, :, block(turned(q, 2), 1)], ra3.at[t, 1], behind3),
            lambda: (sb.at[t, 0, :, block(turned(q, 1), 1)], rf3.at[t, 0, :, hi3], ahead3),
            lambda: (sb.at[t, 0, :, block(turned(q, 3), 0)], rf3.at[t, 1, :, lo3], behind3),
            lambda: (ra3.at[t, 0], rf3.at[t, 0, :, lo3], ahead3),
            lambda: (ra3.at[t, 1], rf3.at[t, 1, :, hi3], behind3),
        )[i]()
        here = (0, 0, 0, 0, 1, 1, 2, 2, 2, 2, 3, 3)[i]
        there = (0, 1, 2, 2, 2, 2, 3, 4, 5, 5, 5, 5)[i]
        return send(src, dst, self.ss.at[t, here], self.rs.at[t, there], device)

    def sent(self, t, group):
        took((self.sb, self.ra, self.rf3, self.ra3)[group].at[t], self.ss.at[t, group])

    def arrived(self, t, group):
        ref = (self.ra.at[t, 0], self.ra.at[t, 1], self.rf.at[t], self.ra3.at[t, 0], self.ra3.at[t, 1], self.rf3.at[t])
        took(ref[group], self.rs.at[t, group])

    def start(self, t, k):
        p = self.axes[k][0]
        h = 2 * self.rows
        pieces = ((turned(p, 2), 0, 4), (turned(p, 3), 0, 2), (turned(p, 1), 2, 4))

        def one(i):
            value = self.term(t, i, k, *pieces).astype(BF16)
            self.sb[t, 0, i] = value[: 2 * h]
            self.sb[t, 1, i] = value[2 * h :]

        self.each(one)
        for i in range(4):
            self.copy(t, k, i).start()

    def merge(self, t, k):
        p = self.axes[k][0]
        h = 2 * self.rows
        for way in range(2):
            self.arrived(t, way)

        def one(i):
            mine = self.term(t, i, k, (turned(p, 1), 0, 2), (turned(p, 3), 2, 4))
            for way in range(2):
                part = mine[way * h : (way + 1) * h]
                self.ra[t, way, i] = (part + self.ra[t, way, i].astype(F32)).astype(BF16)

        self.each(one)
        for way in range(2):
            self.copy(t, k, 4 + way).start()

    def cross(self, t, k):
        p = self.axes[k][0]
        self.sent(t, 0)
        self.arrived(t, 2)

        def one(i):
            own = self.term(t, i, k, (p, 0, 4))
            self.sb[t, 0, i] = (own + self.rf[t, 0, i].astype(F32) + self.rf[t, 1, i].astype(F32)).astype(BF16)

        self.each(one)
        for i in (6, 7, 8, 9):
            self.copy(t, k, i).start()

    def merge_cross(self, t, k):
        q = self.axes[1 - k][0]
        for way, dest in ((0, turned(q, 1)), (1, turned(q, 3))):
            self.arrived(t, 3 + way)

            def one(i):
                mine = self.sb[t, 0, i, self.block(dest, way), :]
                self.ra3[t, way, i] = (mine.astype(F32) + self.ra3[t, way, i].astype(F32)).astype(BF16)

            self.each(one)
            self.copy(t, k, 10 + way).start()

    def end(self, t, k):
        q = self.axes[1 - k][0]
        self.arrived(t, 5)

        def one(i):
            mine = self.sb[t, 0, i, self.block(q, None), :].astype(F32)
            self.finish(t, i, k, mine + self.rf3[t, 0, i].astype(F32) + self.rf3[t, 1, i].astype(F32))

        self.each(one)

    def drain(self, t, k):
        for group in (1, 2, 3):
            self.sent(t, group)


LO, HI = pl.ds(0, 128), pl.ds(128, 128)


class Line:
    def __init__(self, part, came, sems, base):
        z, x, c, y = spot()
        ahead, behind = at(z, x, c, turned(y, 1)), at(z, x, c, turned(y, 3))
        self.part, self.came = part, came
        ways = (
            (part.at[1, LO], came.at[2, LO], ahead),
            (part.at[1, HI], came.at[2, HI], behind),
            (part.at[0, HI], came.at[0, HI], ahead),
            (part.at[2, LO], came.at[1, LO], behind),
            (came.at[2, LO], came.at[0, LO], ahead),
            (came.at[2, HI], came.at[1, HI], behind),
        )
        self.copies = [send(src, dst, sems.at[0, base + i], sems.at[1, base + i], to) for i, (src, dst, to) in enumerate(ways)]

    def start(self, *which):
        for i in which:
            self.copies[i].start()

    def merge(self):
        for i, piece, rows in ((0, 0, LO), (1, 2, HI)):
            self.copies[i].wait_recv()
            self.came[2, rows] = (self.came[2, rows].astype(F32) + self.part[piece, rows].astype(F32)).astype(BF16)
            self.copies[4 + i].start()

    def total(self, own):
        for copy in self.copies[2:]:
            copy.wait_recv()
        for copy in self.copies:
            copy.wait_send()
        return own + self.came[0].astype(F32) + self.came[1].astype(F32)


class Share:
    def __init__(self, ref, sems, base):
        z, x, c, y = spot()
        ahead, behind = at(z, x, c, turned(y, 1)), at(z, x, c, turned(y, 3))
        next_y, last_y, far_y = turned(y, 1), turned(y, 3), turned(y, 2)
        out = (
            (ref.at[y, LO], ahead),
            (ref.at[y, HI], behind),
            (ref.at[y, HI], ahead),
            (ref.at[y, LO], behind),
            (ref.at[last_y, LO], ahead),
            (ref.at[next_y, HI], behind),
        )
        into = (
            ref.at[last_y, LO],
            ref.at[next_y, HI],
            ref.at[last_y, HI],
            ref.at[next_y, LO],
            ref.at[far_y, LO],
            ref.at[far_y, HI],
        )
        self.copies = [send(src, src, sems.at[0, base + i], sems.at[1, base + i], to) for i, (src, to) in enumerate(out)]
        self.arrivals = [send(dst, dst, sems.at[0, base + i], sems.at[1, base + i], ahead) for i, dst in enumerate(into)]

    def start(self):
        for copy in self.copies[:4]:
            copy.start()

    def pass_on(self):
        for i in range(2):
            self.arrivals[i].wait_recv()
            self.copies[4 + i].start()

    def finish(self):
        for arrival in self.arrivals[2:]:
            arrival.wait_recv()
        for copy in self.copies:
            copy.wait_send()


FFN_TILES, FFN_PARTS, FFN_WIDTH, FFN_HALF = 4, 3, 512, 256
ATT_TILES, ATT_WIDTH = 5, 256
PACK = 32


EPS = 1e-05
NEG = -1e30
HIGH = lax.Precision.HIGHEST
ROWS = 256
WINDOW = 64
SPAN = ROWS + WINDOW
COLS = 512
HEADS, KEY_HEADS, DIM = 8, 2, 64
STATE = 72


def mm(a, b):
    return jnp.dot(a, b, preferred_element_type=F32)


def mm_nt(a, b, precision=None):
    return lax.dot_general(a, b, (((1,), (1,)), ((), ())), precision=precision, preferred_element_type=F32)


def mm_tn(a, b, precision=None):
    return lax.dot_general(a, b, (((0,), (0,)), ((), ())), precision=precision, preferred_element_type=F32)


def halves(value):
    top = value.astype(BF16)
    return top, (value - top.astype(F32)).astype(BF16)


def down_rows(a_q, a_k, a_v):
    return jnp.concatenate([a[...].astype(F32) for a in (a_q, a_k, a_v)], axis=0).astype(BF16)


def soft_pair(rows, table):
    both = mm(rows, jnp.concatenate([table, -table], axis=1))
    left = lax.broadcasted_iota(jnp.int32, both.shape, 1) < DIM
    upper = jnp.max(jnp.where(left, both, NEG), axis=1, keepdims=True)
    lower = jnp.max(jnp.where(left, NEG, both), axis=1, keepdims=True)
    grown = jnp.exp(both - jnp.where(left, upper, lower))
    sum_left = jnp.sum(jnp.where(left, grown, 0.0), axis=1, keepdims=True)
    sum_right = jnp.sum(jnp.where(left, 0.0, grown), axis=1, keepdims=True)
    return grown * jnp.where(left, 1.0 / sum_left, 1.0 / sum_right)


def doc_at(positions, lengths):
    first = lengths[0]
    second = first + lengths[1]
    return (
        (positions >= 0).astype(jnp.int32)
        + (positions >= first).astype(jnp.int32)
        + (positions >= second).astype(jnp.int32)
    )


def write_mask(mask, lengths):
    base = lax.axis_index("seq") * ROWS
    row = lax.broadcasted_iota(jnp.int32, (ROWS, SPAN), 0) + base
    column = lax.broadcasted_iota(jnp.int32, (ROWS, SPAN), 1) + base - WINDOW
    same = doc_at(row, lengths) == doc_at(column, lengths)
    offset = row - column
    here = jnp.where(offset < WINDOW, 0.0, NEG)
    mask[...] = jnp.where(same & (offset >= 0), here, 2.0 * NEG)


def middle(count, first, lengths):
    base = lax.axis_index("seq") * ROWS + first
    position = lax.broadcasted_iota(jnp.int32, (count, 1), 0) + base
    return (doc_at(position, lengths) == 2).astype(F32)


def value_columns(kv):
    lane = lax.broadcasted_iota(jnp.int32, kv.shape, 1)
    v = jnp.concatenate([kv[:, DIM:], kv[:, :DIM]], axis=1)
    return jnp.where(lane < DIM, v, jnp.where(lane == DIM, 1.0, 0.0).astype(kv.dtype))


class Scan:
    def __init__(self, refs, reverse):
        self.own, self.pair, self.line, self.plane, self.sem = refs
        self.reverse = reverse
        z, x, c, y = spot()
        self.z, self.x, self.c = z, x, c
        self.sibling = at(z, x, 1 - c, y)
        self.x_mates = [at(z, turned(x, i), c, y) for i in (1, 2, 3)]
        self.z_mates = [at(turned(z, i), x, c, y) for i in (1, 2, 3)]

    @staticmethod
    def scratch(shape):
        return [
            pltpu.VMEM((3, *shape), F32),
            pltpu.VMEM(shape, F32),
            pltpu.VMEM((3, *shape), F32),
            pltpu.VMEM((3, *shape), F32),
            pltpu.SemaphoreType.DMA((2, 7)),
        ]

    def pair_copy(self):
        return send(self.own.at[0], self.pair, self.sem.at[0, 0], self.sem.at[1, 0], self.sibling)

    def line_copy(self, i):
        return send(self.own.at[1], self.line.at[i], self.sem.at[0, 1 + i], self.sem.at[1, 1 + i], self.x_mates[i])

    def plane_copy(self, i):
        return send(self.own.at[2], self.plane.at[i], self.sem.at[0, 4 + i], self.sem.at[1, 4 + i], self.z_mates[i])

    def counts(self, me, other):
        return ((other > me) if self.reverse else (other < me)).astype(F32)

    def open(self):
        self.pair_copy().start()

    def along_x(self):
        self.pair_copy().wait()
        self.own[1] = self.own[0] + self.pair[...]
        for i in range(3):
            self.line_copy(i).start()

    def along_z(self):
        for i in range(3):
            self.line_copy(i).wait()
        self.own[2] = self.own[1] + self.line[0] + self.line[1] + self.line[2]
        for i in range(3):
            self.plane_copy(i).start()

    def close(self, total):
        for i in range(3):
            self.plane_copy(i).wait()
        for i in range(3):
            total = total + self.line[i] * self.counts(self.x, turned(self.x, 3 - i))
        for i in range(3):
            total = total + self.plane[i] * self.counts(self.z, turned(self.z, 3 - i))
        return total


def front_kernel(
    x_ref, gain_one, gain_two, a_q, a_k, a_v, b_q, b_k, b_v, f_q, f_k, a_out, b_out, lengths, w_q, w_k, w_v, w_o, cot_hbm,
    normed_out, low_out, qh, kv_out, state_out, att_out, stat_out, mixed_out, lowmix_out, hidden_out, g_out, scales_out, xt_out,
    wq, wk, wv, wo, cot, w_sem, phq, phk, num, mask, q_rows, stat, brief, tail_sem,
    part, came, y_sem, low_part, square, square_came,
    *scan_refs,
):
    z, x, c, y = spot()
    s = lax.axis_index("seq")
    following, leading = (lax.rem(s + 1, 32), y), (lax.rem(s + 31, 32), y)
    y_mates = [at(z, x, c, turned(y, i)) for i in (1, 2, 3)]
    scan = Scan(scan_refs, False)
    partners = [following, leading, scan.sibling] + scan.x_mates + scan.z_mates + y_mates
    greet(partners)
    loads = [
        pltpu.make_async_copy(src, dst, w_sem.at[i])
        for i, (src, dst) in enumerate(((w_q, wq), (w_k, wk), (w_v, wv), (w_o, wo), (cot_hbm, cot)))
    ]
    for load in loads:
        load.start()
    for i in range(4):
        rows = pl.ds(64 * i, 64)
        value = x_ref[rows, :].astype(F32)
        scale = lax.rsqrt(jnp.mean(value * value, axis=1, keepdims=True) + EPS)
        scales_out[rows, 0:1] = scale
        normed_out[rows, :] = (value * scale * gain_one[...]).astype(BF16)
    write_mask(mask, lengths)
    low_out[...] = mm_nt(normed_out[...], down_rows(a_q, a_k, a_v)).astype(BF16)
    low = low_out[...]
    loads[1].wait()
    loads[2].wait()
    k = (mm(normed_out[...], wk[...]) + mm(low[:, 8:16], b_k[...])).astype(BF16)
    v = (mm(normed_out[...], wv[...]) + mm(low[:, 16:24], b_v[...])).astype(BF16)
    for j in range(KEY_HEADS):
        cut = slice(j * DIM, (j + 1) * DIM)
        kv_out[j, WINDOW:] = jnp.concatenate([k[:, cut], v[:, cut]], axis=1)
    tail = send(
        kv_out.at[:, pl.ds(ROWS, WINDOW)], kv_out.at[:, pl.ds(0, WINDOW)], tail_sem.at[0], tail_sem.at[1], following
    )
    greeted(partners)
    tail.start()
    loads[0].wait()
    for i in range(2):
        cut = slice(i * 256, (i + 1) * 256)
        q_rows[:, cut] = (mm(normed_out[...], wq[:, cut]) + mm(low[:, :8], b_q[:, cut])).astype(BF16)
    for h in range(HEADS):
        qh[h] = q_rows[:, h * DIM : (h + 1) * DIM]
    inside = middle(ROWS, 0, lengths)
    for j in range(KEY_HEADS):
        phk[j, WINDOW:] = soft_pair(kv_out[j, WINDOW:][:, :DIM], f_k[j]).astype(BF16)
        counted = (phk[j, WINDOW:].astype(F32) * inside).astype(BF16)
        rows = value_columns(kv_out[j, WINDOW:])
        settled = mm_tn(rows[: ROWS - WINDOW], counted[: ROWS - WINDOW])[:STATE]
        brief[0, j] = settled
        scan.own[0, j] = settled + mm_tn(rows[ROWS - WINDOW :], counted[ROWS - WINDOW :])[:STATE]
    brief_turn = send(brief.at[0], brief.at[1], tail_sem.at[2], tail_sem.at[3], scan.sibling)
    brief_turn.start()
    scan.open()

    def features(i, carry):
        phq[i] = soft_pair(qh[i], f_q[i]).astype(BF16)
        phq[i + 4] = soft_pair(qh[i + 4], f_q[i + 4]).astype(BF16)
        return carry

    lax.fori_loop(0, 2, features, 0)
    scan.along_x()
    lax.fori_loop(2, 4, features, 0)
    tail.wait()
    inside = middle(WINDOW, -WINDOW, lengths)
    for j in range(KEY_HEADS):
        phk[j, :WINDOW] = soft_pair(kv_out[j, :WINDOW][:, :DIM], f_k[j]).astype(BF16)
        counted = (phk[j, :WINDOW].astype(F32) * inside).astype(BF16)
        brief[2, j] = mm_tn(value_columns(kv_out[j, :WINDOW]), counted)[:STATE]
    brief_turn.wait()

    def one_head(h, j):
        kv = kv_out[j]
        distant = mask[...] == NEG
        scores = mm_nt(qh[h], kv[:, :DIM]) * (DIM**-0.5) + mask[...]
        top = jnp.max(scores, axis=1, keepdims=True)
        weights = jnp.exp(scores - top)
        total = weights + jnp.where(distant, mm_nt(phq[h], phk[j]) * jnp.exp(-top), 0.0)
        high = total.astype(BF16)
        rest = jnp.where(distant, total - high.astype(F32), 0.0).astype(BF16)
        v = kv[:, DIM:]
        num[h] = mm(high, v) + mm(rest, v)
        stat[h, :, 0:1] = top
        stat[h, :, 1:2] = jnp.sum(total, axis=1, keepdims=True)

    def inner(i, carry):
        one_head(i, 0)
        one_head(i + 4, 1)
        return carry

    lax.fori_loop(0, 2, inner, 0)
    scan.along_z()
    lax.fori_loop(2, 4, inner, 0)
    second = c.astype(F32)
    state_out[...] = scan.close(brief[1] * second - brief[2] * (1.0 - second))
    mine = middle(ROWS, 0, lengths)
    for h in range(HEADS):
        top, rest = halves(state_out[h // 4])
        carried = mm_nt(phq[h], top) + mm_nt(phq[h], rest)
        gate = jnp.exp(-stat[h, :, 0:1]) * mine
        total = stat[h, :, 1:2] + gate * carried[:, DIM : DIM + 1]
        stat[h, :, 1:2] = total
        stat[h, :, 2:3] = gate
        cut = slice(h * DIM, (h + 1) * DIM)
        attended = (num[h] + gate * carried[:, :DIM]) * (1.0 / total)
        att_out[:, cut] = attended
        mixed_out[:, cut] = attended.astype(BF16)
        stat_out[h] = stat[h].T
    mixed = mixed_out[...]
    low_part[y] = mm_nt(a_out[...], mixed)
    low_turns = [send(low_part.at[y], low_part.at[y], y_sem.at[0, i], y_sem.at[1, i], y_mates[i]) for i in range(3)]
    for turn in low_turns:
        turn.start()
    loads[3].wait()

    def columns(ref, d):
        return ref[:, pl.ds(pl.multiple_of(d * COLS, COLS), COLS)]

    line = Line(part, came, y_sem, 3)
    for i, which in ((1, (0, 1)), (0, (2,)), (2, (3,))):
        part[i] = mm(mixed, columns(wo, turned(y, 1 + i))).astype(BF16)
        line.start(*which)
    value = mm(mixed, columns(wo, y)) + columns(x_ref, y).astype(F32)

    def by_owner(m, rows):
        for i in range(16):
            flat = rows[:, i * 128 : (i + 1) * 128].T
            xt_out[m, 0, i // 4, i % 4] = flat[:64]
            xt_out[m, 1, i // 4, i % 4] = flat[64:]

    by_owner(0, normed_out)
    for i in range(3):
        here = low_part.at[turned(y, 3 - i)]
        send(here, here, y_sem.at[0, i], y_sem.at[1, i], y_mates[i]).wait()
    low_sum = low_part[0] + low_part[1] + low_part[2] + low_part[3]
    lowmix_out[...] = low_sum.T.astype(BF16)
    value = value + mm(lowmix_out[...], columns(b_out, y))
    line.merge()
    loads[4].wait()
    by_owner(1, cot)
    value = line.total(value)
    hidden_out[...] = value
    g_out[y] = (value * columns(gain_two, y)).astype(BF16)
    share = Share(g_out, y_sem, 12)
    square[...] = mm_nt(jnp.ones((8, COLS), F32), value * value, HIGH)
    square_turns = [
        send(square, square_came.at[i], y_sem.at[0, 9 + i], y_sem.at[1, 9 + i], y_mates[i]) for i in range(3)
    ]
    for turn in square_turns:
        turn.start()
    share.start()
    for turn in square_turns:
        turn.wait()
    mean = (square[...] + square_came[0] + square_came[1] + square_came[2]) * (1.0 / 2048)
    scales_out[:, 1:2] = lax.rsqrt(mean + EPS).T[:, 0:1]
    share.pass_on()
    share.finish()


def front(*args):
    anywhere = pl.BlockSpec(memory_space=pl.ANY)
    vmem = pl.BlockSpec(memory_space=pltpu.VMEM)
    shapes = (
        ((ROWS, 2048), BF16),
        ((ROWS, 24), BF16),
        ((HEADS, ROWS, DIM), BF16),
        ((KEY_HEADS, SPAN, 128), BF16),
        ((KEY_HEADS, STATE, 128), F32),
        ((ROWS, 512), F32),
        ((HEADS, 8, ROWS), F32),
        ((ROWS, 512), BF16),
        ((ROWS, 8), BF16),
        ((ROWS, COLS), F32),
        ((4, ROWS, COLS), BF16),
        ((ROWS, 2), F32),
        ((2, 2, 4, 4, 64, ROWS), BF16),
    )
    return pl.pallas_call(
        front_kernel,
        out_shape=tuple(jax.ShapeDtypeStruct(*shape) for shape in shapes),
        in_specs=[vmem] * 13 + [pl.BlockSpec(memory_space=pltpu.SMEM)] + [anywhere] * 5,
        out_specs=(vmem,) * len(shapes),
        scratch_shapes=[
            pltpu.VMEM((2048, 512), BF16),
            pltpu.VMEM((2048, 128), BF16),
            pltpu.VMEM((2048, 128), BF16),
            pltpu.VMEM((512, 2048), BF16),
            pltpu.VMEM((ROWS, 2048), BF16),
            pltpu.SemaphoreType.DMA((5,)),
            pltpu.VMEM((HEADS, ROWS, 128), BF16),
            pltpu.VMEM((KEY_HEADS, SPAN, 128), BF16),
            pltpu.VMEM((HEADS, ROWS, DIM), F32),
            pltpu.VMEM((ROWS, SPAN), F32),
            pltpu.VMEM((ROWS, 512), BF16),
            pltpu.VMEM((HEADS, ROWS, 8), F32),
            pltpu.VMEM((3, KEY_HEADS, STATE, 128), F32),
            pltpu.SemaphoreType.DMA((4,)),
            pltpu.VMEM((3, ROWS, COLS), BF16),
            pltpu.VMEM((3, ROWS, COLS), BF16),
            pltpu.SemaphoreType.DMA((2, 18)),
            pltpu.VMEM((4, 8, ROWS), F32),
            pltpu.VMEM((8, ROWS), F32),
            pltpu.VMEM((3, 8, ROWS), F32),
            *Scan.scratch((KEY_HEADS, STATE, 128)),
        ],
        compiler_params=pltpu.CompilerParams(
            collective_id=1, has_side_effects=True, vmem_limit_bytes=60 * 2**20
        ),
        name="front",
    )(*args)


def soft_back(soft, grad):
    left = lax.broadcasted_iota(jnp.int32, soft.shape, 1) < DIM
    part = soft * grad
    sum_left = jnp.sum(jnp.where(left, part, 0.0), axis=1, keepdims=True)
    sum_right = jnp.sum(jnp.where(left, 0.0, part), axis=1, keepdims=True)
    both = part - soft * jnp.where(left, sum_left, sum_right)
    return both[:, :DIM] - both[:, DIM:]


def late_kernel(
    hidden_in, scales, gain_one, gain_two, mixed, low_mix, att, stat, state, qh, kv, low,
    f_q, f_k, a_q, a_k, a_v, a_out, b_out, b_q, b_k, b_v, lengths,
    g_hbm, normed_hbm, x_hbm, cot_hbm, xt_hbm, w_q, w_k, w_v, w_o, w_gate, w_up, w_down,
    out_block, out_inputs, out_ffn, out_att, out_pack, out_gain,
    wb, x_all, w_sem,
    gs_came, ffn_came, gf_part, dot_part, dot_came, gb, gres, gsum, y_sem,
    xf, yf, xs, sem_ffn, xa, ya, sem_att, pk, sem_pack,
    mask, gh, pq, pkey, dext, dkv, gfq, gfk, ret, ret_came, next_state, ret_sem, glow, gkv, wide, gao, gbo, down_ref,
    first, gain_row, gain_rows_ref, px, px_came, pz, crown, sem_zx, stage, sem_stage, gain_c, gain_x, gain_z, gain_y, sem_gain,
    *rest,
):
    scan = Scan(rest[0:5], True)
    refs_big, refs_mid = rest[5:12], rest[12:19]
    z, x, c, y = spot()
    s = lax.axis_index("seq")
    following, leading = (lax.rem(s + 1, 32), y), (lax.rem(s + 31, 32), y)
    y_mates = [at(z, x, c, turned(y, i)) for i in (1, 2, 3)]
    sibling = scan.sibling
    partners = [following, leading, sibling] + scan.x_mates + scan.z_mates + y_mates
    greet(partners)

    def columns(ref, d):
        return ref[:, pl.ds(pl.multiple_of(d * COLS, COLS), COLS)]

    def to_mates(base, pieces, slots):
        return [
            send(pieces(i), slots.at[i], y_sem.at[0, base + i], y_sem.at[1, base + i], y_mates[i]) for i in range(3)
        ]

    own_rows, far_rows = pl.ds(0, ROWS), pl.ds(ROWS, ROWS)

    def local(i, src, dst):
        return pltpu.make_async_copy(src, dst, w_sem.at[i])

    def turn_at(n):
        return turned(y, (2, 1, 3, 0)[n])

    def part(n):
        return pl.ds(pl.multiple_of(n * COLS, COLS), COLS)

    def held(slot):
        local(slot, w_o.at[:, part(0)], wb.at[slot]).wait()

    def load_forward(u, slot):
        i = slot % 4
        src = (
            lambda: w_gate.at[part(i), part(u)],
            lambda: w_up.at[part(i), part(u)],
            lambda: w_down.at[part(u), part(i)],
        )[slot // 4]()
        local(slot, src, wb.at[slot]).start()

    def load_later(b):
        slot = b % 12
        if b < 32:
            src = (w_gate, w_up)[b % 8 // 4].at[part(turn_at(b // 8)), part(b % 4)]
        elif b < 48:
            src = w_down.at[part(b % 4), part(turn_at((b - 32) // 4))]
        elif b < 52:
            src = w_o.at[:, part(slot)]
        elif b < 56:
            src = w_q.at[part(slot - 4)]
        else:
            rows = part(slot - 8)
            local(slot, w_k.at[rows], wb.at[slot, :, pl.ds(0, 128)]).start()
            local(slot + 4, w_v.at[rows], wb.at[slot, :, pl.ds(128, 128)]).start()
            return
        local(slot, src, wb.at[slot]).start()

    def held_pair(slot):
        rows = part(slot - 8)
        local(slot, w_k.at[rows], wb.at[slot, :, pl.ds(0, 128)]).wait()
        local(slot + 4, w_v.at[rows], wb.at[slot, :, pl.ds(128, 128)]).wait()

    load_g = local(16, g_hbm, gb)
    load_cot = local(17, cot_hbm, x_all)
    load_x = local(18, x_hbm, x_all)
    load_n = [local(19 + i, normed_hbm.at[:, pl.ds(i * COLS, COLS)], gb.at[i]) for i in range(4)]
    load_g.start()
    for slot in range(12):
        load_forward(0, slot)
    load_cot.start()

    left_cot = [
        pltpu.make_async_copy(xt_hbm.at[1, c], xf.at[1, :, :, :, own_rows], w_sem.at[23]),
        send(xt_hbm.at[1, 1 - c], xf.at[1, :, :, :, far_rows], sem_ffn.at[0, 0], sem_ffn.at[1, 0], sibling),
    ]
    left_g = send(xs, xf.at[0, :, :, :, far_rows], sem_ffn.at[0, 1], sem_ffn.at[1, 1], sibling)

    def right_ffn(t):
        return send(yf.at[t, :, own_rows], yf.at[t, :, far_rows], sem_ffn.at[0, 2 + t], sem_ffn.at[1, 2 + t], sibling)

    left_att = [
        pltpu.make_async_copy(xt_hbm.at[0, c], xa.at[0, :, :, :, own_rows], w_sem.at[24]),
        send(xt_hbm.at[0, 1 - c], xa.at[0, :, :, :, far_rows], sem_att.at[0, 0], sem_att.at[1, 0], sibling),
    ]
    left_gb = send(xs, xa.at[1, :, :, :, far_rows], sem_att.at[0, 1], sem_att.at[1, 1], sibling)

    def right_att(t):
        return send(ya.at[t, own_rows], ya.at[t, far_rows], sem_att.at[0, 2 + t], sem_att.at[1, 2 + t], sibling)

    def by_owner(m, xd):
        for i in range(16):
            block = gb[i // 4, :, (i % 4) * 128 : (i % 4 + 1) * 128].T
            xd[m, i // 4, i % 4, :, 0:ROWS] = jnp.where(c == 0, block[:64], block[64:])
            xs[i // 4, i % 4] = jnp.where(c == 0, block[64:], block[:64])

    load_g.wait()
    by_owner(0, xf)
    greeted(partners)
    for copy in left_cot + [left_g]:
        copy.start()

    def product(xd, right):
        def term(t, i, k, *pieces):
            m, yd = right(t, i, k)
            rows = []
            for dest, first, last in pieces:
                piece = xd[m, first:last, dest] if k == 0 else xd[m, dest, first:last]
                rows.append(piece.reshape((last - first) * 64, 2 * ROWS))
            return mm(jnp.concatenate(rows, axis=0), yd)

        return term

    def half_of(k):
        return slice(k * FFN_HALF, (k + 1) * FFN_HALF)

    def finish_ffn(t, i, k, value):
        stage[t // 2 % 2, i, :, half_of(k)] = value

    def write_ffn(u):
        return pltpu.make_async_copy(stage.at[u % 2], out_ffn.at[:, u], sem_stage.at[u % 2])

    def sides(step, u):
        step(2 * u, 0)
        step(2 * u + 1, 1)

    def close_ffn(u):
        if u >= 2:
            write_ffn(u - 2).wait()
        sides(big.end, u)
        write_ffn(u).start()

    def finish_att(t, i, k, value):
        out_att[t] = value

    big = Ring(refs_big, 64, FFN_PARTS, product(xf, lambda t, i, k: (lax.div(i, 2), yf[t // 2, i, :, half_of(k)])), finish_ffn)
    mid = Ring(refs_mid, 64, 1, product(xa, lambda t, i, k: (t // 3, ya[t])), finish_att)

    def begin(u):
        right_ffn(u).wait()
        sides(big.start, u)

    def feed(u, carry):
        def through(first_slot, term):
            value = jnp.zeros((ROWS, COLS), F32)
            for i in range(4):
                slot = first_slot + i
                held(slot)
                value = value + term(i, slot)

                @pl.when(u < 3)
                def _():
                    load_forward(u + 1, slot)

                @pl.when(u == 3)
                def _():
                    load_later(slot)

            return value * scales[:, 1:2]

        gate = through(0, lambda i, slot: mm(gb[i], wb[slot]))
        up = through(4, lambda i, slot: mm(gb[i], wb[slot]))

        @pl.when(u == 0)
        def _():
            load_cot.wait()

        grad = through(8, lambda i, slot: mm_nt(x_all[:, i * COLS : (i + 1) * COLS], wb[slot]))
        sigmoid = jax.nn.sigmoid(gate)
        active = gate * sigmoid
        yf[u, 0, own_rows] = (grad * up * sigmoid * (1.0 + gate * (1.0 - sigmoid))).astype(BF16)
        yf[u, 1, own_rows] = (grad * active).astype(BF16)
        yf[u, 2, own_rows] = (active * up).astype(BF16)
        right_ffn(u).start()

        @pl.when(u == 1)
        def _():
            for copy in left_cot:
                copy.wait()
            left_g.wait()
            begin(0)

        @pl.when(u == 2)
        def _():
            begin(1)

        @pl.when(u == 3)
        def _():
            begin(2)

        return carry

    lax.fori_loop(0, FFN_TILES, feed, 0)
    for copy in left_att:
        copy.start()
    inverse = 1.0 / scales[:, 1:2]
    gs_line = Line(gf_part, gs_came, y_sem, 0)
    dot = jnp.zeros((ROWS, 1), F32)
    for n in range(4):
        value = jnp.zeros((ROWS, COLS), F32)
        for b in range(8 * n, 8 * n + 8):
            held(b % 12)
            value = value + mm_nt(yf[b % 4, b % 8 // 4, 0:ROWS], wb[b % 12])
            load_later(b + 12)
        value = value * inverse
        dot = dot + jnp.sum(value * gb[turn_at(n)].astype(F32), axis=1, keepdims=True)
        if n < 3:
            gf_part[(1, 0, 2)[n]] = value.astype(BF16)
            gs_line.start(*((0, 1), (2,), (3,))[n])
        else:
            gsum[...] = value
    dot_part[...] = jnp.broadcast_to(dot, (ROWS, 128)).T[:8]
    gs_dots = to_mates(6, lambda i: dot_part, dot_came)
    for turn in gs_dots:
        turn.start()
    gs_line.merge()
    begin(3)
    sides(big.merge, 0)

    for turn in gs_dots:
        turn.wait()
    total = gs_line.total(gsum[...])
    gsum[...] = total
    gain_rows = jnp.sum(total * hidden_in[...] * scales[:, 1:2], axis=0, keepdims=True)
    gain_rows_ref[...] = jnp.concatenate([gain_rows[:, i * 128 : (i + 1) * 128] for i in range(4)])

    def mean_column(own):
        return ((own + dot_came[0] + dot_came[1] + dot_came[2]) * (1.0 / 2048)).T[:, 0:1]

    scale = scales[:, 1:2]
    residual = (
        columns(x_all, y).astype(F32)
        + scale * (gsum[...] * columns(gain_two, y))
        - hidden_in[...] * (scale * scale * scale * mean_column(dot_part[...]))
    )
    gres[...] = residual
    gb[y] = residual.astype(BF16)
    gb_share = Share(gb, y_sem, 9)
    gb_share.start()
    load_x.start()

    ffn_turns = to_mates(15, lambda i: gf_part.at[i], ffn_came)
    for n in range(4):
        value = jnp.zeros((ROWS, COLS), F32)
        for b in range(32 + 4 * n, 36 + 4 * n):
            held(b % 12)
            value = value + mm(yf[b % 4, 2, 0:ROWS], wb[b % 12])
            load_later(b + 12)
        if n < 3:
            gf_part[(1, 0, 2)[n]] = value.astype(BF16)
        else:
            out_inputs[...] = value
    gb_share.pass_on()
    sides(big.merge, 1)
    write_mask(mask, lengths)
    def features(i, carry):
        pq[i] = soft_pair(qh[i], f_q[i])
        pq[i + 4] = soft_pair(qh[i + 4], f_q[i + 4])
        return carry

    lax.fori_loop(0, 4, features, 0)
    for j in range(KEY_HEADS):
        pkey[j] = soft_pair(kv[j][:, :DIM], f_k[j])
        pkey[KEY_HEADS + j] = jnp.zeros((SPAN, 128), F32)
    dkv[...] = jnp.zeros(dkv.shape, F32)
    pk[...] = jnp.zeros(pk.shape, F32)
    sides(big.merge, 2)

    gb_share.finish()
    for turn in ffn_turns:
        turn.start()
    for slot in range(4):
        held(slot)
    grad_low = jnp.zeros((ROWS, 8), F32)
    grad_mixed = jnp.zeros((ROWS, COLS), F32)
    for k in range(4):
        cut = slice(k * COLS, (k + 1) * COLS)
        grad_low = grad_low + mm_nt(gb[k], b_out[:, cut])
        grad_mixed = grad_mixed + mm_nt(gb[k], wb[k])
    grad_mixed = grad_mixed + jnp.dot(
        grad_low, a_out[...].astype(F32), precision=HIGH, preferred_element_type=F32
    )
    rounded = grad_mixed.astype(BF16)
    for h in range(HEADS):
        gh[h] = rounded[:, h * DIM : (h + 1) * DIM]
    top, bottom = halves(grad_low)
    gao[...] = mm_tn(top, mixed[...]) + mm_tn(bottom, mixed[...])
    for k in range(4):
        gbo[:, k * COLS : (k + 1) * COLS] = mm_tn(low_mix[...], gb[k])

    lane = lax.broadcasted_iota(jnp.int32, (ROWS, DIM), 1)
    for h in range(HEADS):
        j = h // 4
        grad = gh[h].astype(F32)
        column = stat[h].T
        inverse = 1.0 / column[:, 1:2]
        inner = -jnp.sum(grad * att[:, h * DIM : (h + 1) * DIM], axis=1, keepdims=True) * inverse
        ext = jnp.concatenate([grad * inverse, jnp.where(lane == 0, inner, 0.0)], axis=1)
        dext[h] = ext
        top, bottom = halves(ext * column[:, 2:3])
        phi = pq[h].astype(BF16)
        piece = (mm_tn(top, phi) + mm_tn(bottom, phi))[:STATE]
        scan.own[0, j] = piece if h % 4 == 0 else scan.own[0, j] + piece
    scan.open()

    by_owner(1, xa)
    for load in load_n:
        load.start()
    left_gb.start()
    for t in (3, 4):
        ya[t, 0:ROWS] = mixed[:, (t - 3) * ATT_WIDTH : (t - 2) * ATT_WIDTH]
        right_att(t).start()
    scan.along_x()
    left_gb.wait()
    for t in (3, 4):
        right_att(t).wait()
        mid.start(t, t % 2)

    sides(big.merge, 3)

    def one_head(h, j, q, grad, ext, row_stat, soft):
        keys, values = kv[j][:, :DIM], kv[j][:, DIM:]
        column = row_stat.T
        top, inverse, gate = column[:, 0:1], 1.0 / column[:, 1:2], column[:, 2:3]
        distant = mask[...] == NEG
        phi, phi_key = soft.astype(BF16), pkey[j].astype(BF16)
        damping = jnp.where(distant, jnp.exp(-top), 0.0)
        weights = jnp.exp(mm_nt(q, keys) * (DIM**-0.5) + mask[...] - top)
        grad_weights = mm_nt(grad, values) * inverse + ext[:, DIM : DIM + 1]
        grad_scores = (weights * grad_weights).astype(BF16)
        grad_linear = (damping * grad_weights).astype(BF16)
        both = weights.astype(BF16).astype(F32) + mm_nt(phi, phi_key) * damping
        held_weights = (both * inverse).astype(BF16)
        grad_q = mm(grad_scores, keys) * (DIM**-0.5)
        grad_k = mm_tn(grad_scores, q) * (DIM**-0.5)
        grad_kv = jnp.concatenate([grad_k, mm_tn(held_weights, grad)], axis=1)
        grad_phi_key = mm_tn(grad_linear, phi)
        carried = jnp.dot(
            (ext * gate)[:, :STATE], state[j], precision=HIGH, preferred_element_type=F32
        )
        grad_soft = mm(grad_linear, phi_key) + carried
        high, rest = halves(soft_back(soft, grad_soft))
        grad_q = (grad_q + mm_nt(high, f_q[h]) + mm_nt(rest, f_q[h])).astype(BF16)
        return grad_q, mm_tn(q, high) + mm_tn(q, rest), grad_kv, grad_phi_key

    def backward(i, carry):
        heads = (i, i + 4)
        loaded = [(qh[h], gh[h], dext[h], stat[h], pq[h]) for h in heads]
        results = [one_head(h, j, *loaded[j]) for j, h in enumerate(heads)]
        for j, h in enumerate(heads):
            gh[h], gfq[h] = results[j][:2]
            dkv[j] = dkv[j] + results[j][2]
            pkey[KEY_HEADS + j] = pkey[KEY_HEADS + j] + results[j][3]

        @pl.when(i == 0)
        def _():
            scan.along_z()
            sides(big.cross, 0)

        @pl.when(i == 1)
        def _():
            sides(big.cross, 1)

        @pl.when(i == 2)
        def _():
            sides(big.cross, 2)

        @pl.when(i == 3)
        def _():
            sides(big.cross, 3)

        return carry

    lax.fori_loop(0, 4, backward, 0)

    for j in range(KEY_HEADS):
        ret[j] = jnp.concatenate([dkv[j, :WINDOW], pkey[KEY_HEADS + j, :WINDOW]], axis=1)
    home = [
        send(ret, ret_came, ret_sem.at[0], ret_sem.at[1], leading),
        send(scan.own.at[0], next_state, ret_sem.at[2], ret_sem.at[3], leading),
    ]
    for copy in home:
        copy.start()
    gq = jnp.concatenate([gh[h] for h in range(HEADS)], axis=1)
    for i in range(2):
        ya[i, 0:ROWS] = gq[:, i * ATT_WIDTH : (i + 1) * ATT_WIDTH]
        right_att(i).start()
    down_ref[...] = down_rows(a_q, a_k, a_v)
    for slot in range(4, 8):
        held(slot)
    for slot in range(8, 12):
        held_pair(slot)
    for load in load_n + [load_x]:
        load.wait()
    glow[:, :8] = mm_nt(gq, b_q[...])
    for copy in left_att:
        copy.wait()
    for t in range(2):
        right_att(t).wait()
        mid.start(t, t % 2)
    for k in range(4):
        first[k] = mm_nt(gq, wb[4 + k])

    sides(big.merge_cross, 0)
    sides(big.merge_cross, 1)

    inside = middle(ROWS, 0, lengths)
    suffix = scan.close(scan.pair[...] * (1.0 - c.astype(F32)))
    for copy in home:
        copy.wait()
    joined = (s < 31).astype(F32)
    late_row = lax.broadcasted_iota(jnp.int32, (ROWS, 128), 0) >= ROWS - WINDOW
    for j in range(KEY_HEADS):
        soft = pkey[j, WINDOW:]
        phi = soft.astype(BF16)
        keys = kv[j, WINDOW:][:, :DIM]
        rows = value_columns(kv[j, WINDOW:])[:, :STATE]
        high, rest = halves(suffix[j])
        high_next, rest_next = halves(suffix[j] - joined * next_state[j])
        grad_phi = jnp.where(late_row, mm(rows, high_next) + mm(rows, rest_next), mm(rows, high) + mm(rows, rest))
        grad_phi = grad_phi * inside + pkey[KEY_HEADS + j, WINDOW:]
        grad_v = jnp.where(
            late_row[:, :STATE], mm_nt(phi, high_next) + mm_nt(phi, rest_next), mm_nt(phi, high) + mm_nt(phi, rest)
        )
        grad_v = (grad_v * inside)[:, :DIM]
        last = ROWS - WINDOW
        grad_phi = jnp.concatenate([grad_phi[:last], grad_phi[last:] + ret_came[j][:, 2 * DIM :]], axis=0)
        high, rest = halves(soft_back(soft, grad_phi))
        grad_k = mm_nt(high, f_k[j]) + mm_nt(rest, f_k[j])
        gfk[j] = mm_tn(keys, high) + mm_tn(keys, rest)
        dkv[j, WINDOW:] = dkv[j, WINDOW:] + jnp.concatenate([grad_k, grad_v], axis=1)
        dkv[j, ROWS:] = dkv[j, ROWS:] + ret_came[j][:, : 2 * DIM]
    gk = jnp.concatenate([dkv[j, WINDOW:][:, :DIM] for j in range(KEY_HEADS)], axis=1).astype(BF16)
    gv = jnp.concatenate([dkv[j, WINDOW:][:, DIM:] for j in range(KEY_HEADS)], axis=1).astype(BF16)
    gkv[...] = jnp.concatenate([gk, gv], axis=1)
    ya[2, 0:ROWS] = gkv[...]
    right_att(2).start()

    glow[:, 8:16] = mm_nt(gk, b_k[...])
    glow[:, 16:24] = mm_nt(gv, b_v[...])
    glow_high, glow_rest = halves(glow[...])
    for k in range(4):
        wide[:, k * COLS : (k + 1) * COLS] = mm_tn(glow_high, gb[k]) + mm_tn(glow_rest, gb[k])

    def place(d):
        return d // 16, d // 4 % 4, d % 4

    for i in range(16):
        cut = slice(i * 128, (i + 1) * 128)
        for half in range(2):
            d = place(2 * i + half)
            pk[*d, 0:12] = wide[12 * half : 12 * half + 12, cut]
            pk[*d, 13:16] = 0.25 * gbo[3 * half : 3 * half + 3, cut]
        pk[*place(26 + i // 8), 16 + 2 * (i % 8) : 18 + 2 * (i % 8)] = gbo[6:8, cut]

    def low_half(d, value):
        pk[*place(d), 16 : 16 + value.shape[0]] = value

    for i in range(4):
        pair = jnp.concatenate([gfq[2 * i], gfq[2 * i + 1]], axis=1)
        for part in range(4):
            low_half(4 * i + part, pair[16 * part : 16 * part + 16])
    pair = jnp.concatenate([gfk[0], gfk[1]], axis=1)
    for part in range(4):
        low_half(16 + part, pair[16 * part : 16 * part + 16])
    grad_b = jnp.concatenate(
        [mm_tn(low[:, :8], gq), mm_tn(low[:, 8:16], gkv[:, :128]), mm_tn(low[:, 16:24], gkv[:, 128:])], axis=1
    )
    for i in range(3):
        low_half(20 + i, jnp.concatenate([grad_b[:, 256 * i : 256 * i + 128], grad_b[:, 256 * i + 128 : 256 * i + 256]]))
    for i in range(2):
        low_half(23 + i, jnp.concatenate([gao[:, 256 * i : 256 * i + 128], gao[:, 256 * i + 128 : 256 * i + 256]]))
    low_half(25, gain_rows_ref[...])
    pack_far = send(pk.at[1 - c], pk.at[2], sem_pack.at[0], sem_pack.at[1], sibling)
    pack_far.start()

    for turn in ffn_turns:
        turn.wait()
    out_block[...] = (
        hidden_in[...]
        + out_inputs[...]
        + ffn_came[0].astype(F32)
        + ffn_came[1].astype(F32)
        + ffn_came[2].astype(F32)
    ).astype(BF16)
    gf_line = Line(gf_part, gs_came, y_sem, 18)

    def partial_first(d, dot):
        rows = pl.ds(pl.multiple_of(d * COLS, COLS), COLS)
        down = columns(down_ref, d)
        part = first[d] + mm_nt(gkv[...], wb[8 + d, :, 0:256]) + mm(glow_high, down) + mm(glow_rest, down)
        shaped = part * columns(x_all, d).astype(F32)
        gain_row[:, rows] = jnp.sum(shaped * scales[:, 0:1], axis=0, keepdims=True)
        return part, dot + jnp.sum(shaped * columns(gain_one, d), axis=1, keepdims=True)

    def spread(sems, base, piece, mates, back_piece):
        turns = [send(piece, piece, sems.at[0, base + i], sems.at[1, base + i], mate) for i, mate in enumerate(mates)]
        for turn in turns:
            turn.start()
        return [
            send(back_piece(i), back_piece(i), sems.at[0, base + i], sems.at[1, base + i], mate)
            for i, mate in enumerate(mates)
        ]

    def settle(turns):
        for turn in turns:
            turn.wait()

    dot = jnp.zeros((ROWS, 1), F32)
    for i in (1, 0):
        chunk, dot = partial_first(turned(y, 1 + i), dot)
        gf_part[i] = chunk.astype(BF16)
        gf_line.start(*((2,), (0, 1))[i])

    pack_far.wait()
    x_turns = [send(px.at[i], px_came.at[i], sem_zx.at[0, i], sem_zx.at[1, i], scan.x_mates[i]) for i in range(3)]
    for i in range(3):
        dest = turned(x, 1 + i)
        px[i] = (pk[c, :, dest] + pk[2, :, dest]).astype(BF16)
        x_turns[i].start()
    chunk, dot = partial_first(turned(y, 3), dot)
    gf_part[2] = chunk.astype(BF16)
    gf_line.start(3)
    chunk, dot = partial_first(y, dot)
    gsum[...] = chunk
    dot_part[...] = jnp.broadcast_to(dot, (ROWS, 128)).T[:8]
    dot_turns = to_mates(24, lambda i: dot_part, dot_came)
    for turn in dot_turns:
        turn.start()
    for i in range(16):
        gain_c[c, i : i + 1] = gain_row[:, i * 128 : (i + 1) * 128]
    gain_turns = spread(sem_gain, 0, gain_c.at[c], [sibling], lambda i: gain_c.at[1 - c])
    own_pack = pk[c, :, x] + pk[2, :, x]
    right_att(2).wait()
    mid.start(2, 0)
    gf_line.merge()
    settle(x_turns)
    own_pack = own_pack + px_came[0].astype(F32) + px_came[1].astype(F32) + px_came[2].astype(F32)
    pz[z] = own_pack.astype(BF16)
    z_turns = spread(sem_zx, 3, pz.at[z], scan.z_mates, lambda i: pz.at[turned(z, 3 - i)])
    settle(gain_turns)
    gain_x[x] = gain_c[0] + gain_c[1]
    gain_turns = spread(sem_gain, 1, gain_x.at[x], scan.x_mates, lambda i: gain_x.at[turned(x, 3 - i)])
    for t in (3, 4, 0, 1):
        mid.merge(t, t % 2)
    settle(z_turns)
    own_pack = pz[0].astype(F32) + pz[1].astype(F32) + pz[2].astype(F32) + pz[3].astype(F32)
    crown[y] = own_pack[:, :16]
    y_turns = spread(sem_zx, 10, crown.at[y], y_mates, lambda i: crown.at[turned(y, 3 - i)])
    settle(gain_turns)
    gain_z[z] = gain_x[0] + gain_x[1] + gain_x[2] + gain_x[3]
    gain_turns = spread(sem_gain, 4, gain_z.at[z], scan.z_mates, lambda i: gain_z.at[turned(z, 3 - i)])
    mid.merge(2, 0)
    settle(y_turns)
    top = crown[0] + crown[1] + crown[2] + crown[3]
    out_pack[c, :, x] = jnp.concatenate([top, own_pack[:, 16:]], axis=1).astype(BF16)
    x_turns = spread(sem_zx, 6, out_pack.at[c, :, x], scan.x_mates, lambda i: out_pack.at[c, :, turned(x, 3 - i)])
    settle(gain_turns)
    gain_y[y] = gain_z[0] + gain_z[1] + gain_z[2] + gain_z[3]
    gain_turns = spread(sem_gain, 7, gain_y.at[y], y_mates, lambda i: gain_y.at[turned(y, 3 - i)])
    for t in (3, 4, 0, 1, 2):
        mid.cross(t, t % 2)
    sides(big.merge_cross, 2)
    settle(dot_turns)
    total = gf_line.total(gsum[...])
    scale = scales[:, 0:1]
    out_inputs[...] = (
        gres[...]
        + scale * (total * columns(gain_one, y))
        - columns(x_all, y).astype(F32) * (scale * scale * scale * mean_column(dot_part[...]))
    )
    settle(x_turns)
    last = spread(sem_zx, 9, out_pack.at[c], [sibling], lambda i: out_pack.at[1 - c])
    settle(gain_turns)
    out_gain[...] = gain_y[0] + gain_y[1] + gain_y[2] + gain_y[3]
    for t in (3, 4, 0, 1, 2):
        mid.merge_cross(t, t % 2)
    sides(big.merge_cross, 3)
    for t in range(FFN_TILES):
        close_ffn(t)
    for t in (3, 4, 0, 1, 2):
        mid.end(t, t % 2)
    settle(last)
    write_ffn(2).wait()
    write_ffn(3).wait()
    for u in range(FFN_TILES):
        sides(big.drain, u)
    for t in range(ATT_TILES):
        mid.drain(t, t % 2)


def late(args, weights):
    anywhere = pl.BlockSpec(memory_space=pl.ANY)
    vmem = pl.BlockSpec(memory_space=pltpu.VMEM)
    shapes = (
        ((ROWS, COLS), BF16),
        ((ROWS, COLS), F32),
        ((FFN_PARTS, FFN_TILES, 64, FFN_WIDTH), F32),
        ((ATT_TILES, 64, ATT_WIDTH), F32),
        ((2, 4, 4, PACK, 128), BF16),
        ((16, 128), F32),
    )
    block = (ROWS, COLS)
    return pl.pallas_call(
        late_kernel,
        out_shape=tuple(jax.ShapeDtypeStruct(*shape) for shape in shapes),
        in_specs=[vmem] * 22 + [pl.BlockSpec(memory_space=pltpu.SMEM)] + [anywhere] * 12,
        out_specs=(vmem, vmem, anywhere, vmem, vmem, vmem),
        scratch_shapes=[
            pltpu.VMEM((12, COLS, COLS), BF16),
            pltpu.VMEM((ROWS, 2048), BF16),
            pltpu.SemaphoreType.DMA((25,)),
            pltpu.VMEM((3, *block), BF16),
            pltpu.VMEM((3, *block), BF16),
            pltpu.VMEM((3, *block), BF16),
            pltpu.VMEM((8, ROWS), F32),
            pltpu.VMEM((3, 8, ROWS), F32),
            pltpu.VMEM((4, *block), BF16),
            pltpu.VMEM(block, F32),
            pltpu.VMEM(block, F32),
            pltpu.SemaphoreType.DMA((2, 27)),
            pltpu.VMEM((2, 4, 4, 64, 512), BF16),
            pltpu.VMEM((FFN_TILES, FFN_PARTS, 512, FFN_WIDTH), BF16),
            pltpu.VMEM((4, 4, 64, ROWS), BF16),
            pltpu.SemaphoreType.DMA((2, 2 + FFN_TILES)),
            pltpu.VMEM((2, 4, 4, 64, 512), BF16),
            pltpu.VMEM((ATT_TILES, 512, ATT_WIDTH), BF16),
            pltpu.SemaphoreType.DMA((2, 2 + ATT_TILES)),
            pltpu.VMEM((3, 4, 4, PACK, 128), F32),
            pltpu.SemaphoreType.DMA((2,)),
            pltpu.VMEM((ROWS, SPAN), F32),
            pltpu.VMEM((HEADS, ROWS, DIM), BF16),
            pltpu.VMEM((HEADS, ROWS, 128), F32),
            pltpu.VMEM((2 * KEY_HEADS, SPAN, 128), F32),
            pltpu.VMEM((HEADS, ROWS, 128), F32),
            pltpu.VMEM((KEY_HEADS, SPAN, 128), F32),
            pltpu.VMEM((HEADS, DIM, DIM), F32),
            pltpu.VMEM((KEY_HEADS, DIM, DIM), F32),
            pltpu.VMEM((KEY_HEADS, WINDOW, 256), F32),
            pltpu.VMEM((KEY_HEADS, WINDOW, 256), F32),
            pltpu.VMEM((KEY_HEADS, STATE, 128), F32),
            pltpu.SemaphoreType.DMA((4,)),
            pltpu.VMEM((ROWS, 24), F32),
            pltpu.VMEM((ROWS, 256), BF16),
            pltpu.VMEM((24, 2048), F32),
            pltpu.VMEM((8, COLS), F32),
            pltpu.VMEM((8, 2048), F32),
            pltpu.VMEM((24, 2048), BF16),
            pltpu.VMEM((4, *block), F32),
            pltpu.VMEM((1, 2048), F32),
            pltpu.VMEM((4, 128), F32),
            pltpu.VMEM((3, 4, PACK, 128), BF16),
            pltpu.VMEM((3, 4, PACK, 128), BF16),
            pltpu.VMEM((4, 4, PACK, 128), BF16),
            pltpu.VMEM((4, 4, 16, 128), F32),
            pltpu.SemaphoreType.DMA((2, 13)),
            pltpu.VMEM((2, FFN_PARTS, 64, FFN_WIDTH), F32),
            pltpu.SemaphoreType.DMA((2,)),
            pltpu.VMEM((2, 16, 128), F32),
            pltpu.VMEM((4, 16, 128), F32),
            pltpu.VMEM((4, 16, 128), F32),
            pltpu.VMEM((4, 16, 128), F32),
            pltpu.SemaphoreType.DMA((2, 10)),
            *Scan.scratch((KEY_HEADS, STATE, 128)),
            *Ring.scratch(2 * FFN_TILES, FFN_PARTS, 64, FFN_HALF),
            *Ring.scratch(ATT_TILES, 1, 64, ATT_WIDTH),
        ],
        compiler_params=pltpu.CompilerParams(
            collective_id=2, has_side_effects=True, vmem_limit_bytes=63 * 2**20 + 2**19
        ),
        name="late",
    )(*args, *weights)


def finish_kernel(
    block, inputs, ffn_sums, att_sums, packed, gains,
    block_out, inputs_out, gain_one, w_q, a_q, b_q, w_k, a_k, b_k, w_v, a_v, b_v, f_q, f_k, w_o, a_o, b_o, gain_two,
    w_gate, w_up, w_down,
):
    block_out[...] = block[...]
    pack = packed[...].astype(F32)
    inputs_out[...] = inputs[...]
    for i in range(4):
        cut = slice(i * FFN_WIDTH, (i + 1) * FFN_WIDTH)
        w_gate[:, cut] = ffn_sums[0, i]
        w_up[:, cut] = ffn_sums[1, i]
        w_down[:, cut] = ffn_sums[2, i]
    for i in range(2):
        cut = slice(i * ATT_WIDTH, (i + 1) * ATT_WIDTH)
        w_q[:, cut] = att_sums[i]
        w_o[:, cut] = att_sums[3 + i]
    w_k[...] = att_sums[2, :, :128]
    w_v[...] = att_sums[2, :, 128:]
    for i in range(16):
        cut = slice(i * 128, (i + 1) * 128)
        rows = jnp.concatenate([pack[2 * i, :12], pack[2 * i + 1, :12]], axis=0)
        a_q[:, cut] = rows[:8]
        a_k[:, cut] = rows[8:16]
        a_v[:, cut] = rows[16:]
        last = 16 + 2 * (i % 8)
        b_o[:, cut] = jnp.concatenate(
            [pack[2 * i, 13:16], pack[2 * i + 1, 13:16], pack[26 + i // 8, last : last + 2]], axis=0
        )

    def tile(i):
        return pack[20 + i // 2, 16 + 8 * (i % 2) : 24 + 8 * (i % 2)]

    for i in range(4):
        cut = slice(i * 128, (i + 1) * 128)
        for part in range(4):
            rows = pack[4 * i + part, 16:]
            f_q[2 * i, 16 * part : 16 * part + 16] = rows[:, :DIM]
            f_q[2 * i + 1, 16 * part : 16 * part + 16] = rows[:, DIM:]
        rows = pack[16 + i, 16:]
        f_k[0, 16 * i : 16 * i + 16] = rows[:, :DIM]
        f_k[1, 16 * i : 16 * i + 16] = rows[:, DIM:]
        b_q[:, cut] = tile(i)
        a_o[:, cut] = tile(6 + i)
        gain_two[:, cut] = pack[25, 16 + i : 17 + i]
        gain_one[:, cut] = gains[pl.ds(4 * lax.axis_index("head") + i, 1), :]
    b_k[...] = tile(4)
    b_v[...] = tile(5)


def finish(block, inputs, ffn_sums, att_sums, pack, gains):
    vmem = pl.BlockSpec(memory_space=pltpu.VMEM)
    shapes = (
        (ROWS, COLS), (ROWS, COLS), (1, COLS), (64, COLS), (8, 2048), (8, COLS), (64, 128), (8, 2048), (8, 128),
        (64, 128), (8, 2048), (8, 128), (HEADS, DIM, DIM), (KEY_HEADS, DIM, DIM), (64, COLS), (8, COLS), (8, 2048),
        (1, COLS), (64, 2048), (64, 2048), (64, 2048),
    )
    outs = pl.pallas_call(
        finish_kernel,
        out_shape=tuple(jax.ShapeDtypeStruct(shape, F32 if i else BF16) for i, shape in enumerate(shapes)),
        in_specs=[vmem] * 6,
        out_specs=(vmem,) * len(shapes),
        compiler_params=pltpu.CompilerParams(vmem_limit_bytes=63 * 2**20),
        name="finish",
    )(block, inputs, ffn_sums, att_sums, pack.reshape(32, 32, 128), gains)
    return tuple(
        out[0] if i in (2, 17) else out.T if i in (4, 7, 10, 14, 15, 20) else out for i, out in enumerate(outs)
    )


def body(
    inputs,
    gain_first,
    w_query,
    a_query,
    b_query,
    key_projection_weight,
    a_key,
    key_adapter_second,
    value_projection_weight,
    a_value,
    value_adapter_second,
    feature_query,
    key_hedgehog_map,
    w_out,
    a_out,
    b_out,
    gain_second,
    w_gate,
    w_up,
    w_down,
    lengths,
    cotangent,
):
    gain_one, gain_two = gain_first[None], gain_second[None]
    a_in = (a_query.T, a_key.T, a_value.T)
    a_out = a_out.T
    projections = (w_query, key_projection_weight, value_projection_weight, w_out)
    normed, low, queries, kv, state, att, stat, mixed, low_mix, hidden_in, g, scales, xt = front(
        inputs, gain_one, gain_two, *a_in, b_query, key_adapter_second, value_adapter_second,
        feature_query, key_hedgehog_map, a_out, b_out, lengths, *projections, cotangent,
    )
    block_out, grad_inputs, out_ffn, out_att, out_pack, out_gain = late(
        (
            hidden_in, scales, gain_one, gain_two, mixed, low_mix, att, stat, state, queries, kv, low,
            feature_query, key_hedgehog_map, *a_in, a_out, b_out, b_query, key_adapter_second,
            value_adapter_second, lengths,
        ),
        (g, normed, inputs, cotangent, xt, *projections, w_gate, w_up, w_down),
    )
    return finish(block_out, grad_inputs, out_ffn, out_att, out_pack, out_gain)


def solution(mesh):
    return jax.shard_map(
        body,
        mesh=mesh,
        in_specs=(
            P("seq", None),
            P(),
            P(None, "head"),
            P(),
            P(None, "head"),
            P(None, "head"),
            P(),
            P(None, "head"),
            P(None, "head"),
            P(),
            P(None, "head"),
            P("head", None, None),
            P("head", None, None),
            P("head", None),
            P("head", None),
            P(),
            P(),
            P(None, "head"),
            P(None, "head"),
            P("head", None),
            P(),
            P("seq", None),
        ),
        out_specs=(
            P("seq", "head"),
            P("seq", "head"),
            P("head"),
            P("seq", "head"),
            P(),
            P(None, "head"),
            P("seq", "head"),
            P(),
            P(None, "head"),
            P("seq", "head"),
            P(),
            P(None, "head"),
            P("head", None, None),
            P("head", None, None),
            P("head", "seq"),
            P("head", None),
            P(),
            P("head"),
            P("seq", "head"),
            P("seq", "head"),
            P("head", "seq"),
        ),
        check_vma=False,
    )
```
